32 devices in a mesh: dp: 8 (over y, x, core), mp: 4 (over z).
Axes of the slice: x: 2, y: 2, z: 4, core: 2. Of those that a mesh axis runs over, the one named last changes fastest.
Arguments:
- layer_input: bfloat16 [8, 1024, 2048], P(None, 'dp', 'mp'), may hold values from -6 to 6
- output_grad: bfloat16 [8, 1024, 2048], P('dp', None, 'mp'), may hold values from -6 to 6
- seq_lengths: int32 [8], replicated, may hold values from 1 to 1024, 4352 in all
- deal_order: int32 [8], replicated, may hold values from 0 to 7, each once
- bucket_index: int32 [2047], replicated, may hold values from 0 to 31
- query_weight: float32 [2048, 2048], P('dp', 'mp'), may hold values from -0.015625 to 0.015625
- key_weight: float32 [2048, 2048], P('dp', 'mp'), may hold values from -0.125 to 0.125
- value_weight: float32 [2048, 2048], P('dp', 'mp'), may hold values from -0.125 to 0.125
- out_weight: float32 [2048, 2048], P('mp', 'dp'), may hold values from -1 to 1
- gate_weight: float32 [2048, 5120], P('dp', 'mp'), may hold values from -0.125 to 0.125
- up_weight: float32 [2048, 5120], P('dp', 'mp'), may hold values from -0.125 to 0.125
- down_weight: float32 [5120, 2048], P('mp', 'dp'), may hold values from -0.078125 to 0.078125
- attn_gain: float32 [2048], P('dp'), may hold values from 0.5 to 1.5
- ffn_gain: float32 [2048], P('dp'), may hold values from 0.5 to 1.5
- bias_table: float32 [32, 32], P('dp', 'mp'), may hold values from -6 to 6
- query_moment: float32 [2048, 2048], P('dp', 'mp'), may hold values from -12 to 12
- key_moment: float32 [2048, 2048], P('dp', 'mp'), may hold values from -1.5 to 1.5
- value_moment: float32 [2048, 2048], P('dp', 'mp'), may hold values from -1.5 to 1.5
- out_moment: float32 [2048, 2048], P('mp', 'dp'), may hold values from -0.18 to 0.18
- gate_moment: float32 [2048, 5120], P('dp', 'mp'), may hold values from -0.6 to 0.6
- up_moment: float32 [2048, 5120], P('dp', 'mp'), may hold values from -0.6 to 0.6
- down_moment: float32 [5120, 2048], P('mp', 'dp'), may hold values from -0.9 to 0.9
- attn_gain_moment: float32 [2048], P('dp'), may hold values from -2.4 to 2.4
- ffn_gain_moment: float32 [2048], P('dp'), may hold values from -1.2 to 1.2
- table_moment: float32 [32, 32], P('dp', 'mp'), may hold values from -2.1 to 2.1
Outputs:
- layer_out: bfloat16 [8, 1024, 2048], P('dp', None, 'mp')
- input_grad: bfloat16 [8, 1024, 2048], P(None, 'dp', 'mp')
- grad_norm: float32 [], replicated
- next_query_moment: float32 [2048, 2048], P('dp', 'mp')
- next_key_moment: float32 [2048, 2048], P('dp', 'mp')
- next_value_moment: float32 [2048, 2048], P('dp', 'mp')
- next_out_moment: float32 [2048, 2048], P('mp', 'dp')
- next_gate_moment: float32 [2048, 5120], P('dp', 'mp')
- next_up_moment: float32 [2048, 5120], P('dp', 'mp')
- next_down_moment: float32 [5120, 2048], P('mp', 'dp')
- next_attn_gain_moment: float32 [2048], P('dp')
- next_ffn_gain_moment: float32 [2048], P('dp')
- next_table_moment: float32 [32, 32], P('dp', 'mp')
The draws below stay inside these ranges and needn't reach their ends.
Inputs may be any that keep to these rules, and one draw needn't show every extreme that they name: `seq_lengths`: one sequence has exactly 1024 valid tokens. Every sequence is named once; index g of dp processes sequence deal_order[g]. `bucket_index`: entry r + 1023 is the bucket of key position minus query position r.
All inputs are finite; a program needn't handle non-finite values.
Results may differ from the reference program's by a relative error of at most 0.015.
Values may be sent and summed in bfloat16 or wider, within the bound.
No kernel may reach another device: no remote copies, remote signals or barrier semaphores. Data moves between devices by JAX's collectives and lax.ppermute only.
A program may use at most 320 MiB of HBM per device.

```python
import math
import jax
import jax.numpy as jnp
import numpy as np
from jax import lax

D = 2048
H = 32
DH = 64
FF = 5120
NB = 32
LMAX = 1024
SEQS = 8


def place_ends(array, stream_key, smallest, largest):
    longest = array.shape.index(max(array.shape))
    spots = []
    for shift in (0, 1):
        where = [jax.random.randint(jax.random.fold_in(stream_key, axis), (), 0, length) for axis, length in enumerate(array.shape)]
        where[longest] = (where[longest] + shift) % array.shape[longest]
        spots.append(tuple(where))
    return array.at[spots[0]].set(smallest).at[spots[1]].set(largest)


def levels(own_key, dims, pieces, smallest, high):
    factor_of, own = 1.0, jax.random.fold_in(own_key, 6)
    for dim, parts in pieces:
        heights = jnp.exp(jax.random.uniform(jax.random.fold_in(own, dim), (parts,), jnp.float32, smallest / len(pieces), high / len(pieces)))
        factor_of = factor_of * jnp.repeat(heights, dims[dim] // parts).reshape([-1 if axis == dim else 1 for axis in range(len(dims))])
    return factor_of


def profile(count, total, most, lean):
    weights = [(1 << 20) // math.isqrt(rank ** lean) + 1 for rank in range(2, count + 1)]
    rest, given = total - most - (count - 1), [1] * (count - 1)
    while rest > 0:
        free = [i for i in range(count - 1) if given[i] < most]
        mass, budget = sum([weights[i] for i in free]), rest
        for i in free:
            extra = min(most - given[i], max(1, budget * weights[i] // mass), rest)
            given[i] = given[i] + extra
            rest = rest - extra
    return np.array([most] + given)


def ragged(own_key, amount, total, most, skew):
    if amount == 2:
        one = jax.random.randint(own_key, (), max(1, total - most), min(most, total - 1) + 1)
        return jnp.stack([one, total - one])
    tallies = jnp.asarray(profile(amount, total, most, skew), jnp.int32)
    couples = (amount - 1) // 2
    donor, taker = tallies[1:1 + 2 * couples:2], tallies[2:2 + 2 * couples:2]
    slack = jnp.minimum(donor - 1, most - taker)
    shifted = jax.random.randint(jax.random.fold_in(own_key, 1), (couples,), 0, 1 << 20) % (slack + 1)
    tallies = tallies.at[1:1 + 2 * couples:2].set(donor - shifted).at[2:2 + 2 * couples:2].set(taker + shifted)
    return tallies[jax.random.permutation(jax.random.fold_in(own_key, 2), amount)]


def gaussian(key, extent, spread, most, shards=(), kind=jnp.bfloat16):
    entries = jax.random.normal(key, extent, jnp.float32) * spread
    if len(shards) > 0:
        entries = levels(key, extent, shards, -0.22, 0.18) * entries
    return jnp.clip(entries, min=-most, max=most).astype(kind)


def setup_inputs(seed: int = 0) -> dict:
    splits = jax.random.split(jax.random.key(seed), 26)
    return {
        "layer_input": gaussian(splits[0], (SEQS, LMAX, D), 1.0, 6.0, ((1, 8), (2, 4))),
        "output_grad": gaussian(splits[1], (SEQS, LMAX, D), 1.0, 6.0, ((0, 8), (2, 4))),
        "seq_lengths": ragged(splits[2], SEQS, SEQS * LMAX * 17 // 32, LMAX, 2).astype(jnp.int32),
        "deal_order": jax.random.permutation(splits[3], SEQS).astype(jnp.int32),
        "bucket_index": place_ends(jax.random.randint(splits[4], (2 * LMAX - 1,), 0, NB), jax.random.fold_in(splits[4], 1), 0, NB - 1).astype(jnp.int32),
        "query_weight": gaussian(splits[5], (D, H * DH), (D * DH) ** -0.5, 0.015625, ((0, 8), (1, 4)), jnp.float32),
        "key_weight": gaussian(splits[6], (D, H * DH), D ** -0.5, 0.125, ((0, 8), (1, 4)), jnp.float32),
        "value_weight": gaussian(splits[7], (D, H * DH), D ** -0.5, 0.125, ((0, 8), (1, 4)), jnp.float32),
        "out_weight": gaussian(splits[8], (H * DH, D), (H * DH * 16 // LMAX) ** -0.5, 1.0, ((0, 4), (1, 8)), jnp.float32),
        "gate_weight": gaussian(splits[9], (D, FF), D ** -0.5, 0.125, ((0, 8), (1, 4)), jnp.float32),
        "up_weight": gaussian(splits[10], (D, FF), D ** -0.5, 0.125, ((0, 8), (1, 4)), jnp.float32),
        "down_weight": gaussian(splits[11], (FF, D), FF ** -0.5, 0.078125, ((0, 4), (1, 8)), jnp.float32),
        "attn_gain": jnp.clip(1.0 + 0.1 * jax.random.normal(splits[12], (D,), jnp.float32), 0.5, 1.5),
        "ffn_gain": jnp.clip(1.0 + 0.1 * jax.random.normal(splits[13], (D,), jnp.float32), 0.5, 1.5),
        "bias_table": gaussian(splits[14], (NB, H), 1.0, 6.0, ((0, 8), (1, 4)), jnp.float32),
        "query_moment": gaussian(splits[15], (D, H * DH), 2.0, 12.0, ((0, 8), (1, 4)), jnp.float32),
        "key_moment": gaussian(splits[16], (D, H * DH), 0.25, 1.5, ((0, 8), (1, 4)), jnp.float32),
        "value_moment": gaussian(splits[17], (D, H * DH), 0.25, 1.5, ((0, 8), (1, 4)), jnp.float32),
        "out_moment": gaussian(splits[18], (H * DH, D), 0.03, 0.18, ((0, 4), (1, 8)), jnp.float32),
        "gate_moment": gaussian(splits[19], (D, FF), 0.1, 0.6, ((0, 8), (1, 4)), jnp.float32),
        "up_moment": gaussian(splits[20], (D, FF), 0.1, 0.6, ((0, 8), (1, 4)), jnp.float32),
        "down_moment": gaussian(splits[21], (FF, D), 0.15, 0.9, ((0, 4), (1, 8)), jnp.float32),
        "attn_gain_moment": gaussian(splits[22], (D,), 0.4, 2.4, ((0, 8),), jnp.float32),
        "ffn_gain_moment": gaussian(splits[23], (D,), 0.2, 1.2, ((0, 8),), jnp.float32),
        "table_moment": gaussian(splits[24], (NB, H), 0.35, 2.1, ((0, 8), (1, 4)), jnp.float32),
    }


EPS = 1e-06
NEG = -1e+30

@jax.custom_vjp
def low(v):
    return lax.optimization_barrier(v.astype(jnp.bfloat16)).astype(jnp.float32)

@jax.custom_vjp
def low_back(v):
    return v

def low_keep(v):
    return (low(v), None)

def low_pass(kept, grad):
    return (grad,)

def back_keep(v):
    return (v, None)

def back_low(kept, grad):
    return (low(grad),)
low.defvjp(low_keep, low_pass)
low_back.defvjp(back_keep, back_low)

def matmul_hi(left, right):
    return jnp.dot(left, right, precision=lax.Precision.HIGHEST, preferred_element_type=jnp.float32)

def one_sequence(seq_rows, seq_len, weights, bias_full):
    query_w, key_w, value_w, out_w, gate_w, up_w, down_w, gain_first, gain_second = weights
    inv_first = lax.rsqrt(lax.optimization_barrier(jnp.mean(seq_rows * seq_rows, axis=-1, keepdims=True)) + EPS)
    h_first = low(seq_rows * inv_first * gain_first)
    queries = low(low_back(matmul_hi(h_first, query_w))).reshape(LMAX, H, DH)
    key_rows = low(low_back(matmul_hi(h_first, key_w))).reshape(LMAX, H, DH)
    values = low(low_back(matmul_hi(h_first, value_w))).reshape(LMAX, H, DH)
    scores = jnp.einsum('qhd,khd->hqk', queries, key_rows, precision=lax.Precision.HIGHEST) + bias_full
    scores = low_back(scores)
    key_valid = jnp.arange(LMAX, dtype=jnp.int32) < seq_len
    scores = jnp.where(key_valid[None, None, :], scores, NEG)
    row_peak = lax.optimization_barrier(jnp.max(scores, axis=-1, keepdims=True))
    exp_terms = jnp.exp(scores - row_peak)
    soft = exp_terms / lax.optimization_barrier(jnp.sum(exp_terms, axis=-1, keepdims=True))
    mixed_rows = jnp.einsum('hqk,khd->qhd', low(soft), values, precision=lax.Precision.HIGHEST)
    attended = low(low_back(mixed_rows)).reshape(LMAX, H * DH)
    after_attn = seq_rows + low_back(matmul_hi(attended, out_w))
    inv_second = lax.rsqrt(lax.optimization_barrier(jnp.mean(after_attn * after_attn, axis=-1, keepdims=True)) + EPS)
    h_second = low(after_attn * inv_second * gain_second)
    gate_pre = low_back(matmul_hi(h_second, gate_w))
    up_pre = low_back(matmul_hi(h_second, up_w))
    hidden = low(jax.nn.gelu(gate_pre, approximate=True) * up_pre)
    return after_attn + low_back(matmul_hi(hidden, down_w))

def layer(inputs, params, seq_lengths, deal_order, bucket_index):
    rounded = [low(item) for item in params]
    weights = tuple(rounded[:9])
    table_low = rounded[9]
    dealt = jnp.take(inputs, deal_order, axis=0)
    dealt_len = jnp.take(seq_lengths, deal_order, axis=0)
    rel_rows = jnp.take(table_low, bucket_index, axis=0)
    positions = jnp.arange(LMAX, dtype=jnp.int32)
    offsets = (positions[None, :] - positions[:, None] + (LMAX - 1)).astype(jnp.int32)
    bias_full = jnp.transpose(jnp.take(rel_rows, offsets, axis=0), (2, 0, 1))

    def per_sequence(pair):
        return one_sequence(pair[0], pair[1], weights, bias_full)
    return lax.map(jax.checkpoint(per_sequence), (dealt, dealt_len))

def reference(layer_input, output_grad, seq_lengths, deal_order, bucket_index, query_weight, key_weight, value_weight, out_weight, gate_weight, up_weight, down_weight, attn_gain, ffn_gain, bias_table, query_moment, key_moment, value_moment, out_moment, gate_moment, up_moment, down_moment, attn_gain_moment, ffn_gain_moment, table_moment):
    params = (query_weight, key_weight, value_weight, out_weight, gate_weight, up_weight, down_weight, attn_gain, ffn_gain, bias_table)
    moments = (query_moment, key_moment, value_moment, out_moment, gate_moment, up_moment, down_moment, attn_gain_moment, ffn_gain_moment, table_moment)
    inputs = layer_input.astype(jnp.float32)

    def forward(inputs_in, params_in):
        return layer(inputs_in, params_in, seq_lengths, deal_order, bucket_index)
    outputs, back = jax.vjp(forward, inputs, params)
    dealt_len = jnp.take(seq_lengths, deal_order, axis=0)
    row_valid = (jnp.arange(LMAX, dtype=jnp.int32)[None, :] < dealt_len[:, None]).astype(jnp.float32)
    grad_y = output_grad.astype(jnp.float32) * row_valid[:, :, None]
    grad_in, grads = back(grad_y)
    total_sq = jnp.zeros((), jnp.float32)
    for grad_item in grads:
        total_sq = total_sq + jnp.sum(grad_item * grad_item)
    grad_norm = jnp.sqrt(total_sq)
    limit = math.sqrt(4 * D * H * DH + 3 * D * FF + 2 * D + NB * H)
    factor = jnp.minimum(1.0, limit / grad_norm)
    fresh = [0.5 * moments[index] + 0.5 * (factor * grads[index]) for index in range(10)]
    return (outputs.astype(jnp.bfloat16), grad_in.astype(jnp.bfloat16), grad_norm, fresh[0], fresh[1], fresh[2], fresh[3], fresh[4], fresh[5], fresh[6], fresh[7], fresh[8], fresh[9])
```

```python
import functools
import math

import jax
import jax.numpy as jnp
from jax import lax
from jax.experimental import pallas as pl
from jax.experimental.pallas import tpu as pltpu
from jax.sharding import PartitionSpec as P

D = 2048
H = 32
DH = 64
FF = 5120
NB = 32


EPS = 1e-06
NEG = -1e30
LANES = 128
BLOCK_ROWS = 256

NN = (((1,), (0,)), ((), ()))
NT = (((1,), (1,)), ((), ()))
TN = (((0,), (0,)), ((), ()))


def dot(left, right, dims=NN):
    return lax.dot_general(left, right, dims, preferred_element_type=jnp.float32)


def pick_head(pair_rows, which):
    lane = lax.broadcasted_iota(jnp.int32, (1, LANES), 1)
    return jnp.where(lane // DH == which, pair_rows, jnp.zeros_like(pair_rows))


def forward_kernel(length, rel_ref, query_ref, key_ref, value_ref, out_ref, soft_ref, skew):
    block = pl.program_id(1)
    rows = query_ref.shape[0]
    key_count = key_ref.shape[0]
    width = rel_ref.shape[2]

    @pl.when(block == 0)
    def _():
        for which in range(2):
            spread = jnp.broadcast_to(rel_ref[0, which : which + 1, :], (LANES, width))
            skew[which] = pltpu.roll(spread, width - (LANES - 1), 1, stride=1, stride_axis=0)

    key_at = lax.broadcasted_iota(jnp.int32, (1, key_count), 1)
    key_mask = jnp.where(key_at < length[0], 0.0, NEG)
    keys = key_ref[...]
    values = value_ref[...]
    mixed = jnp.zeros((rows, LANES), jnp.float32)
    for which in range(2):
        products = dot(pick_head(query_ref[...], which), keys, NT)
        parts = []
        for part in range(rows // LANES):
            offset = pl.multiple_of(key_count - LANES * (part + 1) - rows * block, LANES)
            parts.append(
                products[LANES * part : LANES * (part + 1)] + skew[which, :, pl.ds(offset, key_count)]
            )
        scores = jnp.concatenate(parts, 0) + key_mask
        exp_terms = jnp.exp(scores - jnp.max(scores, axis=1, keepdims=True))
        total = jnp.sum(exp_terms, axis=1, keepdims=True)
        soft_low = (exp_terms * (1.0 / total)).astype(jnp.bfloat16)
        soft_ref[which] = soft_low
        mixed = mixed + dot(soft_low, pick_head(values, which))
    out_ref[...] = mixed.astype(jnp.bfloat16)


def attend_forward(qkv, rel_rows, length):
    seq_len = qkv.shape[0]
    columns = qkv.shape[1] // 3
    pairs = columns // LANES
    width = rel_rows.shape[1]
    rows = min(BLOCK_ROWS, seq_len)
    return pl.pallas_call(
        forward_kernel,
        grid_spec=pltpu.PrefetchScalarGridSpec(
            num_scalar_prefetch=1,
            grid=(pairs, seq_len // rows),
            in_specs=[
                pl.BlockSpec((1, 2, width), lambda pair, block, n: (pair, 0, 0)),
                pl.BlockSpec((rows, LANES), lambda pair, block, n: (block, pair)),
                pl.BlockSpec((seq_len, LANES), lambda pair, block, n: (0, pairs + pair)),
                pl.BlockSpec((seq_len, LANES), lambda pair, block, n: (0, 2 * pairs + pair)),
            ],
            out_specs=[
                pl.BlockSpec((rows, LANES), lambda pair, block, n: (block, pair)),
                pl.BlockSpec((2, rows, seq_len), lambda pair, block, n: (pair, block, 0)),
            ],
            scratch_shapes=[pltpu.VMEM((2, LANES, width), jnp.float32)],
        ),
        out_shape=[
            jax.ShapeDtypeStruct((seq_len, columns), jnp.bfloat16),
            jax.ShapeDtypeStruct((2 * pairs, seq_len, seq_len), jnp.bfloat16),
        ],
        compiler_params=pltpu.CompilerParams(vmem_limit_bytes=40 << 20),
        cost_estimate=pl.CostEstimate(
            flops=16 * seq_len * seq_len * columns,
            bytes_accessed=4 * pairs * seq_len * seq_len,
            transcendentals=2 * pairs * seq_len * seq_len,
        ),
        name="attend_forward",
    )(length.reshape(1), rel_rows.reshape(pairs, 2, width), qkv, qkv, qkv)


def backward_kernel(
    soft_ref,
    query_ref,
    grad_ref,
    out_ref,
    key_ref,
    value_ref,
    grad_qkv_ref,
    rel_ref,
    skew,
    key_acc,
    value_acc,
):
    pair = pl.program_id(0)
    block = pl.program_id(1)
    rows = query_ref.shape[0]
    key_count = key_ref.shape[0]
    columns = grad_qkv_ref.shape[1] // 3

    @pl.when(block == 0)
    def _():
        skew[...] = jnp.zeros_like(skew)
        key_acc[...] = jnp.zeros_like(key_acc)
        value_acc[...] = jnp.zeros_like(value_acc)

    keys = key_ref[...]
    values = value_ref[...]
    queries = query_ref[...]
    grads = grad_ref[...]
    inner = grads.astype(jnp.float32) * out_ref[...].astype(jnp.float32)
    grad_query = jnp.zeros((rows, LANES), jnp.float32)
    for which in range(2):
        grad_head = pick_head(grads, which)
        row_inner = jnp.sum(pick_head(inner, which), axis=1, keepdims=True)
        grad_soft = dot(grad_head, values, NT)
        soft_low = soft_ref[which]
        grad_scores = soft_low.astype(jnp.float32) * (grad_soft - row_inner)
        for part in range(rows // LANES):
            offset = pl.multiple_of(key_count - LANES * (part + 1) - rows * block, LANES)
            skew[which, :, pl.ds(offset, key_count)] += grad_scores[
                LANES * part : LANES * (part + 1)
            ]
        grad_low = grad_scores.astype(jnp.bfloat16)
        grad_query = grad_query + dot(grad_low, pick_head(keys, which))
        key_acc[...] += dot(pick_head(queries, which), grad_low, TN)
        value_acc[...] += dot(grad_head, soft_low, TN)
    own_rows = pl.ds(pl.multiple_of(block * rows, rows), rows)
    own_columns = pl.multiple_of(pair * LANES, LANES)
    grad_qkv_ref[own_rows, pl.ds(own_columns, LANES)] = grad_query.astype(jnp.bfloat16)

    @pl.when(block == pl.num_programs(1) - 1)
    def _():
        grad_qkv_ref[:, pl.ds(columns + own_columns, LANES)] = key_acc[...].T.astype(jnp.bfloat16)
        grad_qkv_ref[:, pl.ds(2 * columns + own_columns, LANES)] = value_acc[...].T.astype(
            jnp.bfloat16
        )
        down = lax.broadcasted_iota(jnp.int32, (LANES, LANES), 0)
        across = lax.broadcasted_iota(jnp.int32, (LANES, LANES), 1)
        flip = (down + across == LANES - 1).astype(jnp.float32)
        for which in range(2):
            turned = lax.dot_general(
                flip,
                skew[which],
                NN,
                precision=lax.Precision.HIGHEST,
                preferred_element_type=jnp.float32,
            )
            rel_ref[0, which : which + 1, :] = jnp.sum(
                pltpu.roll(turned, 0, 1, stride=1, stride_axis=0), axis=0, keepdims=True
            )


def attend_backward(soft_low, qkv, grad_heads, attended):
    seq_len, columns = attended.shape
    pairs = columns // LANES
    width = 2 * seq_len
    rows = min(BLOCK_ROWS, seq_len)
    row_block = pl.BlockSpec((rows, LANES), lambda pair, block: (block, pair))
    grad_qkv, rel_grad = pl.pallas_call(
        backward_kernel,
        grid=(pairs, seq_len // rows),
        in_specs=[
            pl.BlockSpec((2, rows, seq_len), lambda pair, block: (pair, block, 0)),
            row_block,
            row_block,
            row_block,
            pl.BlockSpec((seq_len, LANES), lambda pair, block: (0, pairs + pair)),
            pl.BlockSpec((seq_len, LANES), lambda pair, block: (0, 2 * pairs + pair)),
        ],
        out_specs=[
            pl.BlockSpec((seq_len, 3 * columns), lambda pair, block: (0, 0)),
            pl.BlockSpec((1, 2, width), lambda pair, block: (pair, 0, 0)),
        ],
        scratch_shapes=[
            pltpu.VMEM((2, LANES, width), jnp.float32),
            pltpu.VMEM((LANES, seq_len), jnp.float32),
            pltpu.VMEM((LANES, seq_len), jnp.float32),
        ],
        out_shape=[
            jax.ShapeDtypeStruct((seq_len, 3 * columns), jnp.bfloat16),
            jax.ShapeDtypeStruct((pairs, 2, width), jnp.float32),
        ],
        compiler_params=pltpu.CompilerParams(vmem_limit_bytes=40 << 20),
        cost_estimate=pl.CostEstimate(
            flops=40 * seq_len * seq_len * columns,
            bytes_accessed=4 * pairs * seq_len * seq_len,
            transcendentals=0,
        ),
        name="attend_backward",
    )(soft_low, qkv, grad_heads, attended, qkv, qkv)
    return grad_qkv, rel_grad.reshape(2 * pairs, width)


def around(block):
    count = lax.axis_size("mp")
    return lax.ppermute(block, "mp", [(i, (i + 1) % count) for i in range(count)])


def ring_gather(own):
    blocks = [own]
    for _ in range(lax.axis_size("mp") - 1):
        blocks.append(around(blocks[-1]))
    return blocks


def ring_scatter(part_of):
    running = part_of(1).astype(jnp.bfloat16)
    for step in range(2, lax.axis_size("mp")):
        running = (around(running).astype(jnp.float32) + part_of(step)).astype(jnp.bfloat16)
    return around(running).astype(jnp.float32) + part_of(0)


def update(moment, grad_owned, factor):
    return 0.5 * moment + (0.5 * factor) * grad_owned


def shards(
    layer_input,
    output_grad,
    seq_lengths,
    deal_order,
    bucket_index,
    query_weight,
    key_weight,
    value_weight,
    out_weight,
    gate_weight,
    up_weight,
    down_weight,
    attn_gain,
    ffn_gain,
    bias_table,
    query_moment,
    key_moment,
    value_moment,
    out_moment,
    gate_moment,
    up_moment,
    down_moment,
    attn_gain_moment,
    ffn_gain_moment,
    table_moment,
):
    low = jnp.bfloat16
    f32 = jnp.float32
    group_index = lax.axis_index("dp")
    member = lax.axis_index("mp")
    group_count = lax.axis_size("dp")
    tensor_count = lax.axis_size("mp")

    def back(step):
        return lax.rem(member - step + tensor_count, tensor_count)

    picked = jnp.take(layer_input, deal_order, axis=0)
    x_own = lax.all_to_all(picked, "dp", split_axis=0, concat_axis=1, tiled=True)[0]
    length = seq_lengths[deal_order[group_index]]
    seq_len, quarter = x_own.shape
    features = quarter * tensor_count
    part_rows = seq_len // tensor_count
    row_valid = lax.broadcasted_iota(jnp.int32, (seq_len, 1), 0) < length

    def row_part(array, step):
        return lax.dynamic_slice_in_dim(array, back(step) * part_rows, part_rows, 0)

    def column_part(array, step):
        return lax.dynamic_slice_in_dim(array, back(step) * quarter, quarter, 1)

    def set_rows(whole, part, step):
        return lax.dynamic_update_slice_in_dim(whole, part, back(step) * part_rows, 0)

    def whole_columns(parts):
        whole = jnp.zeros((seq_len, features), parts[0].dtype)
        for step, part in enumerate(parts):
            whole = lax.dynamic_update_slice_in_dim(whole, part, back(step) * quarter, 1)
        return whole

    small = jnp.concatenate([attn_gain, ffn_gain, bias_table.reshape(-1)]).astype(low)
    small = lax.all_gather(small, "dp", axis=0)
    gain_size = attn_gain.shape[0]
    first_gain = small[:, :gain_size].reshape(-1).astype(f32)
    second_gain = small[:, gain_size : 2 * gain_size].reshape(-1).astype(f32)
    full_table = small[:, 2 * gain_size :].reshape(NB, bias_table.shape[1])
    qkv_weight = jnp.concatenate([query_weight, key_weight, value_weight], axis=1).astype(low)
    qkv_weight = lax.all_gather(qkv_weight, "dp", axis=0, tiled=True)
    gate_up = jnp.concatenate([gate_weight, up_weight], axis=1).astype(low)
    out_down = jnp.concatenate([out_weight, down_weight], axis=0).astype(low)
    heads_columns = out_weight.shape[0]
    units = down_weight.shape[0]
    gate_up, out_down = lax.optimization_barrier((gate_up, out_down, qkv_weight))[:2]
    out_down = lax.all_gather(out_down, "dp", axis=1, tiled=True)
    gate_up = lax.optimization_barrier((gate_up, out_down))[0]
    gate_up = lax.all_gather(gate_up, "dp", axis=0, tiled=True)
    full_out = out_down[:heads_columns]
    full_down = out_down[heads_columns:]

    x_rows = whole_columns(ring_gather(x_own))
    grad_own = jnp.where(row_valid, output_grad[0], jnp.zeros((), low))
    grad_own, x_rows = lax.optimization_barrier((grad_own, x_rows))
    grad_y = whole_columns(ring_gather(grad_own))

    offsets = jnp.concatenate([bucket_index, jnp.full((1,), NB, jnp.int32)])
    bucket_hot = offsets[:, None] == lax.broadcasted_iota(jnp.int32, (2 * seq_len, NB), 1)
    rel_rows = dot(full_table, bucket_hot.astype(low), (((0,), (1,)), ((), ())))

    x_float = x_rows.astype(f32)
    inv_first = lax.rsqrt(jnp.mean(x_float * x_float, axis=-1, keepdims=True) + EPS)
    h_first = (x_float * inv_first * first_gain).astype(low)
    qkv = dot(h_first, qkv_weight).astype(low)
    attended, soft_low = attend_forward(qkv, rel_rows, length)
    attn_branch = ring_scatter(lambda step: dot(row_part(attended, step), full_out))

    after_attn = row_part(x_rows, 0).astype(f32) + attn_branch
    inv_second = lax.rsqrt(jnp.mean(after_attn * after_attn, axis=-1, keepdims=True) + EPS)
    h_second = (after_attn * inv_second * second_gain).astype(low)

    h_parts = ring_gather(h_second)
    hidden = jnp.zeros((seq_len, units), low)
    gate_up_grads = []
    for step, h_part in enumerate(h_parts):
        both = dot(h_part, gate_up)
        mixed, mix_back = jax.vjp(
            lambda gate_in, up_in: jax.nn.gelu(gate_in, approximate=True) * up_in,
            both[:, :units],
            both[:, units:],
        )
        hidden = set_rows(hidden, mixed.astype(low), step)
        grad_hidden = dot(row_part(grad_y, step), full_down, NT)
        gate_up_grads.append(jnp.concatenate(mix_back(grad_hidden), axis=1).astype(low))
    grad_h_second = ring_scatter(lambda step: dot(gate_up_grads[step], gate_up, NT))
    h_rotated = jnp.concatenate(h_parts, axis=0)
    grads_rotated = jnp.concatenate(gate_up_grads, axis=0)
    grad_gate_up = dot(h_rotated, grads_rotated, TN).astype(low)
    grad_down = dot(hidden, grad_y, TN).astype(low)
    owned_gate_up = lax.psum_scatter(grad_gate_up, "dp", scatter_dimension=0, tiled=True)
    owned_down = lax.psum_scatter(grad_down, "dp", scatter_dimension=1, tiled=True)

    grad_ffn_gain = jnp.sum(grad_h_second * (after_attn * inv_second), axis=0)
    weighted = grad_h_second * second_gain
    row_inner = jnp.mean(weighted * after_attn, axis=-1, keepdims=True)
    grad_after = (
        row_part(grad_y, 0).astype(f32)
        + inv_second * weighted
        - after_attn * (inv_second * inv_second * inv_second) * row_inner
    ).astype(low)
    after_parts = ring_gather(grad_after)
    grad_after = jnp.zeros((seq_len, features), low)
    grad_heads = jnp.zeros((seq_len, heads_columns), low)
    for step, part in enumerate(after_parts):
        grad_after = set_rows(grad_after, part, step)
        grad_heads = set_rows(grad_heads, dot(part, full_out, NT).astype(low), step)
    grad_out = dot(attended, grad_after, TN).astype(low)
    owned_out = lax.psum_scatter(grad_out, "dp", scatter_dimension=1, tiled=True)

    grad_qkv, rel_grad = attend_backward(soft_low, qkv, grad_heads, attended)
    grad_qkv_weight = dot(h_first, grad_qkv, TN).astype(low)
    owned_qkv = lax.psum_scatter(grad_qkv_weight, "dp", scatter_dimension=0, tiled=True)
    grad_table = lax.dot_general(
        bucket_hot.astype(f32),
        rel_grad,
        (((0,), (1,)), ((), ())),
        precision=lax.Precision.HIGHEST,
        preferred_element_type=f32,
    )
    grad_h_first = ring_scatter(
        lambda step: dot(
            grad_qkv,
            lax.dynamic_slice_in_dim(qkv_weight, back(step) * quarter, quarter, 0),
            NT,
        )
    )
    own_gain = lax.dynamic_slice_in_dim(first_gain, member * quarter, quarter, 0)
    x_own = x_own.astype(f32)
    grad_attn_gain = jnp.sum(grad_h_first * (x_own * inv_first), axis=0)
    weighted = grad_h_first * own_gain
    row_inner = lax.psum(jnp.sum(weighted * x_own, axis=-1), "mp")[:, None] / features
    grad_input = (
        column_part(grad_after, 0).astype(f32)
        + inv_first * weighted
        - x_own * (inv_first * inv_first * inv_first) * row_inner
    ).astype(low)
    came_back = lax.all_to_all(grad_input[None], "dp", split_axis=1, concat_axis=0, tiled=True)
    group_iota = lax.broadcasted_iota(jnp.int32, (group_count, group_count), 1)
    place = jnp.argmax(deal_order[None, :] == group_iota.T, axis=1)
    input_grad = jnp.take(came_back, place, axis=0)

    hidden, grad_after = lax.optimization_barrier((hidden, grad_after))

    def output_part(step):
        part = dot(hidden, column_part(full_down, step))
        mine = row_part(part, 0) + column_part(after_attn, step)
        return set_rows(part, mine, 0)

    layer_out = ring_scatter(output_part).astype(low)[None]

    local_sq = jnp.zeros((), f32)
    for piece in (owned_qkv, owned_out, owned_gate_up, owned_down):
        piece = piece.astype(f32)
        local_sq = local_sq + jnp.sum(piece * piece)
    heads_dev = bias_table.shape[1]
    first_wide = lax.dynamic_update_slice_in_dim(
        jnp.zeros((features,), f32), grad_attn_gain, member * quarter, 0
    )
    table_wide = lax.dynamic_update_slice_in_dim(
        jnp.zeros((NB, heads_dev * tensor_count), f32), grad_table, member * heads_dev, 1
    )
    sums = lax.psum(
        jnp.concatenate([first_wide, grad_ffn_gain, table_wide.reshape(-1), local_sq[None]]),
        ("dp", "mp"),
    )
    total_sq = sums[-1] + jnp.sum(sums[:-1] * sums[:-1])
    grad_norm = jnp.sqrt(total_sq)
    limit = math.sqrt(4 * D * H * DH + 3 * D * FF + 2 * D + NB * H)
    factor = jnp.minimum(1.0, limit / grad_norm)
    owned_first = lax.dynamic_slice_in_dim(sums, group_index * gain_size, gain_size, 0)
    owned_second = lax.dynamic_slice_in_dim(
        sums, features + group_index * gain_size, gain_size, 0
    )
    table_rows = bias_table.shape[0]
    owned_table = lax.dynamic_slice(
        sums[2 * features : -1].reshape(NB, heads_dev * tensor_count),
        (group_index * table_rows, member * heads_dev),
        (table_rows, heads_dev),
    )
    return (
        layer_out,
        input_grad,
        grad_norm,
        update(query_moment, owned_qkv[:, :heads_columns], factor),
        update(key_moment, owned_qkv[:, heads_columns : 2 * heads_columns], factor),
        update(value_moment, owned_qkv[:, 2 * heads_columns :], factor),
        update(out_moment, owned_out, factor),
        update(gate_moment, owned_gate_up[:, :units], factor),
        update(up_moment, owned_gate_up[:, units:], factor),
        update(down_moment, owned_down, factor),
        update(attn_gain_moment, owned_first, factor),
        update(ffn_gain_moment, owned_second, factor),
        update(table_moment, owned_table, factor),
    )


def solution(mesh):
    in_specs = (
        P(None, "dp", "mp"),
        P("dp", None, "mp"),
        P(),
        P(),
        P(),
        P("dp", "mp"),
        P("dp", "mp"),
        P("dp", "mp"),
        P("mp", "dp"),
        P("dp", "mp"),
        P("dp", "mp"),
        P("mp", "dp"),
        P("dp"),
        P("dp"),
        P("dp", "mp"),
        P("dp", "mp"),
        P("dp", "mp"),
        P("dp", "mp"),
        P("mp", "dp"),
        P("dp", "mp"),
        P("dp", "mp"),
        P("mp", "dp"),
        P("dp"),
        P("dp"),
        P("dp", "mp"),
    )
    out_specs = (
        P("dp", None, "mp"),
        P(None, "dp", "mp"),
        P(),
        P("dp", "mp"),
        P("dp", "mp"),
        P("dp", "mp"),
        P("mp", "dp"),
        P("dp", "mp"),
        P("dp", "mp"),
        P("mp", "dp"),
        P("dp"),
        P("dp"),
        P("dp", "mp"),
    )
    return jax.shard_map(shards, mesh=mesh, in_specs=in_specs, out_specs=out_specs, check_vma=False)
```

```python
import functools
import math

import jax
import jax.numpy as jnp
from jax import lax
from jax.experimental import pallas as pl
from jax.experimental.pallas import tpu as pltpu
from jax.sharding import PartitionSpec as P

D = 2048
H = 32
DH = 64
FF = 5120
NB = 32


EPS = 1e-06
NEG = -1e30
LANES = 128
BLOCK_ROWS = 256

NN = (((1,), (0,)), ((), ()))
NT = (((1,), (1,)), ((), ()))
TN = (((0,), (0,)), ((), ()))


def dot(left, right, dims=NN):
    return lax.dot_general(left, right, dims, preferred_element_type=jnp.float32)


def pick_head(pair_rows, which):
    lane = lax.broadcasted_iota(jnp.int32, (1, LANES), 1)
    return jnp.where(lane // DH == which, pair_rows, jnp.zeros_like(pair_rows))


def forward_kernel(length, rel_ref, query_ref, key_ref, value_ref, out_ref, soft_ref, skew):
    block = pl.program_id(1)
    rows = query_ref.shape[0]
    key_count = key_ref.shape[0]
    width = rel_ref.shape[2]

    @pl.when(block == 0)
    def _():
        for which in range(2):
            spread = jnp.broadcast_to(rel_ref[0, which : which + 1, :], (LANES, width))
            skew[which] = pltpu.roll(spread, width - (LANES - 1), 1, stride=1, stride_axis=0)

    key_at = lax.broadcasted_iota(jnp.int32, (1, key_count), 1)
    key_mask = jnp.where(key_at < length[0], 0.0, NEG)
    keys = key_ref[...]
    values = value_ref[...]
    mixed = jnp.zeros((rows, LANES), jnp.float32)
    for which in range(2):
        products = dot(pick_head(query_ref[...], which), keys, NT)
        parts = []
        for part in range(rows // LANES):
            offset = pl.multiple_of(key_count - LANES * (part + 1) - rows * block, LANES)
            parts.append(
                products[LANES * part : LANES * (part + 1)] + skew[which, :, pl.ds(offset, key_count)]
            )
        scores = jnp.concatenate(parts, 0) + key_mask
        exp_terms = jnp.exp(scores - jnp.max(scores, axis=1, keepdims=True))
        total = jnp.sum(exp_terms, axis=1, keepdims=True)
        soft_low = (exp_terms * (1.0 / total)).astype(jnp.bfloat16)
        soft_ref[which] = soft_low
        mixed = mixed + dot(soft_low, pick_head(values, which))
    out_ref[...] = mixed.astype(jnp.bfloat16)


def attend_forward(qkv, rel_rows, length, first, last, so_far=None):
    seq_len = qkv.shape[0]
    columns = qkv.shape[1] // 3
    pairs = columns // LANES
    width = rel_rows.shape[1]
    rows = min(BLOCK_ROWS, seq_len)
    kernel = forward_kernel
    operands = [length.reshape(1), rel_rows.reshape(pairs, 2, width), qkv, qkv, qkv]
    in_specs = [
        pl.BlockSpec((1, 2, width), lambda pair, block, n: (first + pair, 0, 0)),
        pl.BlockSpec((rows, LANES), lambda pair, block, n: (block, first + pair)),
        pl.BlockSpec((seq_len, LANES), lambda pair, block, n: (0, pairs + first + pair)),
        pl.BlockSpec((seq_len, LANES), lambda pair, block, n: (0, 2 * pairs + first + pair)),
    ]
    aliases = {}
    if so_far is not None:
        kernel = second_forward_kernel
        operands += so_far
        in_specs += [pl.BlockSpec(memory_space=pl.ANY)] * 2
        aliases = {5: 0, 6: 1}
    return pl.pallas_call(
        kernel,
        grid_spec=pltpu.PrefetchScalarGridSpec(
            num_scalar_prefetch=1,
            grid=(last - first, seq_len // rows),
            in_specs=in_specs,
            out_specs=[
                pl.BlockSpec((rows, LANES), lambda pair, block, n: (block, first + pair)),
                pl.BlockSpec((2, rows, seq_len), lambda pair, block, n: (first + pair, block, 0)),
            ],
            scratch_shapes=[pltpu.VMEM((2, LANES, width), jnp.float32)],
        ),
        out_shape=[
            jax.ShapeDtypeStruct((seq_len, columns), jnp.bfloat16),
            jax.ShapeDtypeStruct((2 * pairs, seq_len, seq_len), jnp.bfloat16),
        ],
        input_output_aliases=aliases,
        compiler_params=pltpu.CompilerParams(vmem_limit_bytes=40 << 20),
        cost_estimate=pl.CostEstimate(
            flops=16 * seq_len * seq_len * columns * (last - first) // pairs,
            bytes_accessed=4 * (last - first) * seq_len * seq_len,
            transcendentals=2 * (last - first) * seq_len * seq_len,
        ),
        name="attend_forward",
    )(*operands)


def second_forward_kernel(
    length, rel_ref, query_ref, key_ref, value_ref, _, __, out_ref, soft_ref, skew
):
    forward_kernel(length, rel_ref, query_ref, key_ref, value_ref, out_ref, soft_ref, skew)


def backward_kernel(
    first,
    soft_ref,
    query_ref,
    grad_ref,
    out_ref,
    key_ref,
    value_ref,
    *rest,
):
    grad_qkv_ref, rel_ref, skew, key_acc, value_acc = rest[-5:]
    pair = first + pl.program_id(0)
    block = pl.program_id(1)
    rows = query_ref.shape[0]
    key_count = key_ref.shape[0]
    columns = grad_qkv_ref.shape[1] // 3

    @pl.when(block == 0)
    def _():
        skew[...] = jnp.zeros_like(skew)
        key_acc[...] = jnp.zeros_like(key_acc)
        value_acc[...] = jnp.zeros_like(value_acc)

    if len(rest) > 5:

        @pl.when((block == 0) & (pair == first))
        def _():
            grad_qkv_ref[...] = rest[0][...]

    keys = key_ref[...]
    values = value_ref[...]
    queries = query_ref[...]
    grads = grad_ref[...]
    inner = grads.astype(jnp.float32) * out_ref[...].astype(jnp.float32)
    grad_query = jnp.zeros((rows, LANES), jnp.float32)
    for which in range(2):
        grad_head = pick_head(grads, which)
        row_inner = jnp.sum(pick_head(inner, which), axis=1, keepdims=True)
        grad_soft = dot(grad_head, values, NT)
        soft_low = soft_ref[which]
        grad_scores = soft_low.astype(jnp.float32) * (grad_soft - row_inner)
        for part in range(rows // LANES):
            offset = pl.multiple_of(key_count - LANES * (part + 1) - rows * block, LANES)
            skew[which, :, pl.ds(offset, key_count)] += grad_scores[
                LANES * part : LANES * (part + 1)
            ]
        grad_low = grad_scores.astype(jnp.bfloat16)
        grad_query = grad_query + dot(grad_low, pick_head(keys, which))
        key_acc[...] += dot(pick_head(queries, which), grad_low, TN)
        value_acc[...] += dot(grad_head, soft_low, TN)
    own_rows = pl.ds(pl.multiple_of(block * rows, rows), rows)
    own_columns = pl.multiple_of(pair * LANES, LANES)
    grad_qkv_ref[own_rows, pl.ds(own_columns, LANES)] = grad_query.astype(jnp.bfloat16)

    @pl.when(block == pl.num_programs(1) - 1)
    def _():
        grad_qkv_ref[:, pl.ds(columns + own_columns, LANES)] = key_acc[...].T.astype(jnp.bfloat16)
        grad_qkv_ref[:, pl.ds(2 * columns + own_columns, LANES)] = value_acc[...].T.astype(
            jnp.bfloat16
        )
        down = lax.broadcasted_iota(jnp.int32, (LANES, LANES), 0)
        across = lax.broadcasted_iota(jnp.int32, (LANES, LANES), 1)
        flip = (down + across == LANES - 1).astype(jnp.float32)
        for which in range(2):
            turned = lax.dot_general(
                flip,
                skew[which],
                NN,
                precision=lax.Precision.HIGHEST,
                preferred_element_type=jnp.float32,
            )
            rel_ref[0, which : which + 1, :] = jnp.sum(
                pltpu.roll(turned, 0, 1, stride=1, stride_axis=0), axis=0, keepdims=True
            )


def attend_backward(soft_low, qkv, grad_heads, attended, first, last, so_far=()):
    seq_len, columns = attended.shape
    pairs = columns // LANES
    width = 2 * seq_len
    rows = min(BLOCK_ROWS, seq_len)
    row_block = pl.BlockSpec((rows, LANES), lambda pair, block: (block, first + pair))
    whole = pl.BlockSpec((seq_len, 3 * columns), lambda pair, block: (0, 0))
    grad_qkv, rel_grad = pl.pallas_call(
        functools.partial(backward_kernel, first),
        grid=(last - first, seq_len // rows),
        in_specs=[
            pl.BlockSpec((2, rows, seq_len), lambda pair, block: (first + pair, block, 0)),
            row_block,
            row_block,
            row_block,
            pl.BlockSpec((seq_len, LANES), lambda pair, block: (0, pairs + first + pair)),
            pl.BlockSpec((seq_len, LANES), lambda pair, block: (0, 2 * pairs + first + pair)),
        ]
        + [whole] * len(so_far),
        out_specs=[whole, pl.BlockSpec((1, 2, width), lambda pair, block: (pair, 0, 0))],
        scratch_shapes=[
            pltpu.VMEM((2, LANES, width), jnp.float32),
            pltpu.VMEM((LANES, seq_len), jnp.float32),
            pltpu.VMEM((LANES, seq_len), jnp.float32),
        ],
        out_shape=[
            jax.ShapeDtypeStruct((seq_len, 3 * columns), jnp.bfloat16),
            jax.ShapeDtypeStruct((last - first, 2, width), jnp.float32),
        ],
        compiler_params=pltpu.CompilerParams(vmem_limit_bytes=48 << 20),
        cost_estimate=pl.CostEstimate(
            flops=40 * seq_len * seq_len * columns * (last - first) // pairs,
            bytes_accessed=4 * (last - first) * seq_len * seq_len,
            transcendentals=0,
        ),
        name="attend_backward",
    )(soft_low, qkv, grad_heads, attended, qkv, qkv, *so_far)
    return grad_qkv, rel_grad.reshape(2 * (last - first), width)


def around(block):
    count = lax.axis_size("mp")
    return lax.ppermute(block, "mp", [(i, (i + 1) % count) for i in range(count)])


def together(*values):
    return lax.optimization_barrier(values)


def ring_gather(own):
    blocks = [own]
    for _ in range(lax.axis_size("mp") - 1):
        blocks.append(around(blocks[-1]))
    return blocks


def add_low(received, term):
    return (received.astype(jnp.float32) + term).astype(jnp.bfloat16)


def ring_scatter(part_of):
    count = lax.axis_size("mp")
    running = part_of(1).astype(jnp.bfloat16)
    for step in range(2, count):
        received, term = together(around(running), part_of(step))
        running = add_low(received, term)
    received, term = together(around(running), part_of(0))
    return received.astype(jnp.float32) + term


def total_over(value, axis):
    count = lax.axis_size(axis)
    apart = 1
    while apart < count:
        value = value + lax.ppermute(value, axis, [(i, i ^ apart) for i in range(count)])
        apart *= 2
    return value


def update(moment, grad_owned, factor):
    return 0.5 * moment + (0.5 * factor) * grad_owned


def shards(
    layer_input,
    output_grad,
    seq_lengths,
    deal_order,
    bucket_index,
    query_weight,
    key_weight,
    value_weight,
    out_weight,
    gate_weight,
    up_weight,
    down_weight,
    attn_gain,
    ffn_gain,
    bias_table,
    query_moment,
    key_moment,
    value_moment,
    out_moment,
    gate_moment,
    up_moment,
    down_moment,
    attn_gain_moment,
    ffn_gain_moment,
    table_moment,
):
    low = jnp.bfloat16
    f32 = jnp.float32
    group_index = lax.axis_index("dp")
    member = lax.axis_index("mp")
    group_count = lax.axis_size("dp")
    tensor_count = lax.axis_size("mp")

    def back(step):
        return lax.rem(member - step + tensor_count, tensor_count)

    qkv_weight = jnp.concatenate([query_weight, key_weight, value_weight], axis=1).astype(low)
    picked = jnp.take(layer_input, deal_order, axis=0)
    picked, qkv_weight = lax.optimization_barrier((picked, qkv_weight))
    dealt = lax.all_to_all(picked, "dp", split_axis=0, concat_axis=0, tiled=True)
    x_own = dealt.reshape(-1, dealt.shape[2])
    length = seq_lengths[deal_order[group_index]]
    seq_len, quarter = x_own.shape
    features = quarter * tensor_count
    part_rows = seq_len // tensor_count
    row_valid = lax.broadcasted_iota(jnp.int32, (seq_len, 1), 0) < length

    def row_part(array, step):
        return lax.dynamic_slice_in_dim(array, back(step) * part_rows, part_rows, 0)

    def column_part(array, step):
        return lax.dynamic_slice_in_dim(array, back(step) * quarter, quarter, 1)

    def set_rows(whole, part, step):
        return lax.dynamic_update_slice_in_dim(whole, part, back(step) * part_rows, 0)

    def whole_columns(parts):
        whole = jnp.zeros((seq_len, features), parts[0].dtype)
        for step, part in enumerate(parts):
            whole = lax.dynamic_update_slice_in_dim(whole, part, back(step) * quarter, 1)
        return whole

    small = jnp.concatenate([attn_gain, ffn_gain, bias_table.reshape(-1)]).astype(low)
    small = lax.all_gather(small, "dp", axis=0)
    gain_size = attn_gain.shape[0]
    first_gain = small[:, :gain_size].reshape(-1).astype(f32)
    second_gain = small[:, gain_size : 2 * gain_size].reshape(-1).astype(f32)
    full_table = small[:, 2 * gain_size :].reshape(NB, bias_table.shape[1])
    qkv_weight = lax.all_gather(qkv_weight, "dp", axis=0, tiled=True)
    gate_up = jnp.concatenate([gate_weight, up_weight], axis=1).astype(low)
    out_down = jnp.concatenate([out_weight, down_weight], axis=0).astype(low)
    heads_columns = out_weight.shape[0]
    units = down_weight.shape[0]
    out_down, x_own = together(out_down, x_own)
    out_down = lax.all_gather(out_down, "dp", axis=1, tiled=True)

    def down_columns(step):
        return lax.dynamic_slice(
            out_down, (heads_columns, back(step) * quarter), (units, quarter)
        )

    x_parts = ring_gather(x_own)
    gate_up, x_parts[1] = together(gate_up, x_parts[1])
    gate_up = lax.all_gather(gate_up, "dp", axis=0, tiled=True)
    grad_own = jnp.where(row_valid, output_grad[0], jnp.zeros((), low))
    grad_own, x_parts[-1] = together(grad_own, x_parts[-1])
    x_rows = whole_columns(x_parts)
    grad_parts = [grad_own, around(grad_own)]

    offsets = jnp.concatenate([bucket_index, jnp.full((1,), NB, jnp.int32)])
    bucket_hot = offsets[:, None] == lax.broadcasted_iota(jnp.int32, (2 * seq_len, NB), 1)
    rel_rows = dot(full_table, bucket_hot.astype(low), (((0,), (1,)), ((), ())))

    x_float = x_rows.astype(f32)
    inv_first = lax.rsqrt(jnp.mean(x_float * x_float, axis=-1, keepdims=True) + EPS)
    h_first = (x_float * inv_first * first_gain).astype(low)
    qkv = dot(h_first, qkv_weight).astype(low)
    pairs = heads_columns // LANES
    half = pairs // 2
    so_far = attend_forward(qkv, rel_rows, length, 0, half)
    rel_rows, grad_parts[1], *so_far = lax.optimization_barrier((rel_rows, grad_parts[1], *so_far))
    grad_parts.append(around(grad_parts[1]))
    attended, soft_low = attend_forward(qkv, rel_rows, length, half, pairs, so_far)
    attended, grad_parts[2] = together(attended, grad_parts[2])
    grad_parts.append(around(grad_parts[2]))
    attn_branch = ring_scatter(
        lambda step: dot(row_part(attended, step), out_down[:heads_columns])
    )
    attn_branch, *grad_parts = together(attn_branch, *grad_parts)
    grad_y = whole_columns(grad_parts)

    after_attn = row_part(x_rows, 0).astype(f32) + attn_branch
    inv_second = lax.rsqrt(jnp.mean(after_attn * after_attn, axis=-1, keepdims=True) + EPS)
    h_second = (after_attn * inv_second * second_gain).astype(low)

    h_parts = [h_second]
    hidden = jnp.zeros((seq_len, units), low)
    gate_up_grads = []
    terms = {}

    def normed_part(step):
        return dot(gate_up_grads[step], gate_up, NT)

    for step in range(tensor_count):
        if step == 1:
            h_parts[1], gate_up_grads[0] = together(h_parts[1], gate_up_grads[0])
        elif step == 2:
            h_parts[2], gate_up_grads[1], terms[0] = together(
                h_parts[2], gate_up_grads[1], normed_part(0)
            )
        elif step == 3:
            h_parts[3], gate_up_grads[2], terms[1] = together(
                h_parts[3], gate_up_grads[2], normed_part(1).astype(low)
            )
            running = around(terms[1])
        if step < tensor_count - 1:
            h_parts.append(around(h_parts[step]))
        both = dot(h_parts[step], gate_up)
        mixed, mix_back = jax.vjp(
            lambda gate_in, up_in: jax.nn.gelu(gate_in, approximate=True) * up_in,
            both[:, :units],
            both[:, units:],
        )
        hidden = set_rows(hidden, mixed.astype(low), step)
        grad_hidden = dot(row_part(grad_y, step), out_down[heads_columns:], NT)
        gate_up_grads.append(jnp.concatenate(mix_back(grad_hidden), axis=1).astype(low))

    received, terms[2], gate_up_grads[3] = together(running, normed_part(2), gate_up_grads[3])
    running = around(add_low(received, terms[2]))
    h_rotated = jnp.concatenate(h_parts, axis=0)
    grads_rotated = jnp.concatenate(gate_up_grads, axis=0)
    grad_gate_up = dot(h_rotated, grads_rotated, TN).astype(low)
    received, terms[3], grad_gate_up = together(running, normed_part(3), grad_gate_up)
    owned_gate_up = lax.psum_scatter(grad_gate_up, "dp", scatter_dimension=0, tiled=True)
    running = around(add_low(received, terms[3]))
    grad_down = dot(hidden, grad_y, TN).astype(low)
    received, terms[0], grad_down, hidden = together(running, terms[0], grad_down, hidden)
    owned_down = lax.psum_scatter(grad_down, "dp", scatter_dimension=1, tiled=True)
    grad_h_second = received.astype(f32) + terms[0]

    grad_ffn_gain = jnp.sum(grad_h_second * (after_attn * inv_second), axis=0)
    weighted = grad_h_second * second_gain
    row_inner = jnp.mean(weighted * after_attn, axis=-1, keepdims=True)
    grad_after = (
        row_part(grad_y, 0).astype(f32)
        + inv_second * weighted
        - after_attn * (inv_second * inv_second * inv_second) * row_inner
    ).astype(low)

    def output_part(step):
        part = dot(hidden, down_columns(step))
        mine = row_part(part, 0) + column_part(after_attn, step)
        return set_rows(part, mine, 0)

    after_parts = [grad_after]
    after_parts.append(around(after_parts[0]))
    output_terms = [output_part(step) for step in range(tensor_count)]
    after_parts[1], output_terms[1], output_terms[2] = together(
        after_parts[1], output_terms[1], output_terms[2]
    )
    after_parts.append(around(after_parts[1]))
    after_parts[2], output_terms[3], output_terms[0] = together(
        after_parts[2], output_terms[3], output_terms[0]
    )
    after_parts.append(around(after_parts[2]))
    grad_after = jnp.zeros((seq_len, features), low)
    grad_heads = jnp.zeros((seq_len, heads_columns), low)
    for step in range(tensor_count):
        if step == tensor_count - 1:
            grad_after, grad_heads, after_parts[step] = together(
                grad_after, grad_heads, after_parts[step]
            )
        part = after_parts[step]
        grad_after = set_rows(grad_after, part, step)
        grad_heads = set_rows(grad_heads, dot(part, out_down[:heads_columns], NT).astype(low), step)
    output_first = output_terms[1].astype(low)
    output_first, grad_after, grad_heads = together(output_first, grad_after, grad_heads)
    output_sum = around(output_first)
    grad_out = dot(attended, grad_after, TN).astype(low)
    grad_out, grad_heads = together(grad_out, grad_heads)
    owned_out = lax.psum_scatter(grad_out, "dp", scatter_dimension=1, tiled=True)

    def square_sum(piece):
        return jnp.sum(jnp.square(piece.astype(f32)))

    first_grads, first_rel = attend_backward(soft_low, qkv, grad_heads, attended, 0, half)
    output_sum, first_grads, early_sq = together(
        output_sum, first_grads, square_sum(owned_gate_up)
    )
    output_sum = around(add_low(output_sum, output_terms[2]))
    grad_qkv, second_rel = attend_backward(
        soft_low, qkv, grad_heads, attended, half, pairs, (first_grads,)
    )
    rel_grad = jnp.concatenate([first_rel, second_rel], axis=0)
    grad_qkv, output_sum, down_sq = together(grad_qkv, output_sum, square_sum(owned_down))

    def first_part(step):
        weight = lax.dynamic_slice_in_dim(qkv_weight, back(step) * quarter, quarter, 0)
        return dot(grad_qkv, weight, NT)

    running, grad_qkv = together(first_part(1).astype(low), grad_qkv)
    running = around(running)
    grad_qkv_weight = dot(h_first, grad_qkv, TN).astype(low)
    owned_qkv = lax.psum_scatter(grad_qkv_weight, "dp", scatter_dimension=0, tiled=True)
    received, term, grad_qkv_weight = together(running, first_part(2), grad_qkv_weight)
    running = around(add_low(received, term))
    inner = jnp.sum(grad_qkv.astype(f32) * qkv.astype(f32), axis=-1)
    inner = total_over(inner.reshape(-1, LANES), "mp").reshape(-1, 1) / features
    received, term = together(running, first_part(3))
    running = around(add_low(received, term))
    grad_table = lax.dot_general(
        bucket_hot.astype(f32),
        rel_grad,
        (((0,), (1,)), ((), ())),
        precision=lax.Precision.HIGHEST,
        preferred_element_type=f32,
    )
    early_sq = early_sq + down_sq + square_sum(owned_out)
    received, term, grad_table, early_sq, inner = together(
        running, first_part(0), grad_table, early_sq, inner
    )
    received, term, output_sum = together(received, term, output_sum)
    for step in range(3, tensor_count):
        output_sum = around(add_low(output_sum, output_terms[step]))
    grad_h_first = received.astype(f32) + term
    own_gain = lax.dynamic_slice_in_dim(first_gain, member * quarter, quarter, 0)
    x_own = x_own.astype(f32)
    grad_attn_gain = jnp.sum(grad_h_first * (x_own * inv_first), axis=0)
    grad_input = (
        column_part(grad_after, 0).astype(f32)
        + inv_first * (grad_h_first * own_gain)
        - x_own * (inv_first * inv_first) * inner
    ).astype(low)
    came_back = lax.all_to_all(
        grad_input.reshape(group_count, -1, quarter), "dp", split_axis=0, concat_axis=0, tiled=True
    )
    group_iota = lax.broadcasted_iota(jnp.int32, (group_count, group_count), 0)
    place = jnp.argmax(deal_order[None, :] == group_iota, axis=1)
    input_grad = jnp.take(came_back, place, axis=0)

    local_sq = early_sq + square_sum(owned_qkv)
    heads_dev = bias_table.shape[1]
    first_wide = lax.dynamic_update_slice_in_dim(
        jnp.zeros((features,), f32), grad_attn_gain, member * quarter, 0
    )
    table_wide = lax.dynamic_update_slice_in_dim(
        jnp.zeros((NB, heads_dev * tensor_count), f32), grad_table, member * heads_dev, 1
    )
    sums = jnp.concatenate([first_wide, grad_ffn_gain, table_wide.reshape(-1)])
    small_count = sums.shape[0]
    sums = jnp.concatenate([sums, jnp.broadcast_to(local_sq, (LANES,))])
    sums = total_over(sums.reshape(-1, LANES), "dp")
    sums, output_sum = together(sums, output_sum)
    layer_out = (output_sum.astype(f32) + output_terms[0]).astype(low)[None]
    sums = total_over(sums, "mp").reshape(-1)
    total_sq = sums[small_count] + jnp.sum(sums[:small_count] * sums[:small_count])
    grad_norm = jnp.sqrt(total_sq)
    limit = math.sqrt(4 * D * H * DH + 3 * D * FF + 2 * D + NB * H)
    factor = jnp.minimum(1.0, limit / grad_norm)
    owned_first = lax.dynamic_slice_in_dim(sums, group_index * gain_size, gain_size, 0)
    owned_second = lax.dynamic_slice_in_dim(
        sums, features + group_index * gain_size, gain_size, 0
    )
    table_rows = bias_table.shape[0]
    owned_table = lax.dynamic_slice(
        sums[2 * features : small_count].reshape(NB, heads_dev * tensor_count),
        (group_index * table_rows, member * heads_dev),
        (table_rows, heads_dev),
    )
    return (
        layer_out,
        input_grad,
        grad_norm,
        update(query_moment, owned_qkv[:, :heads_columns], factor),
        update(key_moment, owned_qkv[:, heads_columns : 2 * heads_columns], factor),
        update(value_moment, owned_qkv[:, 2 * heads_columns :], factor),
        update(out_moment, owned_out, factor),
        update(gate_moment, owned_gate_up[:, :units], factor),
        update(up_moment, owned_gate_up[:, units:], factor),
        update(down_moment, owned_down, factor),
        update(attn_gain_moment, owned_first, factor),
        update(ffn_gain_moment, owned_second, factor),
        update(table_moment, owned_table, factor),
    )


def solution(mesh):
    in_specs = (
        P(None, "dp", "mp"),
        P("dp", None, "mp"),
        P(),
        P(),
        P(),
        P("dp", "mp"),
        P("dp", "mp"),
        P("dp", "mp"),
        P("mp", "dp"),
        P("dp", "mp"),
        P("dp", "mp"),
        P("mp", "dp"),
        P("dp"),
        P("dp"),
        P("dp", "mp"),
        P("dp", "mp"),
        P("dp", "mp"),
        P("dp", "mp"),
        P("mp", "dp"),
        P("dp", "mp"),
        P("dp", "mp"),
        P("mp", "dp"),
        P("dp"),
        P("dp"),
        P("dp", "mp"),
    )
    out_specs = (
        P("dp", None, "mp"),
        P(None, "dp", "mp"),
        P(),
        P("dp", "mp"),
        P("dp", "mp"),
        P("dp", "mp"),
        P("mp", "dp"),
        P("dp", "mp"),
        P("dp", "mp"),
        P("mp", "dp"),
        P("dp"),
        P("dp"),
        P("dp", "mp"),
    )
    return jax.shard_map(shards, mesh=mesh, in_specs=in_specs, out_specs=out_specs, check_vma=False)
```

```python
import functools
import math

import jax
import jax.numpy as jnp
from jax import lax
from jax.experimental import pallas as pl
from jax.experimental.pallas import tpu as pltpu
from jax.sharding import PartitionSpec as P

D = 2048
H = 32
DH = 64
FF = 5120
NB = 32


EPS = 1e-06
NEG = -1e30
LANES = 128
BLOCK_ROWS = 256

NN = (((1,), (0,)), ((), ()))
NT = (((1,), (1,)), ((), ()))
TN = (((0,), (0,)), ((), ()))


def dot(left, right, dims=NN):
    return lax.dot_general(left, right, dims, preferred_element_type=jnp.float32)


def pick_head(pair_rows, which):
    lane = lax.broadcasted_iota(jnp.int32, (1, LANES), 1)
    return jnp.where(lane // DH == which, pair_rows, jnp.zeros_like(pair_rows))


def forward_kernel(length, rel_ref, query_ref, key_ref, value_ref, out_ref, soft_ref, skew):
    block = pl.program_id(1)
    rows = query_ref.shape[0]
    key_count = key_ref.shape[0]
    width = rel_ref.shape[2]

    @pl.when(block == 0)
    def _():
        for which in range(2):
            spread = jnp.broadcast_to(rel_ref[0, which : which + 1, :], (LANES, width))
            skew[which] = pltpu.roll(spread, width - (LANES - 1), 1, stride=1, stride_axis=0)

    key_at = lax.broadcasted_iota(jnp.int32, (1, key_count), 1)
    key_mask = jnp.where(key_at < length[0], 0.0, NEG)
    keys = key_ref[...]
    values = value_ref[...]
    mixed = jnp.zeros((rows, LANES), jnp.float32)
    for which in range(2):
        products = dot(pick_head(query_ref[...], which), keys, NT)
        parts = []
        for part in range(rows // LANES):
            offset = pl.multiple_of(key_count - LANES * (part + 1) - rows * block, LANES)
            parts.append(
                products[LANES * part : LANES * (part + 1)] + skew[which, :, pl.ds(offset, key_count)]
            )
        scores = jnp.concatenate(parts, 0) + key_mask
        exp_terms = jnp.exp(scores - jnp.max(scores, axis=1, keepdims=True))
        total = jnp.sum(exp_terms, axis=1, keepdims=True)
        soft_low = (exp_terms * (1.0 / total)).astype(jnp.bfloat16)
        soft_ref[which] = soft_low
        mixed = mixed + dot(soft_low, pick_head(values, which))
    out_ref[...] = mixed.astype(jnp.bfloat16)


def attend_forward(qkv, rel_rows, length, first, last, so_far=None):
    seq_len = qkv.shape[0]
    columns = qkv.shape[1] // 3
    pairs = columns // LANES
    width = rel_rows.shape[1]
    rows = min(BLOCK_ROWS, seq_len)
    kernel = forward_kernel
    operands = [length.reshape(1), rel_rows.reshape(pairs, 2, width), qkv, qkv, qkv]
    in_specs = [
        pl.BlockSpec((1, 2, width), lambda pair, block, n: (first + pair, 0, 0)),
        pl.BlockSpec((rows, LANES), lambda pair, block, n: (block, first + pair)),
        pl.BlockSpec((seq_len, LANES), lambda pair, block, n: (0, pairs + first + pair)),
        pl.BlockSpec((seq_len, LANES), lambda pair, block, n: (0, 2 * pairs + first + pair)),
    ]
    aliases = {}
    if so_far is not None:
        kernel = second_forward_kernel
        operands += so_far
        in_specs += [pl.BlockSpec(memory_space=pl.ANY)] * 2
        aliases = {5: 0, 6: 1}
    return pl.pallas_call(
        kernel,
        grid_spec=pltpu.PrefetchScalarGridSpec(
            num_scalar_prefetch=1,
            grid=(last - first, seq_len // rows),
            in_specs=in_specs,
            out_specs=[
                pl.BlockSpec((rows, LANES), lambda pair, block, n: (block, first + pair)),
                pl.BlockSpec((2, rows, seq_len), lambda pair, block, n: (first + pair, block, 0)),
            ],
            scratch_shapes=[pltpu.VMEM((2, LANES, width), jnp.float32)],
        ),
        out_shape=[
            jax.ShapeDtypeStruct((seq_len, columns), jnp.bfloat16),
            jax.ShapeDtypeStruct((2 * pairs, seq_len, seq_len), jnp.bfloat16),
        ],
        input_output_aliases=aliases,
        compiler_params=pltpu.CompilerParams(vmem_limit_bytes=40 << 20),
        cost_estimate=pl.CostEstimate(
            flops=16 * seq_len * seq_len * columns * (last - first) // pairs,
            bytes_accessed=4 * (last - first) * seq_len * seq_len,
            transcendentals=2 * (last - first) * seq_len * seq_len,
        ),
        name="attend_forward",
    )(*operands)


def second_forward_kernel(
    length, rel_ref, query_ref, key_ref, value_ref, _, __, out_ref, soft_ref, skew
):
    forward_kernel(length, rel_ref, query_ref, key_ref, value_ref, out_ref, soft_ref, skew)


def backward_kernel(
    first,
    soft_ref,
    query_ref,
    grad_ref,
    out_ref,
    key_ref,
    value_ref,
    *rest,
):
    grad_qkv_ref, rel_ref, skew, key_acc, value_acc = rest[-5:]
    pair = first + pl.program_id(0)
    block = pl.program_id(1)
    rows = query_ref.shape[0]
    key_count = key_ref.shape[0]
    columns = grad_qkv_ref.shape[1] // 3

    @pl.when(block == 0)
    def _():
        skew[...] = jnp.zeros_like(skew)
        key_acc[...] = jnp.zeros_like(key_acc)
        value_acc[...] = jnp.zeros_like(value_acc)

    if len(rest) > 5:

        @pl.when((block == 0) & (pair == first))
        def _():
            grad_qkv_ref[...] = rest[0][...]

    keys = key_ref[...]
    values = value_ref[...]
    queries = query_ref[...]
    grads = grad_ref[...]
    inner = grads.astype(jnp.float32) * out_ref[...].astype(jnp.float32)
    grad_query = jnp.zeros((rows, LANES), jnp.float32)
    for which in range(2):
        grad_head = pick_head(grads, which)
        row_inner = jnp.sum(pick_head(inner, which), axis=1, keepdims=True)
        grad_soft = dot(grad_head, values, NT)
        soft_low = soft_ref[which]
        grad_scores = soft_low.astype(jnp.float32) * (grad_soft - row_inner)
        for part in range(rows // LANES):
            offset = pl.multiple_of(key_count - LANES * (part + 1) - rows * block, LANES)
            skew[which, :, pl.ds(offset, key_count)] += grad_scores[
                LANES * part : LANES * (part + 1)
            ]
        grad_low = grad_scores.astype(jnp.bfloat16)
        grad_query = grad_query + dot(grad_low, pick_head(keys, which))
        key_acc[...] += dot(pick_head(queries, which), grad_low, TN)
        value_acc[...] += dot(grad_head, soft_low, TN)
    own_rows = pl.ds(pl.multiple_of(block * rows, rows), rows)
    own_columns = pl.multiple_of(pair * LANES, LANES)
    grad_qkv_ref[own_rows, pl.ds(own_columns, LANES)] = grad_query.astype(jnp.bfloat16)

    @pl.when(block == pl.num_programs(1) - 1)
    def _():
        grad_qkv_ref[:, pl.ds(columns + own_columns, LANES)] = key_acc[...].T.astype(jnp.bfloat16)
        grad_qkv_ref[:, pl.ds(2 * columns + own_columns, LANES)] = value_acc[...].T.astype(
            jnp.bfloat16
        )
        down = lax.broadcasted_iota(jnp.int32, (LANES, LANES), 0)
        across = lax.broadcasted_iota(jnp.int32, (LANES, LANES), 1)
        flip = (down + across == LANES - 1).astype(jnp.float32)
        for which in range(2):
            turned = lax.dot_general(
                flip,
                skew[which],
                NN,
                precision=lax.Precision.HIGHEST,
                preferred_element_type=jnp.float32,
            )
            rel_ref[0, which : which + 1, :] = jnp.sum(
                pltpu.roll(turned, 0, 1, stride=1, stride_axis=0), axis=0, keepdims=True
            )


def attend_backward(soft_low, qkv, grad_heads, attended, first, last, so_far=()):
    seq_len, columns = attended.shape
    pairs = columns // LANES
    width = 2 * seq_len
    rows = min(BLOCK_ROWS, seq_len)
    row_block = pl.BlockSpec((rows, LANES), lambda pair, block: (block, first + pair))
    whole = pl.BlockSpec((seq_len, 3 * columns), lambda pair, block: (0, 0))
    grad_qkv, rel_grad = pl.pallas_call(
        functools.partial(backward_kernel, first),
        grid=(last - first, seq_len // rows),
        in_specs=[
            pl.BlockSpec((2, rows, seq_len), lambda pair, block: (first + pair, block, 0)),
            row_block,
            row_block,
            row_block,
            pl.BlockSpec((seq_len, LANES), lambda pair, block: (0, pairs + first + pair)),
            pl.BlockSpec((seq_len, LANES), lambda pair, block: (0, 2 * pairs + first + pair)),
        ]
        + [whole] * len(so_far),
        out_specs=[whole, pl.BlockSpec((1, 2, width), lambda pair, block: (pair, 0, 0))],
        scratch_shapes=[
            pltpu.VMEM((2, LANES, width), jnp.float32),
            pltpu.VMEM((LANES, seq_len), jnp.float32),
            pltpu.VMEM((LANES, seq_len), jnp.float32),
        ],
        out_shape=[
            jax.ShapeDtypeStruct((seq_len, 3 * columns), jnp.bfloat16),
            jax.ShapeDtypeStruct((last - first, 2, width), jnp.float32),
        ],
        compiler_params=pltpu.CompilerParams(vmem_limit_bytes=48 << 20),
        cost_estimate=pl.CostEstimate(
            flops=40 * seq_len * seq_len * columns * (last - first) // pairs,
            bytes_accessed=4 * (last - first) * seq_len * seq_len,
            transcendentals=0,
        ),
        name="attend_backward",
    )(soft_low, qkv, grad_heads, attended, qkv, qkv, *so_far)
    return grad_qkv, rel_grad.reshape(2 * (last - first), width)


def around(block):
    count = lax.axis_size("mp")
    return lax.ppermute(block, "mp", [(i, (i + 1) % count) for i in range(count)])


def together(*values):
    return lax.optimization_barrier(values)


def ring_gather(own):
    blocks = [own]
    for _ in range(lax.axis_size("mp") - 1):
        blocks.append(around(blocks[-1]))
    return blocks


def add_low(received, term):
    return (received.astype(jnp.float32) + term).astype(jnp.bfloat16)


def ring_scatter(part_of):
    count = lax.axis_size("mp")
    running = part_of(1).astype(jnp.bfloat16)
    for step in range(2, count):
        received, term = together(around(running), part_of(step))
        running = add_low(received, term)
    received, term = together(around(running), part_of(0))
    return received.astype(jnp.float32) + term


def total_over(value, axis):
    count = lax.axis_size(axis)
    apart = 1
    while apart < count:
        value = value + lax.ppermute(value, axis, [(i, i ^ apart) for i in range(count)])
        apart *= 2
    return value


def update(moment, grad_owned, factor):
    return 0.5 * moment + (0.5 * factor) * grad_owned


def shards(
    layer_input,
    output_grad,
    seq_lengths,
    deal_order,
    bucket_index,
    query_weight,
    key_weight,
    value_weight,
    out_weight,
    gate_weight,
    up_weight,
    down_weight,
    attn_gain,
    ffn_gain,
    bias_table,
    query_moment,
    key_moment,
    value_moment,
    out_moment,
    gate_moment,
    up_moment,
    down_moment,
    attn_gain_moment,
    ffn_gain_moment,
    table_moment,
):
    low = jnp.bfloat16
    f32 = jnp.float32
    group_index = lax.axis_index("dp")
    member = lax.axis_index("mp")
    group_count = lax.axis_size("dp")
    tensor_count = lax.axis_size("mp")

    def back(step):
        return lax.rem(member - step + tensor_count, tensor_count)

    picked = jnp.take(layer_input, deal_order, axis=0)
    dealt = lax.all_to_all(picked, "dp", split_axis=0, concat_axis=0, tiled=True)
    x_own = dealt.reshape(-1, dealt.shape[2])
    length = seq_lengths[deal_order[group_index]]
    seq_len, quarter = x_own.shape
    features = quarter * tensor_count
    part_rows = seq_len // tensor_count

    small = jnp.concatenate([attn_gain, ffn_gain, bias_table.reshape(-1)]).astype(low)
    x_own, grad_next, small = together(
        x_own, around(output_grad[0]), lax.all_gather(small, "dp", axis=0)
    )
    grad_parts = [output_grad[0], grad_next]
    row_valid = lax.broadcasted_iota(jnp.int32, (seq_len, 1), 0) < length

    def valid_rows(part):
        return jnp.where(row_valid, part, jnp.zeros((), low))

    def row_part(array, step):
        return lax.dynamic_slice_in_dim(array, back(step) * part_rows, part_rows, 0)

    def column_part(array, step):
        return lax.dynamic_slice_in_dim(array, back(step) * quarter, quarter, 1)

    def set_rows(whole, part, step):
        return lax.dynamic_update_slice_in_dim(whole, part, back(step) * part_rows, 0)

    def set_columns(whole, part, step):
        return lax.dynamic_update_slice_in_dim(whole, part, back(step) * quarter, 1)

    def whole_columns(parts, start):
        whole = jnp.broadcast_to(start[:1, :1], (seq_len, features))
        for step, part in enumerate(parts):
            whole = set_columns(whole, part, step)
        return whole

    gain_size = attn_gain.shape[0]
    first_gain = small[:, :gain_size].reshape(-1).astype(f32)
    second_gain = small[:, gain_size : 2 * gain_size].reshape(-1).astype(f32)
    full_table = small[:, 2 * gain_size :].reshape(NB, bias_table.shape[1])
    qkv_weight = jnp.concatenate([query_weight, key_weight, value_weight], axis=1).astype(low)
    qkv_weight, x_own = together(qkv_weight, x_own)
    qkv_weight = lax.all_gather(qkv_weight, "dp", axis=0, tiled=True)
    gate_up = jnp.concatenate([gate_weight, up_weight], axis=1).astype(low)
    out_down = jnp.concatenate([out_weight, down_weight], axis=0).astype(low)
    heads_columns = out_weight.shape[0]
    units = down_weight.shape[0]
    x_parts = ring_gather(x_own)
    out_down, x_parts[1] = together(out_down, x_parts[1])
    out_down = lax.all_gather(out_down, "dp", axis=1, tiled=True)
    gate_up, x_parts[2] = together(gate_up, x_parts[2])
    gate_up = lax.all_gather(gate_up, "dp", axis=0, tiled=True)

    def down_columns(step):
        return lax.dynamic_slice(
            out_down, (heads_columns, back(step) * quarter), (units, quarter)
        )

    grad_parts[1], x_parts[-1] = together(grad_parts[1], x_parts[-1])
    x_rows = whole_columns(x_parts, x_own)
    grad_parts.append(around(grad_parts[1]))

    offsets = jnp.concatenate([bucket_index, jnp.full((1,), NB, jnp.int32)])
    bucket_hot = offsets[:, None] == lax.broadcasted_iota(jnp.int32, (2 * seq_len, NB), 1)
    rel_rows = dot(full_table, bucket_hot.astype(low), (((0,), (1,)), ((), ())))

    x_float = x_rows.astype(f32)
    inv_first = lax.rsqrt(jnp.mean(x_float * x_float, axis=-1, keepdims=True) + EPS)
    h_first = (x_float * inv_first * first_gain).astype(low)
    qkv = dot(h_first, qkv_weight).astype(low)
    pairs = heads_columns // LANES
    so_far = attend_forward(qkv, rel_rows, length, 0, 1)
    rel_rows, grad_parts[2], *so_far = together(rel_rows, grad_parts[2], *so_far)
    grad_parts.append(around(grad_parts[2]))
    attended, soft_low = attend_forward(qkv, rel_rows, length, 1, pairs, so_far)
    attended, grad_parts[3] = together(attended, grad_parts[3])

    def attended_part(step):
        return dot(row_part(attended, step), out_down[:heads_columns])

    running = around(attended_part(1).astype(low))
    grad_y = whole_columns([valid_rows(part) for part in grad_parts[:-1]], attended)
    received, term, grad_y = together(running, attended_part(2), grad_y)
    running = around(add_low(received, term))
    grad_y = set_columns(grad_y, valid_rows(grad_parts[-1]), tensor_count - 1)
    received, term, last_term, grad_y = together(
        running, attended_part(3), attended_part(0), grad_y
    )
    running = around(add_low(received, term))
    attn_branch = running.astype(f32) + last_term

    after_attn = row_part(x_rows, 0).astype(f32) + attn_branch
    inv_second = lax.rsqrt(jnp.mean(after_attn * after_attn, axis=-1, keepdims=True) + EPS)
    h_second = (after_attn * inv_second * second_gain).astype(low)

    h_parts = [h_second]
    hidden = jnp.broadcast_to(h_second[:1, :1], (seq_len, units))
    gate_up_grads = []
    terms = {}

    def square_sum(piece):
        return jnp.sum(jnp.square(piece.astype(f32)))

    def normed_part(step):
        return dot(gate_up_grads[step], gate_up, NT)

    for step in range(tensor_count):
        if step == 1:
            h_parts[1], gate_up_grads[0], hidden = together(h_parts[1], gate_up_grads[0], hidden)
        elif step == 2:
            h_parts[2], gate_up_grads[1], hidden, terms[0] = together(
                h_parts[2], gate_up_grads[1], hidden, normed_part(0)
            )
        elif step == 3:
            h_parts[3], gate_up_grads[2], hidden, terms[1] = together(
                h_parts[3], gate_up_grads[2], hidden, normed_part(1).astype(low)
            )
            running = around(terms[1])
        if step < tensor_count - 1:
            h_parts.append(around(h_parts[step]))
        both = dot(h_parts[step], gate_up)
        mixed, mix_back = jax.vjp(
            lambda gate_in, up_in: jax.nn.gelu(gate_in, approximate=True) * up_in,
            both[:, :units],
            both[:, units:],
        )
        hidden = set_rows(hidden, mixed.astype(low), step)
        grad_hidden = dot(row_part(grad_y, step), out_down[heads_columns:], NT)
        gate_up_grads.append(jnp.concatenate(mix_back(grad_hidden), axis=1).astype(low))

    received, terms[2], terms[3], gate_up_grads[3], hidden = together(
        running, normed_part(2), normed_part(3), gate_up_grads[3], hidden
    )
    running = around(add_low(received, terms[2]))
    h_rotated = jnp.concatenate(h_parts, axis=0)
    grads_rotated = jnp.concatenate(gate_up_grads, axis=0)
    grad_gate_up = dot(h_rotated, grads_rotated, TN).astype(low)
    received, grad_gate_up = together(running, grad_gate_up)
    owned_gate_up = lax.psum_scatter(grad_gate_up, "dp", scatter_dimension=0, tiled=True)
    running = around(add_low(received, terms[3]))
    grad_down = dot(hidden, grad_y, TN).astype(low)
    received, terms[0], grad_down, hidden = together(running, terms[0], grad_down, hidden)
    owned_down = lax.psum_scatter(grad_down, "dp", scatter_dimension=1, tiled=True)
    grad_h_second = received.astype(f32) + terms[0]

    grad_ffn_gain = jnp.sum(grad_h_second * (after_attn * inv_second), axis=0)
    weighted = grad_h_second * second_gain
    row_inner = jnp.mean(weighted * after_attn, axis=-1, keepdims=True)
    grad_after = (
        row_part(grad_y, 0).astype(f32)
        + inv_second * weighted
        - after_attn * (inv_second * inv_second * inv_second) * row_inner
    ).astype(low)

    def output_part(step):
        part = dot(hidden, down_columns(step))
        mine = row_part(part, 0) + column_part(after_attn, step)
        return set_rows(part, mine, 0)

    after_parts = [grad_after]
    after_parts.append(around(after_parts[0]))
    output_terms = [output_part(step) for step in range(tensor_count)]
    after_parts[1], output_terms[1], output_terms[2] = together(
        after_parts[1], output_terms[1], output_terms[2]
    )
    after_parts.append(around(after_parts[1]))
    after_parts[2], output_terms[3], output_terms[0] = together(
        after_parts[2], output_terms[3], output_terms[0]
    )
    after_parts.append(around(after_parts[2]))
    grad_after = grad_y
    grad_heads = jnp.zeros((seq_len, heads_columns), low)
    for step in range(tensor_count):
        if step == tensor_count - 1:
            grad_after, grad_heads, after_parts[step] = together(
                grad_after, grad_heads, after_parts[step]
            )
        part = after_parts[step]
        grad_after = set_rows(grad_after, part, step)
        grad_heads = set_rows(grad_heads, dot(part, out_down[:heads_columns], NT).astype(low), step)
    output_first = output_terms[1].astype(low)
    output_first, grad_after, grad_heads = together(output_first, grad_after, grad_heads)
    output_sum = around(output_first)

    half = pairs // 2
    first_grads, first_rel = attend_backward(soft_low, qkv, grad_heads, attended, 0, half)
    output_sum, first_grads, owned_gate_up = together(output_sum, first_grads, owned_gate_up)
    output_sum = around(add_low(output_sum, output_terms[2]))
    grad_out = dot(attended, grad_after, TN).astype(low)
    first_grads, grad_out = together(first_grads, grad_out)
    owned_out = lax.psum_scatter(grad_out, "dp", scatter_dimension=1, tiled=True)
    grad_qkv, second_rel = attend_backward(
        soft_low, qkv, grad_heads, attended, half, pairs, (first_grads,)
    )
    rel_grad = jnp.concatenate([first_rel, second_rel], axis=0)
    grad_qkv, output_sum, owned_down = together(grad_qkv, output_sum, owned_down)
    output_sent = add_low(output_sum, output_terms[3])

    def first_part(step):
        weight = lax.dynamic_slice_in_dim(qkv_weight, back(step) * quarter, quarter, 0)
        return dot(grad_qkv, weight, NT)

    running, grad_qkv = together(first_part(1).astype(low), grad_qkv)
    running = around(running)
    grad_qkv_weight = dot(h_first, grad_qkv, TN).astype(low)
    received, term, grad_qkv_weight = together(running, first_part(2), grad_qkv_weight)
    owned_qkv = lax.psum_scatter(grad_qkv_weight, "dp", scatter_dimension=0, tiled=True)
    running = around(add_low(received, term))
    inner = jnp.sum(grad_qkv.astype(f32) * qkv.astype(f32), axis=-1)
    inner = total_over(inner.reshape(-1, LANES), "mp").reshape(-1, 1) / features
    received, term, owned_out = together(running, first_part(3), owned_out)
    running = around(add_low(received, term))
    grad_table = lax.dot_general(
        bucket_hot.astype(f32),
        rel_grad,
        (((0,), (1,)), ((), ())),
        precision=lax.Precision.HIGHEST,
        preferred_element_type=f32,
    )
    early_sq = square_sum(owned_gate_up) + square_sum(owned_down) + square_sum(owned_out)
    received, term, grad_table, early_sq, inner, output_sent = together(
        running, first_part(0), grad_table, early_sq, inner, output_sent
    )
    output_sum = around(output_sent)
    grad_h_first = received.astype(f32) + term
    own_gain = lax.dynamic_slice_in_dim(first_gain, member * quarter, quarter, 0)
    x_own = x_own.astype(f32)
    grad_attn_gain = jnp.sum(grad_h_first * (x_own * inv_first), axis=0)
    grad_input = (
        column_part(grad_after, 0).astype(f32)
        + inv_first * (grad_h_first * own_gain)
        - x_own * (inv_first * inv_first) * inner
    ).astype(low)
    came_back = lax.all_to_all(
        grad_input.reshape(group_count, -1, quarter), "dp", split_axis=0, concat_axis=0, tiled=True
    )
    group_iota = lax.broadcasted_iota(jnp.int32, (group_count, group_count), 0)
    place = jnp.argmax(deal_order[None, :] == group_iota, axis=1)
    input_grad = jnp.take(came_back, place, axis=0)

    local_sq = early_sq + square_sum(owned_qkv)
    heads_dev = bias_table.shape[1]
    first_wide = lax.dynamic_update_slice_in_dim(
        jnp.zeros((features,), f32), grad_attn_gain, member * quarter, 0
    )
    table_wide = lax.dynamic_update_slice_in_dim(
        jnp.zeros((NB, heads_dev * tensor_count), f32), grad_table, member * heads_dev, 1
    )
    sums = jnp.concatenate([first_wide, grad_ffn_gain, table_wide.reshape(-1)])
    small_count = sums.shape[0]
    sums = jnp.concatenate([sums, jnp.broadcast_to(local_sq, (LANES,))])
    sums = total_over(sums.reshape(-1, LANES), "dp")
    sums, output_sum = together(sums, output_sum)
    layer_out = (output_sum.astype(f32) + output_terms[0]).astype(low)[None]
    sums = total_over(sums, "mp").reshape(-1)
    total_sq = sums[small_count] + jnp.sum(sums[:small_count] * sums[:small_count])
    grad_norm = jnp.sqrt(total_sq)
    limit = math.sqrt(4 * D * H * DH + 3 * D * FF + 2 * D + NB * H)
    factor = jnp.minimum(1.0, limit / grad_norm)
    owned_first = lax.dynamic_slice_in_dim(sums, group_index * gain_size, gain_size, 0)
    owned_second = lax.dynamic_slice_in_dim(
        sums, features + group_index * gain_size, gain_size, 0
    )
    table_rows = bias_table.shape[0]
    owned_table = lax.dynamic_slice(
        sums[2 * features : small_count].reshape(NB, heads_dev * tensor_count),
        (group_index * table_rows, member * heads_dev),
        (table_rows, heads_dev),
    )
    return (
        layer_out,
        input_grad,
        grad_norm,
        update(query_moment, owned_qkv[:, :heads_columns], factor),
        update(key_moment, owned_qkv[:, heads_columns : 2 * heads_columns], factor),
        update(value_moment, owned_qkv[:, 2 * heads_columns :], factor),
        update(out_moment, owned_out, factor),
        update(gate_moment, owned_gate_up[:, :units], factor),
        update(up_moment, owned_gate_up[:, units:], factor),
        update(down_moment, owned_down, factor),
        update(attn_gain_moment, owned_first, factor),
        update(ffn_gain_moment, owned_second, factor),
        update(table_moment, owned_table, factor),
    )


def solution(mesh):
    in_specs = (
        P(None, "dp", "mp"),
        P("dp", None, "mp"),
        P(),
        P(),
        P(),
        P("dp", "mp"),
        P("dp", "mp"),
        P("dp", "mp"),
        P("mp", "dp"),
        P("dp", "mp"),
        P("dp", "mp"),
        P("mp", "dp"),
        P("dp"),
        P("dp"),
        P("dp", "mp"),
        P("dp", "mp"),
        P("dp", "mp"),
        P("dp", "mp"),
        P("mp", "dp"),
        P("dp", "mp"),
        P("dp", "mp"),
        P("mp", "dp"),
        P("dp"),
        P("dp"),
        P("dp", "mp"),
    )
    out_specs = (
        P("dp", None, "mp"),
        P(None, "dp", "mp"),
        P(),
        P("dp", "mp"),
        P("dp", "mp"),
        P("dp", "mp"),
        P("mp", "dp"),
        P("dp", "mp"),
        P("dp", "mp"),
        P("mp", "dp"),
        P("dp"),
        P("dp"),
        P("dp", "mp"),
    )
    return jax.shard_map(shards, mesh=mesh, in_specs=in_specs, out_specs=out_specs, check_vma=False)
```

```python
import functools
import math

import jax
import jax.numpy as jnp
from jax import lax
from jax.experimental import pallas as pl
from jax.experimental.pallas import tpu as pltpu
from jax.sharding import PartitionSpec as P

D = 2048
H = 32
DH = 64
FF = 5120
NB = 32


EPS = 1e-06
NEG = -1e30
LANES = 128
BLOCK_ROWS = 256

NN = (((1,), (0,)), ((), ()))
NT = (((1,), (1,)), ((), ()))
TN = (((0,), (0,)), ((), ()))


def dot(left, right, dims=NN):
    return lax.dot_general(left, right, dims, preferred_element_type=jnp.float32)


def pick_head(pair_rows, which):
    lane = lax.broadcasted_iota(jnp.int32, (1, LANES), 1)
    return jnp.where(lane // DH == which, pair_rows, jnp.zeros_like(pair_rows))


def forward_kernel(length, rel_ref, query_ref, key_ref, value_ref, out_ref, soft_ref, skew):
    block = pl.program_id(1)
    rows = query_ref.shape[0]
    key_count = key_ref.shape[0]
    width = rel_ref.shape[2]

    @pl.when(block == 0)
    def _():
        for which in range(2):
            spread = jnp.broadcast_to(rel_ref[0, which : which + 1, :], (LANES, width))
            skew[which] = pltpu.roll(spread, width - (LANES - 1), 1, stride=1, stride_axis=0)

    key_at = lax.broadcasted_iota(jnp.int32, (1, key_count), 1)
    key_mask = jnp.where(key_at < length[0], 0.0, NEG)
    keys = key_ref[...]
    values = value_ref[...]
    mixed = jnp.zeros((rows, LANES), jnp.float32)
    for which in range(2):
        products = dot(pick_head(query_ref[...], which), keys, NT)
        parts = []
        for part in range(rows // LANES):
            offset = pl.multiple_of(key_count - LANES * (part + 1) - rows * block, LANES)
            parts.append(
                products[LANES * part : LANES * (part + 1)] + skew[which, :, pl.ds(offset, key_count)]
            )
        scores = jnp.concatenate(parts, 0) + key_mask
        exp_terms = jnp.exp(scores - jnp.max(scores, axis=1, keepdims=True))
        total = jnp.sum(exp_terms, axis=1, keepdims=True)
        soft_low = (exp_terms * (1.0 / total)).astype(jnp.bfloat16)
        soft_ref[which] = soft_low
        mixed = mixed + dot(soft_low, pick_head(values, which))
    out_ref[...] = mixed.astype(jnp.bfloat16)


def attend_forward(qkv, rel_rows, length, first, last, so_far=None):
    seq_len = qkv.shape[0]
    columns = qkv.shape[1] // 3
    pairs = columns // LANES
    width = rel_rows.shape[1]
    rows = min(BLOCK_ROWS, seq_len)
    kernel = forward_kernel
    operands = [length.reshape(1), rel_rows.reshape(pairs, 2, width), qkv, qkv, qkv]
    in_specs = [
        pl.BlockSpec((1, 2, width), lambda pair, block, n: (first + pair, 0, 0)),
        pl.BlockSpec((rows, LANES), lambda pair, block, n: (block, first + pair)),
        pl.BlockSpec((seq_len, LANES), lambda pair, block, n: (0, pairs + first + pair)),
        pl.BlockSpec((seq_len, LANES), lambda pair, block, n: (0, 2 * pairs + first + pair)),
    ]
    aliases = {}
    if so_far is not None:
        kernel = second_forward_kernel
        operands += so_far
        in_specs += [pl.BlockSpec(memory_space=pl.ANY)] * 2
        aliases = {5: 0, 6: 1}
    return pl.pallas_call(
        kernel,
        grid_spec=pltpu.PrefetchScalarGridSpec(
            num_scalar_prefetch=1,
            grid=(last - first, seq_len // rows),
            in_specs=in_specs,
            out_specs=[
                pl.BlockSpec((rows, LANES), lambda pair, block, n: (block, first + pair)),
                pl.BlockSpec((2, rows, seq_len), lambda pair, block, n: (first + pair, block, 0)),
            ],
            scratch_shapes=[pltpu.VMEM((2, LANES, width), jnp.float32)],
        ),
        out_shape=[
            jax.ShapeDtypeStruct((seq_len, columns), jnp.bfloat16),
            jax.ShapeDtypeStruct((2 * pairs, seq_len, seq_len), jnp.bfloat16),
        ],
        input_output_aliases=aliases,
        compiler_params=pltpu.CompilerParams(vmem_limit_bytes=40 << 20),
        cost_estimate=pl.CostEstimate(
            flops=16 * seq_len * seq_len * columns * (last - first) // pairs,
            bytes_accessed=4 * (last - first) * seq_len * seq_len,
            transcendentals=2 * (last - first) * seq_len * seq_len,
        ),
        name="attend_forward",
    )(*operands)


def second_forward_kernel(
    length, rel_ref, query_ref, key_ref, value_ref, _, __, out_ref, soft_ref, skew
):
    forward_kernel(length, rel_ref, query_ref, key_ref, value_ref, out_ref, soft_ref, skew)


def backward_kernel(
    first,
    soft_ref,
    query_ref,
    grad_ref,
    out_ref,
    key_ref,
    value_ref,
    *rest,
):
    grad_qkv_ref, rel_ref, skew, key_acc, value_acc = rest[-5:]
    pair = first + pl.program_id(0)
    block = pl.program_id(1)
    rows = query_ref.shape[0]
    key_count = key_ref.shape[0]
    columns = grad_qkv_ref.shape[1] // 3

    @pl.when(block == 0)
    def _():
        skew[...] = jnp.zeros_like(skew)
        key_acc[...] = jnp.zeros_like(key_acc)
        value_acc[...] = jnp.zeros_like(value_acc)

    if len(rest) > 5:

        @pl.when((block == 0) & (pair == first))
        def _():
            grad_qkv_ref[...] = rest[0][...]

    keys = key_ref[...]
    values = value_ref[...]
    queries = query_ref[...]
    grads = grad_ref[...]
    inner = grads.astype(jnp.float32) * out_ref[...].astype(jnp.float32)
    grad_query = jnp.zeros((rows, LANES), jnp.float32)
    for which in range(2):
        grad_head = pick_head(grads, which)
        row_inner = jnp.sum(pick_head(inner, which), axis=1, keepdims=True)
        grad_soft = dot(grad_head, values, NT)
        soft_low = soft_ref[which]
        grad_scores = soft_low.astype(jnp.float32) * (grad_soft - row_inner)
        for part in range(rows // LANES):
            offset = pl.multiple_of(key_count - LANES * (part + 1) - rows * block, LANES)
            skew[which, :, pl.ds(offset, key_count)] += grad_scores[
                LANES * part : LANES * (part + 1)
            ]
        grad_low = grad_scores.astype(jnp.bfloat16)
        grad_query = grad_query + dot(grad_low, pick_head(keys, which))
        key_acc[...] += dot(pick_head(queries, which), grad_low, TN)
        value_acc[...] += dot(grad_head, soft_low, TN)
    own_rows = pl.ds(pl.multiple_of(block * rows, rows), rows)
    own_columns = pl.multiple_of(pair * LANES, LANES)
    grad_qkv_ref[own_rows, pl.ds(own_columns, LANES)] = grad_query.astype(jnp.bfloat16)

    @pl.when(block == pl.num_programs(1) - 1)
    def _():
        grad_qkv_ref[:, pl.ds(columns + own_columns, LANES)] = key_acc[...].T.astype(jnp.bfloat16)
        grad_qkv_ref[:, pl.ds(2 * columns + own_columns, LANES)] = value_acc[...].T.astype(
            jnp.bfloat16
        )
        down = lax.broadcasted_iota(jnp.int32, (LANES, LANES), 0)
        across = lax.broadcasted_iota(jnp.int32, (LANES, LANES), 1)
        flip = (down + across == LANES - 1).astype(jnp.float32)
        for which in range(2):
            turned = lax.dot_general(
                flip,
                skew[which],
                NN,
                precision=lax.Precision.HIGHEST,
                preferred_element_type=jnp.float32,
            )
            rel_ref[0, which : which + 1, :] = jnp.sum(
                pltpu.roll(turned, 0, 1, stride=1, stride_axis=0), axis=0, keepdims=True
            )


def attend_backward(soft_low, qkv, grad_heads, attended, first, last, so_far=()):
    seq_len, columns = attended.shape
    pairs = columns // LANES
    width = 2 * seq_len
    rows = min(BLOCK_ROWS, seq_len)
    row_block = pl.BlockSpec((rows, LANES), lambda pair, block: (block, first + pair))
    whole = pl.BlockSpec((seq_len, 3 * columns), lambda pair, block: (0, 0))
    grad_qkv, rel_grad = pl.pallas_call(
        functools.partial(backward_kernel, first),
        grid=(last - first, seq_len // rows),
        in_specs=[
            pl.BlockSpec((2, rows, seq_len), lambda pair, block: (first + pair, block, 0)),
            row_block,
            row_block,
            row_block,
            pl.BlockSpec((seq_len, LANES), lambda pair, block: (0, pairs + first + pair)),
            pl.BlockSpec((seq_len, LANES), lambda pair, block: (0, 2 * pairs + first + pair)),
        ]
        + [whole] * len(so_far),
        out_specs=[whole, pl.BlockSpec((1, 2, width), lambda pair, block: (pair, 0, 0))],
        scratch_shapes=[
            pltpu.VMEM((2, LANES, width), jnp.float32),
            pltpu.VMEM((LANES, seq_len), jnp.float32),
            pltpu.VMEM((LANES, seq_len), jnp.float32),
        ],
        out_shape=[
            jax.ShapeDtypeStruct((seq_len, 3 * columns), jnp.bfloat16),
            jax.ShapeDtypeStruct((last - first, 2, width), jnp.float32),
        ],
        compiler_params=pltpu.CompilerParams(vmem_limit_bytes=48 << 20),
        cost_estimate=pl.CostEstimate(
            flops=40 * seq_len * seq_len * columns * (last - first) // pairs,
            bytes_accessed=4 * (last - first) * seq_len * seq_len,
            transcendentals=0,
        ),
        name="attend_backward",
    )(soft_low, qkv, grad_heads, attended, qkv, qkv, *so_far)
    return grad_qkv, rel_grad.reshape(2 * (last - first), width)


def around(block):
    count = lax.axis_size("mp")
    return lax.ppermute(block, "mp", [(i, (i + 1) % count) for i in range(count)])


def together(*values):
    return lax.optimization_barrier(values)


def ring_gather(own):
    blocks = [own]
    for _ in range(lax.axis_size("mp") - 1):
        blocks.append(around(blocks[-1]))
    return blocks


def add_low(received, term):
    return (received.astype(jnp.float32) + term).astype(jnp.bfloat16)


def ring_scatter(part_of):
    count = lax.axis_size("mp")
    running = part_of(1).astype(jnp.bfloat16)
    for step in range(2, count):
        received, term = together(around(running), part_of(step))
        running = add_low(received, term)
    received, term = together(around(running), part_of(0))
    return received.astype(jnp.float32) + term


def total_over(value, axis):
    count = lax.axis_size(axis)
    apart = 1
    while apart < count:
        value = value + lax.ppermute(value, axis, [(i, i ^ apart) for i in range(count)])
        apart *= 2
    return value


def update(moment, grad_owned, factor):
    return 0.5 * moment + (0.5 * factor) * grad_owned


def shards(
    layer_input,
    output_grad,
    seq_lengths,
    deal_order,
    bucket_index,
    query_weight,
    key_weight,
    value_weight,
    out_weight,
    gate_weight,
    up_weight,
    down_weight,
    attn_gain,
    ffn_gain,
    bias_table,
    query_moment,
    key_moment,
    value_moment,
    out_moment,
    gate_moment,
    up_moment,
    down_moment,
    attn_gain_moment,
    ffn_gain_moment,
    table_moment,
):
    low = jnp.bfloat16
    f32 = jnp.float32
    group_index = lax.axis_index("dp")
    member = lax.axis_index("mp")
    group_count = lax.axis_size("dp")
    tensor_count = lax.axis_size("mp")

    def back(step):
        return lax.rem(member - step + tensor_count, tensor_count)

    picked = jnp.take(layer_input, deal_order, axis=0)
    dealt = lax.all_to_all(picked, "dp", split_axis=0, concat_axis=0, tiled=True)
    x_own = dealt.reshape(-1, dealt.shape[2])
    length = seq_lengths[deal_order[group_index]]
    seq_len, quarter = x_own.shape
    features = quarter * tensor_count
    part_rows = seq_len // tensor_count

    small = jnp.concatenate([attn_gain, ffn_gain, bias_table.reshape(-1)]).astype(low)
    x_own, grad_next, small = together(
        x_own, around(output_grad[0]), lax.all_gather(small, "dp", axis=0)
    )
    grad_parts = [output_grad[0], grad_next]
    row_valid = lax.broadcasted_iota(jnp.int32, (seq_len, 1), 0) < length

    def valid_rows(part):
        return jnp.where(row_valid, part, jnp.zeros((), low))

    def row_part(array, step):
        return lax.dynamic_slice_in_dim(array, back(step) * part_rows, part_rows, 0)

    def column_part(array, step):
        return lax.dynamic_slice_in_dim(array, back(step) * quarter, quarter, 1)

    def set_rows(whole, part, step):
        return lax.dynamic_update_slice_in_dim(whole, part, back(step) * part_rows, 0)

    def set_columns(whole, part, step):
        return lax.dynamic_update_slice_in_dim(whole, part, back(step) * quarter, 1)

    def whole_columns(parts, start):
        whole = jnp.broadcast_to(start[:1, :1], (seq_len, features))
        for step, part in enumerate(parts):
            whole = set_columns(whole, part, step)
        return whole

    gain_size = attn_gain.shape[0]
    first_gain = small[:, :gain_size].reshape(-1).astype(f32)
    second_gain = small[:, gain_size : 2 * gain_size].reshape(-1).astype(f32)
    full_table = small[:, 2 * gain_size :].reshape(NB, bias_table.shape[1])
    qkv_weight = jnp.concatenate([query_weight, key_weight, value_weight], axis=1).astype(low)
    qkv_weight, x_own = together(qkv_weight, x_own)
    qkv_weight = lax.all_gather(qkv_weight, "dp", axis=0, tiled=True)
    gate_up = jnp.concatenate([gate_weight, up_weight], axis=1).astype(low)
    out_down = jnp.concatenate([out_weight, down_weight], axis=0).astype(low)
    heads_columns = out_weight.shape[0]
    units = down_weight.shape[0]
    x_parts = ring_gather(x_own)
    out_down, x_parts[1] = together(out_down, x_parts[1])
    out_down = lax.all_gather(out_down, "dp", axis=1, tiled=True)
    gate_up, x_parts[2] = together(gate_up, x_parts[2])
    gate_up = lax.all_gather(gate_up, "dp", axis=0, tiled=True)

    def down_columns(step):
        return lax.dynamic_slice(
            out_down, (heads_columns, back(step) * quarter), (units, quarter)
        )

    grad_parts[1], x_parts[-1] = together(grad_parts[1], x_parts[-1])
    x_rows = whole_columns(x_parts, x_own)
    grad_parts.append(around(grad_parts[1]))

    offsets = jnp.concatenate([bucket_index, jnp.full((1,), NB, jnp.int32)])
    bucket_hot = offsets[:, None] == lax.broadcasted_iota(jnp.int32, (2 * seq_len, NB), 1)
    rel_rows = dot(full_table, bucket_hot.astype(low), (((0,), (1,)), ((), ())))

    x_float = x_rows.astype(f32)
    inv_first = lax.rsqrt(jnp.mean(x_float * x_float, axis=-1, keepdims=True) + EPS)
    h_first = (x_float * inv_first * first_gain).astype(low)
    qkv = dot(h_first, qkv_weight).astype(low)
    pairs = heads_columns // LANES
    so_far = attend_forward(qkv, rel_rows, length, 0, 1)
    rel_rows, grad_parts[2], *so_far = together(rel_rows, grad_parts[2], *so_far)
    grad_parts.append(around(grad_parts[2]))
    attended, soft_low = attend_forward(qkv, rel_rows, length, 1, pairs, so_far)
    attended, grad_parts[3] = together(attended, grad_parts[3])

    def attended_part(step):
        return dot(row_part(attended, step), out_down[:heads_columns])

    running = around(attended_part(1).astype(low))
    grad_y = whole_columns([valid_rows(part) for part in grad_parts[:-1]], attended)
    received, term, grad_y = together(running, attended_part(2), grad_y)
    running = around(add_low(received, term))
    grad_y = set_columns(grad_y, valid_rows(grad_parts[-1]), tensor_count - 1)
    received, term, last_term, grad_y = together(
        running, attended_part(3), attended_part(0), grad_y
    )
    running = around(add_low(received, term))
    attn_branch = running.astype(f32) + last_term

    after_attn = row_part(x_rows, 0).astype(f32) + attn_branch
    inv_second = lax.rsqrt(jnp.mean(after_attn * after_attn, axis=-1, keepdims=True) + EPS)
    h_second = (after_attn * inv_second * second_gain).astype(low)

    h_parts = [h_second]
    hidden = jnp.broadcast_to(h_second[:1, :1], (seq_len, units))
    gate_up_grads = []
    terms = {}

    def square_sum(piece):
        return jnp.sum(jnp.square(piece.astype(f32)))

    def normed_part(step):
        return dot(gate_up_grads[step], gate_up, NT)

    for step in range(tensor_count):
        if step > 0:
            last = step - 1
            term = normed_part(last)
            h_parts[step], gate_up_grads[last], hidden, terms[last] = together(
                h_parts[step],
                gate_up_grads[last],
                hidden,
                term.astype(low) if last == 1 else term,
            )
        if step < tensor_count - 1:
            h_parts.append(around(h_parts[step]))
        else:
            terms[1], h_parts[step] = together(terms[1], h_parts[step])
            running = around(terms[1])
        both = dot(h_parts[step], gate_up)
        mixed, mix_back = jax.vjp(
            lambda gate_in, up_in: jax.nn.gelu(gate_in, approximate=True) * up_in,
            both[:, :units],
            both[:, units:],
        )
        hidden = set_rows(hidden, mixed.astype(low), step)
        grad_hidden = dot(row_part(grad_y, step), out_down[heads_columns:], NT)
        gate_up_grads.append(jnp.concatenate(mix_back(grad_hidden), axis=1).astype(low))

    received, terms[2], terms[3], gate_up_grads[3], hidden = together(
        running, terms[2], normed_part(3), gate_up_grads[3], hidden
    )
    running = around(add_low(received, terms[2]))
    h_rotated = jnp.concatenate(h_parts, axis=0)
    grads_rotated = jnp.concatenate(gate_up_grads, axis=0)
    grad_gate_up = dot(h_rotated, grads_rotated, TN).astype(low)
    received, grad_gate_up = together(running, grad_gate_up)
    owned_gate_up = lax.psum_scatter(grad_gate_up, "dp", scatter_dimension=0, tiled=True)
    running = around(add_low(received, terms[3]))
    grad_down = dot(hidden, grad_y, TN).astype(low)
    received, terms[0], grad_down, hidden = together(running, terms[0], grad_down, hidden)
    grad_h_second = received.astype(f32) + terms[0]

    grad_ffn_gain = jnp.sum(grad_h_second * (after_attn * inv_second), axis=0)
    weighted = grad_h_second * second_gain
    row_inner = jnp.mean(weighted * after_attn, axis=-1, keepdims=True)
    grad_after = (
        row_part(grad_y, 0).astype(f32)
        + inv_second * weighted
        - after_attn * (inv_second * inv_second * inv_second) * row_inner
    ).astype(low)

    def output_part(step):
        part = dot(hidden, down_columns(step))
        mine = row_part(part, 0) + column_part(after_attn, step)
        return set_rows(part, mine, 0)

    after_parts = [grad_after]
    after_parts.append(around(after_parts[0]))
    output_terms = [output_part(step) for step in range(tensor_count)]
    after_parts[1], output_terms[1], output_terms[2] = together(
        after_parts[1], output_terms[1], output_terms[2]
    )
    after_parts.append(around(after_parts[1]))
    after_parts[2], output_terms[3], output_terms[0] = together(
        after_parts[2], output_terms[3], output_terms[0]
    )
    after_parts.append(around(after_parts[2]))
    grad_after = grad_y
    grad_heads = jnp.zeros((seq_len, heads_columns), low)
    for step in range(tensor_count):
        if step == tensor_count - 1:
            grad_after, grad_heads, after_parts[step] = together(
                grad_after, grad_heads, after_parts[step]
            )
        part = after_parts[step]
        grad_after = set_rows(grad_after, part, step)
        grad_heads = set_rows(grad_heads, dot(part, out_down[:heads_columns], NT).astype(low), step)
    output_first = output_terms[1].astype(low)
    output_first, grad_after, grad_heads = together(output_first, grad_after, grad_heads)
    output_sum = around(output_first)

    grad_out = dot(attended, grad_after, TN).astype(low)
    grad_heads, grad_out = together(grad_heads, grad_out)
    grad_out_down = jnp.concatenate([grad_out, grad_down], axis=0)
    owned_out_down = lax.psum_scatter(grad_out_down, "dp", scatter_dimension=1, tiled=True)
    half = pairs // 2
    first_grads, first_rel = attend_backward(soft_low, qkv, grad_heads, attended, 0, half)
    output_sum, first_grads, owned_gate_up = together(output_sum, first_grads, owned_gate_up)
    output_sum = around(add_low(output_sum, output_terms[2]))
    grad_qkv, second_rel = attend_backward(
        soft_low, qkv, grad_heads, attended, half, pairs, (first_grads,)
    )
    rel_grad = jnp.concatenate([first_rel, second_rel], axis=0)
    grad_qkv, output_sum = together(grad_qkv, output_sum)
    output_sent = add_low(output_sum, output_terms[3])

    def first_part(step):
        weight = lax.dynamic_slice_in_dim(qkv_weight, back(step) * quarter, quarter, 0)
        return dot(grad_qkv, weight, NT)

    running, grad_qkv = together(first_part(1).astype(low), grad_qkv)
    running = around(running)
    grad_qkv_weight = dot(h_first, grad_qkv, TN).astype(low)
    received, term, grad_qkv_weight = together(running, first_part(2), grad_qkv_weight)
    owned_qkv = lax.psum_scatter(grad_qkv_weight, "dp", scatter_dimension=0, tiled=True)
    running = around(add_low(received, term))
    inner = jnp.sum(grad_qkv.astype(f32) * qkv.astype(f32), axis=-1)
    inner = total_over(inner.reshape(-1, LANES), "mp").reshape(-1, 1) / features
    received, term, owned_out_down = together(running, first_part(3), owned_out_down)
    running = around(add_low(received, term))
    grad_table = lax.dot_general(
        bucket_hot.astype(f32),
        rel_grad,
        (((0,), (1,)), ((), ())),
        precision=lax.Precision.HIGHEST,
        preferred_element_type=f32,
    )
    early_sq = square_sum(owned_gate_up) + square_sum(owned_out_down)
    received, term, grad_table, early_sq, inner, output_sent = together(
        running, first_part(0), grad_table, early_sq, inner, output_sent
    )
    output_sum = around(output_sent)
    grad_h_first = received.astype(f32) + term
    own_gain = lax.dynamic_slice_in_dim(first_gain, member * quarter, quarter, 0)
    x_own = x_own.astype(f32)
    grad_attn_gain = jnp.sum(grad_h_first * (x_own * inv_first), axis=0)
    grad_input = (
        column_part(grad_after, 0).astype(f32)
        + inv_first * (grad_h_first * own_gain)
        - x_own * (inv_first * inv_first) * inner
    ).astype(low)
    came_back = lax.all_to_all(
        grad_input.reshape(group_count, -1, quarter), "dp", split_axis=0, concat_axis=0, tiled=True
    )
    group_iota = lax.broadcasted_iota(jnp.int32, (group_count, group_count), 0)
    place = jnp.argmax(deal_order[None, :] == group_iota, axis=1)
    input_grad = jnp.take(came_back, place, axis=0)

    local_sq = early_sq + square_sum(owned_qkv)
    heads_dev = bias_table.shape[1]
    first_wide = lax.dynamic_update_slice_in_dim(
        jnp.zeros((features,), f32), grad_attn_gain, member * quarter, 0
    )
    table_wide = lax.dynamic_update_slice_in_dim(
        jnp.zeros((NB, heads_dev * tensor_count), f32), grad_table, member * heads_dev, 1
    )
    sums = jnp.concatenate([first_wide, grad_ffn_gain, table_wide.reshape(-1)])
    small_count = sums.shape[0]
    sums = jnp.concatenate([sums, jnp.broadcast_to(local_sq, (LANES,))])
    sums = total_over(sums.reshape(-1, LANES), "dp")
    sums, output_sum = together(sums, output_sum)
    layer_out = (output_sum.astype(f32) + output_terms[0]).astype(low)[None]
    sums = total_over(sums, "mp").reshape(-1)
    total_sq = sums[small_count] + jnp.sum(sums[:small_count] * sums[:small_count])
    grad_norm = jnp.sqrt(total_sq)
    limit = math.sqrt(4 * D * H * DH + 3 * D * FF + 2 * D + NB * H)
    factor = jnp.minimum(1.0, limit / grad_norm)
    owned_first = lax.dynamic_slice_in_dim(sums, group_index * gain_size, gain_size, 0)
    owned_second = lax.dynamic_slice_in_dim(
        sums, features + group_index * gain_size, gain_size, 0
    )
    table_rows = bias_table.shape[0]
    owned_table = lax.dynamic_slice(
        sums[2 * features : small_count].reshape(NB, heads_dev * tensor_count),
        (group_index * table_rows, member * heads_dev),
        (table_rows, heads_dev),
    )
    return (
        layer_out,
        input_grad,
        grad_norm,
        update(query_moment, owned_qkv[:, :heads_columns], factor),
        update(key_moment, owned_qkv[:, heads_columns : 2 * heads_columns], factor),
        update(value_moment, owned_qkv[:, 2 * heads_columns :], factor),
        update(out_moment, owned_out_down[:heads_columns], factor),
        update(gate_moment, owned_gate_up[:, :units], factor),
        update(up_moment, owned_gate_up[:, units:], factor),
        update(down_moment, owned_out_down[heads_columns:], factor),
        update(attn_gain_moment, owned_first, factor),
        update(ffn_gain_moment, owned_second, factor),
        update(table_moment, owned_table, factor),
    )


def solution(mesh):
    in_specs = (
        P(None, "dp", "mp"),
        P("dp", None, "mp"),
        P(),
        P(),
        P(),
        P("dp", "mp"),
        P("dp", "mp"),
        P("dp", "mp"),
        P("mp", "dp"),
        P("dp", "mp"),
        P("dp", "mp"),
        P("mp", "dp"),
        P("dp"),
        P("dp"),
        P("dp", "mp"),
        P("dp", "mp"),
        P("dp", "mp"),
        P("dp", "mp"),
        P("mp", "dp"),
        P("dp", "mp"),
        P("dp", "mp"),
        P("mp", "dp"),
        P("dp"),
        P("dp"),
        P("dp", "mp"),
    )
    out_specs = (
        P("dp", None, "mp"),
        P(None, "dp", "mp"),
        P(),
        P("dp", "mp"),
        P("dp", "mp"),
        P("dp", "mp"),
        P("mp", "dp"),
        P("dp", "mp"),
        P("dp", "mp"),
        P("mp", "dp"),
        P("dp"),
        P("dp"),
        P("dp", "mp"),
    )
    return jax.shard_map(shards, mesh=mesh, in_specs=in_specs, out_specs=out_specs, check_vma=False)
```

```python
import functools
import math

import jax
import jax.numpy as jnp
from jax import lax
from jax.experimental import pallas as pl
from jax.experimental.pallas import tpu as pltpu
from jax.sharding import PartitionSpec as P

D = 2048
H = 32
DH = 64
FF = 5120
NB = 32


EPS = 1e-06
NEG = -1e30
LANES = 128
BLOCK_ROWS = 256

NN = (((1,), (0,)), ((), ()))
NT = (((1,), (1,)), ((), ()))
TN = (((0,), (0,)), ((), ()))


def dot(left, right, dims=NN):
    return lax.dot_general(left, right, dims, preferred_element_type=jnp.float32)


def pick_head(pair_rows, which):
    lane = lax.broadcasted_iota(jnp.int32, (1, LANES), 1)
    return jnp.where(lane // DH == which, pair_rows, jnp.zeros_like(pair_rows))


def forward_kernel(length, rel_ref, query_ref, key_ref, value_ref, out_ref, soft_ref, skew):
    block = pl.program_id(1)
    rows = query_ref.shape[0]
    key_count = key_ref.shape[0]
    width = rel_ref.shape[2]

    @pl.when(block == 0)
    def _():
        for which in range(2):
            spread = jnp.broadcast_to(rel_ref[0, which : which + 1, :], (LANES, width))
            skew[which] = pltpu.roll(spread, width - (LANES - 1), 1, stride=1, stride_axis=0)

    key_at = lax.broadcasted_iota(jnp.int32, (1, key_count), 1)
    key_mask = jnp.where(key_at < length[0], 0.0, NEG)
    keys = key_ref[...]
    values = value_ref[...]
    mixed = jnp.zeros((rows, LANES), jnp.float32)
    for which in range(2):
        products = dot(pick_head(query_ref[...], which), keys, NT)
        parts = []
        for part in range(rows // LANES):
            offset = pl.multiple_of(key_count - LANES * (part + 1) - rows * block, LANES)
            parts.append(
                products[LANES * part : LANES * (part + 1)] + skew[which, :, pl.ds(offset, key_count)]
            )
        scores = jnp.concatenate(parts, 0) + key_mask
        exp_terms = jnp.exp(scores - jnp.max(scores, axis=1, keepdims=True))
        total = jnp.sum(exp_terms, axis=1, keepdims=True)
        soft_low = (exp_terms * (1.0 / total)).astype(jnp.bfloat16)
        soft_ref[which] = soft_low
        mixed = mixed + dot(soft_low, pick_head(values, which))
    out_ref[...] = mixed.astype(jnp.bfloat16)


def attend_forward(qkv, rel_rows, length, first, last, so_far=None):
    seq_len = qkv.shape[0]
    columns = qkv.shape[1] // 3
    pairs = columns // LANES
    width = rel_rows.shape[1]
    rows = min(BLOCK_ROWS, seq_len)
    kernel = forward_kernel
    operands = [length.reshape(1), rel_rows.reshape(pairs, 2, width), qkv, qkv, qkv]
    in_specs = [
        pl.BlockSpec((1, 2, width), lambda pair, block, n: (first + pair, 0, 0)),
        pl.BlockSpec((rows, LANES), lambda pair, block, n: (block, first + pair)),
        pl.BlockSpec((seq_len, LANES), lambda pair, block, n: (0, pairs + first + pair)),
        pl.BlockSpec((seq_len, LANES), lambda pair, block, n: (0, 2 * pairs + first + pair)),
    ]
    aliases = {}
    if so_far is not None:
        kernel = second_forward_kernel
        operands += so_far
        in_specs += [pl.BlockSpec(memory_space=pl.ANY)] * 2
        aliases = {5: 0, 6: 1}
    return pl.pallas_call(
        kernel,
        grid_spec=pltpu.PrefetchScalarGridSpec(
            num_scalar_prefetch=1,
            grid=(last - first, seq_len // rows),
            in_specs=in_specs,
            out_specs=[
                pl.BlockSpec((rows, LANES), lambda pair, block, n: (block, first + pair)),
                pl.BlockSpec((2, rows, seq_len), lambda pair, block, n: (first + pair, block, 0)),
            ],
            scratch_shapes=[pltpu.VMEM((2, LANES, width), jnp.float32)],
        ),
        out_shape=[
            jax.ShapeDtypeStruct((seq_len, columns), jnp.bfloat16),
            jax.ShapeDtypeStruct((2 * pairs, seq_len, seq_len), jnp.bfloat16),
        ],
        input_output_aliases=aliases,
        compiler_params=pltpu.CompilerParams(vmem_limit_bytes=40 << 20),
        cost_estimate=pl.CostEstimate(
            flops=16 * seq_len * seq_len * columns * (last - first) // pairs,
            bytes_accessed=4 * (last - first) * seq_len * seq_len,
            transcendentals=2 * (last - first) * seq_len * seq_len,
        ),
        name="attend_forward",
    )(*operands)


def second_forward_kernel(
    length, rel_ref, query_ref, key_ref, value_ref, _, __, out_ref, soft_ref, skew
):
    forward_kernel(length, rel_ref, query_ref, key_ref, value_ref, out_ref, soft_ref, skew)


def backward_kernel(
    first,
    soft_ref,
    query_ref,
    grad_ref,
    out_ref,
    key_ref,
    value_ref,
    *rest,
):
    grad_qkv_ref, rel_ref, skew, key_acc, value_acc = rest[-5:]
    pair = first + pl.program_id(0)
    block = pl.program_id(1)
    rows = query_ref.shape[0]
    key_count = key_ref.shape[0]
    columns = grad_qkv_ref.shape[1] // 3

    @pl.when(block == 0)
    def _():
        skew[...] = jnp.zeros_like(skew)
        key_acc[...] = jnp.zeros_like(key_acc)
        value_acc[...] = jnp.zeros_like(value_acc)

    if len(rest) > 5:

        @pl.when((block == 0) & (pair == first))
        def _():
            grad_qkv_ref[...] = rest[0][...]

    keys = key_ref[...]
    values = value_ref[...]
    queries = query_ref[...]
    grads = grad_ref[...]
    inner = grads.astype(jnp.float32) * out_ref[...].astype(jnp.float32)
    grad_query = jnp.zeros((rows, LANES), jnp.float32)
    for which in range(2):
        grad_head = pick_head(grads, which)
        row_inner = jnp.sum(pick_head(inner, which), axis=1, keepdims=True)
        grad_soft = dot(grad_head, values, NT)
        soft_low = soft_ref[which]
        grad_scores = soft_low.astype(jnp.float32) * (grad_soft - row_inner)
        for part in range(rows // LANES):
            offset = pl.multiple_of(key_count - LANES * (part + 1) - rows * block, LANES)
            skew[which, :, pl.ds(offset, key_count)] += grad_scores[
                LANES * part : LANES * (part + 1)
            ]
        grad_low = grad_scores.astype(jnp.bfloat16)
        grad_query = grad_query + dot(grad_low, pick_head(keys, which))
        key_acc[...] += dot(pick_head(queries, which), grad_low, TN)
        value_acc[...] += dot(grad_head, soft_low, TN)
    own_rows = pl.ds(pl.multiple_of(block * rows, rows), rows)
    own_columns = pl.multiple_of(pair * LANES, LANES)
    grad_qkv_ref[own_rows, pl.ds(own_columns, LANES)] = grad_query.astype(jnp.bfloat16)

    @pl.when(block == pl.num_programs(1) - 1)
    def _():
        grad_qkv_ref[:, pl.ds(columns + own_columns, LANES)] = key_acc[...].T.astype(jnp.bfloat16)
        grad_qkv_ref[:, pl.ds(2 * columns + own_columns, LANES)] = value_acc[...].T.astype(
            jnp.bfloat16
        )
        down = lax.broadcasted_iota(jnp.int32, (LANES, LANES), 0)
        across = lax.broadcasted_iota(jnp.int32, (LANES, LANES), 1)
        flip = (down + across == LANES - 1).astype(jnp.float32)
        for which in range(2):
            turned = lax.dot_general(
                flip,
                skew[which],
                NN,
                precision=lax.Precision.HIGHEST,
                preferred_element_type=jnp.float32,
            )
            rel_ref[0, which : which + 1, :] = jnp.sum(
                pltpu.roll(turned, 0, 1, stride=1, stride_axis=0), axis=0, keepdims=True
            )


def attend_backward(soft_low, qkv, grad_heads, attended, first, last, so_far=()):
    seq_len, columns = attended.shape
    pairs = columns // LANES
    width = 2 * seq_len
    rows = min(BLOCK_ROWS, seq_len)
    row_block = pl.BlockSpec((rows, LANES), lambda pair, block: (block, first + pair))
    whole = pl.BlockSpec((seq_len, 3 * columns), lambda pair, block: (0, 0))
    grad_qkv, rel_grad = pl.pallas_call(
        functools.partial(backward_kernel, first),
        grid=(last - first, seq_len // rows),
        in_specs=[
            pl.BlockSpec((2, rows, seq_len), lambda pair, block: (first + pair, block, 0)),
            row_block,
            row_block,
            row_block,
            pl.BlockSpec((seq_len, LANES), lambda pair, block: (0, pairs + first + pair)),
            pl.BlockSpec((seq_len, LANES), lambda pair, block: (0, 2 * pairs + first + pair)),
        ]
        + [whole] * len(so_far),
        out_specs=[whole, pl.BlockSpec((1, 2, width), lambda pair, block: (pair, 0, 0))],
        scratch_shapes=[
            pltpu.VMEM((2, LANES, width), jnp.float32),
            pltpu.VMEM((LANES, seq_len), jnp.float32),
            pltpu.VMEM((LANES, seq_len), jnp.float32),
        ],
        out_shape=[
            jax.ShapeDtypeStruct((seq_len, 3 * columns), jnp.bfloat16),
            jax.ShapeDtypeStruct((last - first, 2, width), jnp.float32),
        ],
        compiler_params=pltpu.CompilerParams(vmem_limit_bytes=48 << 20),
        cost_estimate=pl.CostEstimate(
            flops=40 * seq_len * seq_len * columns * (last - first) // pairs,
            bytes_accessed=4 * (last - first) * seq_len * seq_len,
            transcendentals=0,
        ),
        name="attend_backward",
    )(soft_low, qkv, grad_heads, attended, qkv, qkv, *so_far)
    return grad_qkv, rel_grad.reshape(2 * (last - first), width)


def around(block):
    count = lax.axis_size("mp")
    return lax.ppermute(block, "mp", [(i, (i + 1) % count) for i in range(count)])


def together(*values):
    return lax.optimization_barrier(values)


def ring_gather(own):
    blocks = [own]
    for _ in range(lax.axis_size("mp") - 1):
        blocks.append(around(blocks[-1]))
    return blocks


def add_low(received, term):
    return (received.astype(jnp.float32) + term).astype(jnp.bfloat16)


def ring_scatter(part_of):
    count = lax.axis_size("mp")
    running = part_of(1).astype(jnp.bfloat16)
    for step in range(2, count):
        received, term = together(around(running), part_of(step))
        running = add_low(received, term)
    received, term = together(around(running), part_of(0))
    return received.astype(jnp.float32) + term


def total_over(value, axis):
    count = lax.axis_size(axis)
    apart = 1
    while apart < count:
        value = value + lax.ppermute(value, axis, [(i, i ^ apart) for i in range(count)])
        apart *= 2
    return value


def update(moment, grad_owned, factor):
    return 0.5 * moment + (0.5 * factor) * grad_owned


def shards(
    layer_input,
    output_grad,
    seq_lengths,
    deal_order,
    bucket_index,
    query_weight,
    key_weight,
    value_weight,
    out_weight,
    gate_weight,
    up_weight,
    down_weight,
    attn_gain,
    ffn_gain,
    bias_table,
    query_moment,
    key_moment,
    value_moment,
    out_moment,
    gate_moment,
    up_moment,
    down_moment,
    attn_gain_moment,
    ffn_gain_moment,
    table_moment,
):
    low = jnp.bfloat16
    f32 = jnp.float32
    group_index = lax.axis_index("dp")
    member = lax.axis_index("mp")
    group_count = lax.axis_size("dp")
    tensor_count = lax.axis_size("mp")

    def back(step):
        return lax.rem(member - step + tensor_count, tensor_count)

    picked = jnp.take(layer_input, deal_order, axis=0)
    dealt = lax.all_to_all(picked, "dp", split_axis=0, concat_axis=0, tiled=True)
    x_own = dealt.reshape(-1, dealt.shape[2])
    length = seq_lengths[deal_order[group_index]]
    seq_len, quarter = x_own.shape
    features = quarter * tensor_count
    part_rows = seq_len // tensor_count

    small = jnp.concatenate([attn_gain, ffn_gain, bias_table.reshape(-1)]).astype(low)
    x_own, grad_next, small = together(
        x_own, around(output_grad[0]), lax.all_gather(small, "dp", axis=0)
    )
    grad_parts = [output_grad[0], grad_next]
    row_valid = lax.broadcasted_iota(jnp.int32, (seq_len, 1), 0) < length

    def valid_rows(part):
        return jnp.where(row_valid, part, jnp.zeros((), low))

    def row_part(array, step):
        return lax.dynamic_slice_in_dim(array, back(step) * part_rows, part_rows, 0)

    def column_part(array, step):
        return lax.dynamic_slice_in_dim(array, back(step) * quarter, quarter, 1)

    def set_rows(whole, part, step):
        return lax.dynamic_update_slice_in_dim(whole, part, back(step) * part_rows, 0)

    def set_columns(whole, part, step):
        return lax.dynamic_update_slice_in_dim(whole, part, back(step) * quarter, 1)

    def whole_columns(parts, start):
        whole = jnp.broadcast_to(start[:1, :1], (seq_len, features))
        for step, part in enumerate(parts):
            whole = set_columns(whole, part, step)
        return whole

    gain_size = attn_gain.shape[0]
    first_gain = small[:, :gain_size].reshape(-1).astype(f32)
    second_gain = small[:, gain_size : 2 * gain_size].reshape(-1).astype(f32)
    full_table = small[:, 2 * gain_size :].reshape(NB, bias_table.shape[1])
    qkv_weight = jnp.concatenate([query_weight, key_weight, value_weight], axis=1).astype(low)
    qkv_weight, x_own = together(qkv_weight, x_own)
    qkv_weight = lax.all_gather(qkv_weight, "dp", axis=0, tiled=True)
    gate_up = jnp.concatenate([gate_weight, up_weight], axis=1).astype(low)
    out_down = jnp.concatenate([out_weight, down_weight], axis=0).astype(low)
    heads_columns = out_weight.shape[0]
    units = down_weight.shape[0]
    x_parts = ring_gather(x_own)
    out_down, x_parts[1] = together(out_down, x_parts[1])
    out_down = lax.all_gather(out_down, "dp", axis=1, tiled=True)
    gate_up, x_parts[2] = together(gate_up, x_parts[2])
    gate_up = lax.all_gather(gate_up, "dp", axis=0, tiled=True)

    def down_columns(step):
        return lax.dynamic_slice(
            out_down, (heads_columns, back(step) * quarter), (units, quarter)
        )

    grad_parts[1], x_parts[-1] = together(grad_parts[1], x_parts[-1])
    x_rows = whole_columns(x_parts, x_own)
    grad_parts.append(around(grad_parts[1]))

    offsets = jnp.concatenate([bucket_index, jnp.full((1,), NB, jnp.int32)])
    bucket_hot = offsets[:, None] == lax.broadcasted_iota(jnp.int32, (2 * seq_len, NB), 1)
    rel_rows = dot(full_table, bucket_hot.astype(low), (((0,), (1,)), ((), ())))

    x_float = x_rows.astype(f32)
    inv_first = lax.rsqrt(jnp.mean(x_float * x_float, axis=-1, keepdims=True) + EPS)
    h_first = (x_float * inv_first * first_gain).astype(low)
    qkv = dot(h_first, qkv_weight).astype(low)
    pairs = heads_columns // LANES
    so_far = attend_forward(qkv, rel_rows, length, 0, 1)
    rel_rows, grad_parts[2], *so_far = together(rel_rows, grad_parts[2], *so_far)
    grad_parts.append(around(grad_parts[2]))
    attended, soft_low = attend_forward(qkv, rel_rows, length, 1, pairs, so_far)
    attended, grad_parts[3] = together(attended, grad_parts[3])

    def attended_part(step):
        return dot(row_part(attended, step), out_down[:heads_columns])

    running = around(attended_part(1).astype(low))
    grad_y = whole_columns([valid_rows(part) for part in grad_parts[:-1]], attended)
    received, term, grad_y = together(running, attended_part(2), grad_y)
    running = around(add_low(received, term))
    grad_y = set_columns(grad_y, valid_rows(grad_parts[-1]), tensor_count - 1)
    received, term, last_term, grad_y = together(
        running, attended_part(3), attended_part(0), grad_y
    )
    running = around(add_low(received, term))
    attn_branch = running.astype(f32) + last_term

    after_attn = row_part(x_rows, 0).astype(f32) + attn_branch
    inv_second = lax.rsqrt(jnp.mean(after_attn * after_attn, axis=-1, keepdims=True) + EPS)
    h_second = (after_attn * inv_second * second_gain).astype(low)

    h_parts = [h_second]
    hidden = jnp.broadcast_to(h_second[:1, :1], (seq_len, units))
    gate_up_grads = []
    terms = {}

    def square_sum(piece):
        return jnp.sum(jnp.square(piece.astype(f32)))

    def normed_part(step):
        return dot(gate_up_grads[step], gate_up, NT)

    for step in range(tensor_count):
        if step > 0:
            last = step - 1
            term = normed_part(last)
            h_parts[step], gate_up_grads[last], hidden, terms[last] = together(
                h_parts[step],
                gate_up_grads[last],
                hidden,
                term.astype(low) if last == 1 else term,
            )
        if step < tensor_count - 1:
            h_parts.append(around(h_parts[step]))
        else:
            terms[1], h_parts[step] = together(terms[1], h_parts[step])
            running = around(terms[1])
        both = dot(h_parts[step], gate_up)
        mixed, mix_back = jax.vjp(
            lambda gate_in, up_in: jax.nn.gelu(gate_in, approximate=True) * up_in,
            both[:, :units],
            both[:, units:],
        )
        hidden = set_rows(hidden, mixed.astype(low), step)
        grad_hidden = dot(row_part(grad_y, step), out_down[heads_columns:], NT)
        gate_up_grads.append(jnp.concatenate(mix_back(grad_hidden), axis=1).astype(low))

    received, terms[2], terms[3], gate_up_grads[3], hidden = together(
        running, terms[2], normed_part(3), gate_up_grads[3], hidden
    )
    running = around(add_low(received, terms[2]))
    h_rotated = jnp.concatenate(h_parts, axis=0)
    grads_rotated = jnp.concatenate(gate_up_grads, axis=0)
    grad_gate_up = dot(h_rotated, grads_rotated, TN).astype(low)
    received, grad_gate_up = together(running, grad_gate_up)
    owned_gate_up = lax.psum_scatter(grad_gate_up, "dp", scatter_dimension=0, tiled=True)
    running = around(add_low(received, terms[3]))
    grad_down = dot(hidden, grad_y, TN).astype(low)
    received, terms[0], grad_down, hidden = together(running, terms[0], grad_down, hidden)
    grad_h_second = received.astype(f32) + terms[0]

    grad_ffn_gain = jnp.sum(grad_h_second * (after_attn * inv_second), axis=0)
    weighted = grad_h_second * second_gain
    row_inner = jnp.mean(weighted * after_attn, axis=-1, keepdims=True)
    grad_after = (
        row_part(grad_y, 0).astype(f32)
        + inv_second * weighted
        - after_attn * (inv_second * inv_second * inv_second) * row_inner
    ).astype(low)

    def output_part(step):
        part = dot(hidden, down_columns(step))
        mine = row_part(part, 0) + column_part(after_attn, step)
        return set_rows(part, mine, 0)

    after_parts = [grad_after]
    after_parts.append(around(after_parts[0]))
    output_terms = [output_part(step) for step in range(tensor_count)]
    after_parts[1], output_terms[1], output_terms[2] = together(
        after_parts[1], output_terms[1], output_terms[2]
    )
    after_parts.append(around(after_parts[1]))
    after_parts[2], output_terms[3], output_terms[0] = together(
        after_parts[2], output_terms[3], output_terms[0]
    )
    after_parts.append(around(after_parts[2]))
    grad_after = grad_y
    grad_heads = jnp.zeros((seq_len, heads_columns), low)
    for step in range(tensor_count):
        if step == tensor_count - 1:
            grad_after, grad_heads, after_parts[step] = together(
                grad_after, grad_heads, after_parts[step]
            )
        part = after_parts[step]
        grad_after = set_rows(grad_after, part, step)
        grad_heads = set_rows(grad_heads, dot(part, out_down[:heads_columns], NT).astype(low), step)
    output_first = output_terms[1].astype(low)
    output_first, grad_after, grad_heads = together(output_first, grad_after, grad_heads)
    output_sum = around(output_first)

    grad_out = dot(attended, grad_after, TN).astype(low)
    grad_heads, grad_out = together(grad_heads, grad_out)
    grad_out_down = jnp.concatenate([grad_out, grad_down], axis=0)
    owned_out_down = lax.psum_scatter(grad_out_down, "dp", scatter_dimension=1, tiled=True)
    half = pairs // 2
    first_grads, first_rel = attend_backward(soft_low, qkv, grad_heads, attended, 0, half)
    output_sum, first_grads, owned_gate_up = together(output_sum, first_grads, owned_gate_up)
    output_sum = around(add_low(output_sum, output_terms[2]))
    grad_qkv, second_rel = attend_backward(
        soft_low, qkv, grad_heads, attended, half, pairs, (first_grads,)
    )
    rel_grad = jnp.concatenate([first_rel, second_rel], axis=0)
    grad_qkv, output_sum = together(grad_qkv, output_sum)
    output_sent = add_low(output_sum, output_terms[3])

    def first_part(step):
        weight = lax.dynamic_slice_in_dim(qkv_weight, back(step) * quarter, quarter, 0)
        return dot(grad_qkv, weight, NT)

    running, grad_qkv = together(first_part(1).astype(low), grad_qkv)
    running = around(running)
    grad_qkv_weight = dot(h_first, grad_qkv, TN).astype(low)
    received, term, grad_qkv_weight = together(running, first_part(2), grad_qkv_weight)
    owned_qkv = lax.psum_scatter(grad_qkv_weight, "dp", scatter_dimension=0, tiled=True)
    running = around(add_low(received, term))
    inner = jnp.sum(grad_qkv.astype(f32) * qkv.astype(f32), axis=-1)
    inner = total_over(inner.reshape(-1, LANES), "mp").reshape(-1, 1) / features
    received, term, owned_out_down = together(running, first_part(3), owned_out_down)
    running = around(add_low(received, term))
    grad_table = lax.dot_general(
        bucket_hot.astype(f32),
        rel_grad,
        (((0,), (1,)), ((), ())),
        precision=lax.Precision.HIGHEST,
        preferred_element_type=f32,
    )
    early_sq = square_sum(owned_gate_up) + square_sum(owned_out_down)
    term, output_sent = together(first_part(0), output_sent)
    output_sum = around(output_sent)
    received, term, grad_table, early_sq, inner = together(
        running, term, grad_table, early_sq, inner
    )
    grad_h_first = received.astype(f32) + term
    own_gain = lax.dynamic_slice_in_dim(first_gain, member * quarter, quarter, 0)
    x_own = x_own.astype(f32)
    grad_attn_gain = jnp.sum(grad_h_first * (x_own * inv_first), axis=0)
    grad_input = (
        column_part(grad_after, 0).astype(f32)
        + inv_first * (grad_h_first * own_gain)
        - x_own * (inv_first * inv_first) * inner
    ).astype(low)
    local_sq = early_sq + square_sum(owned_qkv)
    heads_dev = bias_table.shape[1]
    first_wide = lax.dynamic_update_slice_in_dim(
        jnp.zeros((features,), f32), grad_attn_gain, member * quarter, 0
    )
    table_wide = lax.dynamic_update_slice_in_dim(
        jnp.zeros((NB, heads_dev * tensor_count), f32), grad_table, member * heads_dev, 1
    )
    sums = jnp.concatenate([first_wide, grad_ffn_gain, table_wide.reshape(-1)])
    small_count = sums.shape[0]
    sums = jnp.concatenate([sums, jnp.broadcast_to(local_sq, (LANES,))])
    sums, output_sum = together(sums, output_sum)
    sums = jnp.sum(lax.all_gather(sums.reshape(-1, LANES), "dp", axis=0), axis=0)
    sums, grad_input = together(sums, grad_input)
    came_back = lax.all_to_all(
        grad_input.reshape(group_count, -1, quarter), "dp", split_axis=0, concat_axis=0, tiled=True
    )
    group_iota = lax.broadcasted_iota(jnp.int32, (group_count, group_count), 0)
    place = jnp.argmax(deal_order[None, :] == group_iota, axis=1)
    input_grad = jnp.take(came_back, place, axis=0)

    layer_out = (output_sum.astype(f32) + output_terms[0]).astype(low)[None]
    sums = total_over(sums, "mp").reshape(-1)
    total_sq = sums[small_count] + jnp.sum(sums[:small_count] * sums[:small_count])
    grad_norm = jnp.sqrt(total_sq)
    limit = math.sqrt(4 * D * H * DH + 3 * D * FF + 2 * D + NB * H)
    factor = jnp.minimum(1.0, limit / grad_norm)
    owned_first = lax.dynamic_slice_in_dim(sums, group_index * gain_size, gain_size, 0)
    owned_second = lax.dynamic_slice_in_dim(
        sums, features + group_index * gain_size, gain_size, 0
    )
    table_rows = bias_table.shape[0]
    owned_table = lax.dynamic_slice(
        sums[2 * features : small_count].reshape(NB, heads_dev * tensor_count),
        (group_index * table_rows, member * heads_dev),
        (table_rows, heads_dev),
    )
    return (
        layer_out,
        input_grad,
        grad_norm,
        update(query_moment, owned_qkv[:, :heads_columns], factor),
        update(key_moment, owned_qkv[:, heads_columns : 2 * heads_columns], factor),
        update(value_moment, owned_qkv[:, 2 * heads_columns :], factor),
        update(out_moment, owned_out_down[:heads_columns], factor),
        update(gate_moment, owned_gate_up[:, :units], factor),
        update(up_moment, owned_gate_up[:, units:], factor),
        update(down_moment, owned_out_down[heads_columns:], factor),
        update(attn_gain_moment, owned_first, factor),
        update(ffn_gain_moment, owned_second, factor),
        update(table_moment, owned_table, factor),
    )


def solution(mesh):
    in_specs = (
        P(None, "dp", "mp"),
        P("dp", None, "mp"),
        P(),
        P(),
        P(),
        P("dp", "mp"),
        P("dp", "mp"),
        P("dp", "mp"),
        P("mp", "dp"),
        P("dp", "mp"),
        P("dp", "mp"),
        P("mp", "dp"),
        P("dp"),
        P("dp"),
        P("dp", "mp"),
        P("dp", "mp"),
        P("dp", "mp"),
        P("dp", "mp"),
        P("mp", "dp"),
        P("dp", "mp"),
        P("dp", "mp"),
        P("mp", "dp"),
        P("dp"),
        P("dp"),
        P("dp", "mp"),
    )
    out_specs = (
        P("dp", None, "mp"),
        P(None, "dp", "mp"),
        P(),
        P("dp", "mp"),
        P("dp", "mp"),
        P("dp", "mp"),
        P("mp", "dp"),
        P("dp", "mp"),
        P("dp", "mp"),
        P("mp", "dp"),
        P("dp"),
        P("dp"),
        P("dp", "mp"),
    )
    return jax.shard_map(shards, mesh=mesh, in_specs=in_specs, out_specs=out_specs, check_vma=False)
```

```python
import functools
import math

import jax
import jax.numpy as jnp
from jax import lax
from jax.experimental import pallas as pl
from jax.experimental.pallas import tpu as pltpu
from jax.sharding import PartitionSpec as P

D = 2048
H = 32
DH = 64
FF = 5120
NB = 32


EPS = 1e-06
NEG = -1e30
LANES = 128
BLOCK_ROWS = 256

NN = (((1,), (0,)), ((), ()))
NT = (((1,), (1,)), ((), ()))
TN = (((0,), (0,)), ((), ()))


def dot(left, right, dims=NN):
    return lax.dot_general(left, right, dims, preferred_element_type=jnp.float32)


def pick_head(pair_rows, which):
    lane = lax.broadcasted_iota(jnp.int32, (1, LANES), 1)
    return jnp.where(lane // DH == which, pair_rows, jnp.zeros_like(pair_rows))


def forward_kernel(length, rel_ref, query_ref, key_ref, value_ref, out_ref, soft_ref, skew):
    block = pl.program_id(1)
    rows = query_ref.shape[0]
    key_count = key_ref.shape[0]
    width = rel_ref.shape[2]

    @pl.when(block == 0)
    def _():
        for which in range(2):
            spread = jnp.broadcast_to(rel_ref[0, which : which + 1, :], (LANES, width))
            skew[which] = pltpu.roll(spread, width - (LANES - 1), 1, stride=1, stride_axis=0)

    key_at = lax.broadcasted_iota(jnp.int32, (1, key_count), 1)
    key_mask = jnp.where(key_at < length[0], 0.0, NEG)
    keys = key_ref[...]
    values = value_ref[...]
    mixed = jnp.zeros((rows, LANES), jnp.float32)
    for which in range(2):
        products = dot(pick_head(query_ref[...], which), keys, NT)
        parts = []
        for part in range(rows // LANES):
            offset = pl.multiple_of(key_count - LANES * (part + 1) - rows * block, LANES)
            parts.append(
                products[LANES * part : LANES * (part + 1)] + skew[which, :, pl.ds(offset, key_count)]
            )
        scores = jnp.concatenate(parts, 0) + key_mask
        exp_terms = jnp.exp(scores - jnp.max(scores, axis=1, keepdims=True))
        total = jnp.sum(exp_terms, axis=1, keepdims=True)
        soft_low = (exp_terms * (1.0 / total)).astype(jnp.bfloat16)
        soft_ref[which] = soft_low
        mixed = mixed + dot(soft_low, pick_head(values, which))
    out_ref[...] = mixed.astype(jnp.bfloat16)


def attend_forward(qkv, rel_rows, length, first, last, so_far=None):
    seq_len = qkv.shape[0]
    columns = qkv.shape[1] // 3
    pairs = columns // LANES
    width = rel_rows.shape[1]
    rows = min(BLOCK_ROWS, seq_len)
    kernel = forward_kernel
    operands = [length.reshape(1), rel_rows.reshape(pairs, 2, width), qkv, qkv, qkv]
    in_specs = [
        pl.BlockSpec((1, 2, width), lambda pair, block, n: (first + pair, 0, 0)),
        pl.BlockSpec((rows, LANES), lambda pair, block, n: (block, first + pair)),
        pl.BlockSpec((seq_len, LANES), lambda pair, block, n: (0, pairs + first + pair)),
        pl.BlockSpec((seq_len, LANES), lambda pair, block, n: (0, 2 * pairs + first + pair)),
    ]
    aliases = {}
    if so_far is not None:
        kernel = second_forward_kernel
        operands += so_far
        in_specs += [pl.BlockSpec(memory_space=pl.ANY)] * 2
        aliases = {5: 0, 6: 1}
    return pl.pallas_call(
        kernel,
        grid_spec=pltpu.PrefetchScalarGridSpec(
            num_scalar_prefetch=1,
            grid=(last - first, seq_len // rows),
            in_specs=in_specs,
            out_specs=[
                pl.BlockSpec((rows, LANES), lambda pair, block, n: (block, first + pair)),
                pl.BlockSpec((2, rows, seq_len), lambda pair, block, n: (first + pair, block, 0)),
            ],
            scratch_shapes=[pltpu.VMEM((2, LANES, width), jnp.float32)],
        ),
        out_shape=[
            jax.ShapeDtypeStruct((seq_len, columns), jnp.bfloat16),
            jax.ShapeDtypeStruct((2 * pairs, seq_len, seq_len), jnp.bfloat16),
        ],
        input_output_aliases=aliases,
        compiler_params=pltpu.CompilerParams(vmem_limit_bytes=40 << 20),
        cost_estimate=pl.CostEstimate(
            flops=16 * seq_len * seq_len * columns * (last - first) // pairs,
            bytes_accessed=4 * (last - first) * seq_len * seq_len,
            transcendentals=2 * (last - first) * seq_len * seq_len,
        ),
        name="attend_forward",
    )(*operands)


def second_forward_kernel(
    length, rel_ref, query_ref, key_ref, value_ref, _, __, out_ref, soft_ref, skew
):
    forward_kernel(length, rel_ref, query_ref, key_ref, value_ref, out_ref, soft_ref, skew)


def backward_kernel(
    first,
    soft_ref,
    query_ref,
    grad_ref,
    out_ref,
    key_ref,
    value_ref,
    *rest,
):
    grad_qkv_ref, rel_ref, skew, key_acc, value_acc = rest[-5:]
    pair = first + pl.program_id(0)
    block = pl.program_id(1)
    rows = query_ref.shape[0]
    key_count = key_ref.shape[0]
    columns = grad_qkv_ref.shape[1] // 3

    @pl.when(block == 0)
    def _():
        skew[...] = jnp.zeros_like(skew)
        key_acc[...] = jnp.zeros_like(key_acc)
        value_acc[...] = jnp.zeros_like(value_acc)

    if len(rest) > 5:

        @pl.when((block == 0) & (pair == first))
        def _():
            grad_qkv_ref[...] = rest[0][...]

    keys = key_ref[...]
    values = value_ref[...]
    queries = query_ref[...]
    grads = grad_ref[...]
    inner = grads.astype(jnp.float32) * out_ref[...].astype(jnp.float32)
    grad_query = jnp.zeros((rows, LANES), jnp.float32)
    for which in range(2):
        grad_head = pick_head(grads, which)
        row_inner = jnp.sum(pick_head(inner, which), axis=1, keepdims=True)
        grad_soft = dot(grad_head, values, NT)
        soft_low = soft_ref[which]
        grad_scores = soft_low.astype(jnp.float32) * (grad_soft - row_inner)
        for part in range(rows // LANES):
            offset = pl.multiple_of(key_count - LANES * (part + 1) - rows * block, LANES)
            skew[which, :, pl.ds(offset, key_count)] += grad_scores[
                LANES * part : LANES * (part + 1)
            ]
        grad_low = grad_scores.astype(jnp.bfloat16)
        grad_query = grad_query + dot(grad_low, pick_head(keys, which))
        key_acc[...] += dot(pick_head(queries, which), grad_low, TN)
        value_acc[...] += dot(grad_head, soft_low, TN)
    own_rows = pl.ds(pl.multiple_of(block * rows, rows), rows)
    own_columns = pl.multiple_of(pair * LANES, LANES)
    grad_qkv_ref[own_rows, pl.ds(own_columns, LANES)] = grad_query.astype(jnp.bfloat16)

    @pl.when(block == pl.num_programs(1) - 1)
    def _():
        grad_qkv_ref[:, pl.ds(columns + own_columns, LANES)] = key_acc[...].T.astype(jnp.bfloat16)
        grad_qkv_ref[:, pl.ds(2 * columns + own_columns, LANES)] = value_acc[...].T.astype(
            jnp.bfloat16
        )
        down = lax.broadcasted_iota(jnp.int32, (LANES, LANES), 0)
        across = lax.broadcasted_iota(jnp.int32, (LANES, LANES), 1)
        flip = (down + across == LANES - 1).astype(jnp.float32)
        for which in range(2):
            turned = lax.dot_general(
                flip,
                skew[which],
                NN,
                precision=lax.Precision.HIGHEST,
                preferred_element_type=jnp.float32,
            )
            rel_ref[0, which : which + 1, :] = jnp.sum(
                pltpu.roll(turned, 0, 1, stride=1, stride_axis=0), axis=0, keepdims=True
            )


def attend_backward(soft_low, qkv, grad_heads, attended, first, last, so_far=()):
    seq_len, columns = attended.shape
    pairs = columns // LANES
    width = 2 * seq_len
    rows = min(BLOCK_ROWS, seq_len)
    row_block = pl.BlockSpec((rows, LANES), lambda pair, block: (block, first + pair))
    whole = pl.BlockSpec((seq_len, 3 * columns), lambda pair, block: (0, 0))
    grad_qkv, rel_grad = pl.pallas_call(
        functools.partial(backward_kernel, first),
        grid=(last - first, seq_len // rows),
        in_specs=[
            pl.BlockSpec((2, rows, seq_len), lambda pair, block: (first + pair, block, 0)),
            row_block,
            row_block,
            row_block,
            pl.BlockSpec((seq_len, LANES), lambda pair, block: (0, pairs + first + pair)),
            pl.BlockSpec((seq_len, LANES), lambda pair, block: (0, 2 * pairs + first + pair)),
        ]
        + [whole] * len(so_far),
        out_specs=[whole, pl.BlockSpec((1, 2, width), lambda pair, block: (pair, 0, 0))],
        scratch_shapes=[
            pltpu.VMEM((2, LANES, width), jnp.float32),
            pltpu.VMEM((LANES, seq_len), jnp.float32),
            pltpu.VMEM((LANES, seq_len), jnp.float32),
        ],
        out_shape=[
            jax.ShapeDtypeStruct((seq_len, 3 * columns), jnp.bfloat16),
            jax.ShapeDtypeStruct((last - first, 2, width), jnp.float32),
        ],
        compiler_params=pltpu.CompilerParams(vmem_limit_bytes=48 << 20),
        cost_estimate=pl.CostEstimate(
            flops=40 * seq_len * seq_len * columns * (last - first) // pairs,
            bytes_accessed=4 * (last - first) * seq_len * seq_len,
            transcendentals=0,
        ),
        name="attend_backward",
    )(soft_low, qkv, grad_heads, attended, qkv, qkv, *so_far)
    return grad_qkv, rel_grad.reshape(2 * (last - first), width)


def around(block):
    count = lax.axis_size("mp")
    return lax.ppermute(block, "mp", [(i, (i + 1) % count) for i in range(count)])


def together(*values):
    return lax.optimization_barrier(values)


def ring_gather(own):
    blocks = [own]
    for _ in range(lax.axis_size("mp") - 1):
        blocks.append(around(blocks[-1]))
    return blocks


def add_low(received, term):
    return (received.astype(jnp.float32) + term).astype(jnp.bfloat16)


def ring_scatter(part_of):
    count = lax.axis_size("mp")
    running = part_of(1).astype(jnp.bfloat16)
    for step in range(2, count):
        received, term = together(around(running), part_of(step))
        running = add_low(received, term)
    received, term = together(around(running), part_of(0))
    return received.astype(jnp.float32) + term


def total_over(value, axis):
    count = lax.axis_size(axis)
    apart = 1
    while apart < count:
        value = value + lax.ppermute(value, axis, [(i, i ^ apart) for i in range(count)])
        apart *= 2
    return value


def update(moment, grad_owned, factor):
    return 0.5 * moment + (0.5 * factor) * grad_owned


def shards(
    layer_input,
    output_grad,
    seq_lengths,
    deal_order,
    bucket_index,
    query_weight,
    key_weight,
    value_weight,
    out_weight,
    gate_weight,
    up_weight,
    down_weight,
    attn_gain,
    ffn_gain,
    bias_table,
    query_moment,
    key_moment,
    value_moment,
    out_moment,
    gate_moment,
    up_moment,
    down_moment,
    attn_gain_moment,
    ffn_gain_moment,
    table_moment,
):
    low = jnp.bfloat16
    f32 = jnp.float32
    group_index = lax.axis_index("dp")
    member = lax.axis_index("mp")
    group_count = lax.axis_size("dp")
    tensor_count = lax.axis_size("mp")

    def back(step):
        return lax.rem(member - step + tensor_count, tensor_count)

    picked = jnp.take(layer_input, deal_order, axis=0)
    dealt = lax.all_to_all(picked, "dp", split_axis=0, concat_axis=0, tiled=True)
    x_own = dealt.reshape(-1, dealt.shape[2])
    length = seq_lengths[deal_order[group_index]]
    seq_len, quarter = x_own.shape
    features = quarter * tensor_count
    part_rows = seq_len // tensor_count

    x_own, grad_next = together(x_own, around(output_grad[0]))
    grad_parts = [output_grad[0], grad_next]
    row_valid = lax.broadcasted_iota(jnp.int32, (seq_len, 1), 0) < length

    def valid_rows(part):
        return jnp.where(row_valid, part, jnp.zeros((), low))

    def row_part(array, step):
        return lax.dynamic_slice_in_dim(array, back(step) * part_rows, part_rows, 0)

    def column_part(array, step):
        return lax.dynamic_slice_in_dim(array, back(step) * quarter, quarter, 1)

    def set_rows(whole, part, step):
        return lax.dynamic_update_slice_in_dim(whole, part, back(step) * part_rows, 0)

    def set_columns(whole, part, step):
        return lax.dynamic_update_slice_in_dim(whole, part, back(step) * quarter, 1)

    def whole_columns(parts, start):
        whole = jnp.broadcast_to(start[:1, :1], (seq_len, features))
        for step, part in enumerate(parts):
            whole = set_columns(whole, part, step)
        return whole

    qkv_weight = jnp.concatenate([query_weight, key_weight, value_weight], axis=1).astype(low)
    qkv_weight, x_own = together(qkv_weight, x_own)
    qkv_weight = lax.all_gather(qkv_weight, "dp", axis=0, tiled=True)
    gate_up = jnp.concatenate([gate_weight, up_weight], axis=1).astype(low)
    out_down = jnp.concatenate([out_weight, down_weight], axis=0).astype(low)
    heads_columns = out_weight.shape[0]
    units = down_weight.shape[0]
    x_parts = [x_own, around(x_own)]
    small = jnp.concatenate([attn_gain, ffn_gain, bias_table.reshape(-1)]).astype(low)
    small, x_parts[1] = together(lax.all_gather(small, "dp", axis=0), x_parts[1])
    for step in range(1, tensor_count - 1):
        x_parts.append(around(x_parts[step]))
    out_down, x_parts[1] = together(out_down, x_parts[1])
    out_down = lax.all_gather(out_down, "dp", axis=1, tiled=True)
    gate_up, x_parts[2] = together(gate_up, x_parts[2])
    gate_up = lax.all_gather(gate_up, "dp", axis=0, tiled=True)

    gain_size = attn_gain.shape[0]
    first_gain = small[:, :gain_size].reshape(-1).astype(f32)
    second_gain = small[:, gain_size : 2 * gain_size].reshape(-1).astype(f32)
    full_table = small[:, 2 * gain_size :].reshape(NB, bias_table.shape[1])

    def down_columns(step):
        return lax.dynamic_slice(
            out_down, (heads_columns, back(step) * quarter), (units, quarter)
        )

    grad_parts[1], x_parts[-1] = together(grad_parts[1], x_parts[-1])
    x_rows = whole_columns(x_parts, x_own)
    grad_parts.append(around(grad_parts[1]))

    offsets = jnp.concatenate([bucket_index, jnp.full((1,), NB, jnp.int32)])
    bucket_hot = offsets[:, None] == lax.broadcasted_iota(jnp.int32, (2 * seq_len, NB), 1)
    rel_rows = dot(full_table, bucket_hot.astype(low), (((0,), (1,)), ((), ())))

    x_float = x_rows.astype(f32)
    inv_first = lax.rsqrt(jnp.mean(x_float * x_float, axis=-1, keepdims=True) + EPS)
    h_first = (x_float * inv_first * first_gain).astype(low)
    qkv = dot(h_first, qkv_weight).astype(low)
    pairs = heads_columns // LANES
    so_far = attend_forward(qkv, rel_rows, length, 0, 1)
    rel_rows, grad_parts[2], *so_far = together(rel_rows, grad_parts[2], *so_far)
    grad_parts.append(around(grad_parts[2]))
    attended, soft_low = attend_forward(qkv, rel_rows, length, 1, pairs, so_far)
    attended, grad_parts[3] = together(attended, grad_parts[3])

    def attended_part(step):
        return dot(row_part(attended, step), out_down[:heads_columns])

    running = around(attended_part(1).astype(low))
    grad_y = whole_columns([valid_rows(part) for part in grad_parts[:-1]], attended)
    received, term, grad_y = together(running, attended_part(2), grad_y)
    running = around(add_low(received, term))
    grad_y = set_columns(grad_y, valid_rows(grad_parts[-1]), tensor_count - 1)
    received, term, last_term, grad_y = together(
        running, attended_part(3), attended_part(0), grad_y
    )
    running = around(add_low(received, term))
    attn_branch = running.astype(f32) + last_term

    after_attn = row_part(x_rows, 0).astype(f32) + attn_branch
    inv_second = lax.rsqrt(jnp.mean(after_attn * after_attn, axis=-1, keepdims=True) + EPS)
    h_second = (after_attn * inv_second * second_gain).astype(low)

    h_parts = [h_second]
    hidden = jnp.broadcast_to(h_second[:1, :1], (seq_len, units))
    gate_up_grads = []
    terms = {}

    def square_sum(piece):
        return jnp.sum(jnp.square(piece.astype(f32)))

    def normed_part(step):
        return dot(gate_up_grads[step], gate_up, NT)

    for step in range(tensor_count):
        if step > 0:
            last = step - 1
            term = normed_part(last)
            h_parts[step], gate_up_grads[last], hidden, terms[last] = together(
                h_parts[step],
                gate_up_grads[last],
                hidden,
                term.astype(low) if last == 1 else term,
            )
        if step < tensor_count - 1:
            h_parts.append(around(h_parts[step]))
        else:
            terms[1], h_parts[step] = together(terms[1], h_parts[step])
            running = around(terms[1])
        both = dot(h_parts[step], gate_up)
        mixed, mix_back = jax.vjp(
            lambda gate_in, up_in: jax.nn.gelu(gate_in, approximate=True) * up_in,
            both[:, :units],
            both[:, units:],
        )
        hidden = set_rows(hidden, mixed.astype(low), step)
        grad_hidden = dot(row_part(grad_y, step), out_down[heads_columns:], NT)
        gate_up_grads.append(jnp.concatenate(mix_back(grad_hidden), axis=1).astype(low))

    received, terms[2], terms[3], gate_up_grads[3], hidden = together(
        running, terms[2], normed_part(3), gate_up_grads[3], hidden
    )
    running = around(add_low(received, terms[2]))
    h_rotated = jnp.concatenate(h_parts, axis=0)
    grads_rotated = jnp.concatenate(gate_up_grads, axis=0)
    grad_gate_up = dot(h_rotated, grads_rotated, TN).astype(low)
    received, grad_gate_up = together(running, grad_gate_up)
    owned_gate_up = lax.psum_scatter(grad_gate_up, "dp", scatter_dimension=0, tiled=True)
    running = around(add_low(received, terms[3]))
    grad_down = dot(hidden, grad_y, TN).astype(low)
    received, terms[0], grad_down, hidden = together(running, terms[0], grad_down, hidden)
    grad_h_second = received.astype(f32) + terms[0]

    grad_ffn_gain = jnp.sum(grad_h_second * (after_attn * inv_second), axis=0)
    weighted = grad_h_second * second_gain
    row_inner = jnp.mean(weighted * after_attn, axis=-1, keepdims=True)
    grad_after = (
        row_part(grad_y, 0).astype(f32)
        + inv_second * weighted
        - after_attn * (inv_second * inv_second * inv_second) * row_inner
    ).astype(low)

    def output_part(step):
        part = dot(hidden, down_columns(step))
        mine = row_part(part, 0) + column_part(after_attn, step)
        return set_rows(part, mine, 0)

    after_parts = [grad_after]
    after_parts.append(around(after_parts[0]))
    output_terms = [output_part(step) for step in range(tensor_count)]
    after_parts[1], output_terms[1], output_terms[2] = together(
        after_parts[1], output_terms[1], output_terms[2]
    )
    after_parts.append(around(after_parts[1]))
    after_parts[2], output_terms[3], output_terms[0] = together(
        after_parts[2], output_terms[3], output_terms[0]
    )
    after_parts.append(around(after_parts[2]))
    grad_after = grad_y
    grad_heads = jnp.zeros((seq_len, heads_columns), low)
    for step in range(tensor_count):
        if step == tensor_count - 1:
            grad_after, grad_heads, after_parts[step] = together(
                grad_after, grad_heads, after_parts[step]
            )
        part = after_parts[step]
        grad_after = set_rows(grad_after, part, step)
        grad_heads = set_rows(grad_heads, dot(part, out_down[:heads_columns], NT).astype(low), step)
    output_first = output_terms[1].astype(low)
    output_first, grad_after, grad_heads = together(output_first, grad_after, grad_heads)
    output_sum = around(output_first)

    grad_out = dot(attended, grad_after, TN).astype(low)
    grad_heads, grad_out = together(grad_heads, grad_out)
    grad_out_down = jnp.concatenate([grad_out, grad_down], axis=0)
    owned_out_down = lax.psum_scatter(grad_out_down, "dp", scatter_dimension=1, tiled=True)
    half = pairs // 2
    first_grads, first_rel = attend_backward(soft_low, qkv, grad_heads, attended, 0, half)
    output_sum, first_grads, owned_gate_up = together(output_sum, first_grads, owned_gate_up)
    output_sum = around(add_low(output_sum, output_terms[2]))
    grad_qkv, second_rel = attend_backward(
        soft_low, qkv, grad_heads, attended, half, pairs, (first_grads,)
    )
    rel_grad = jnp.concatenate([first_rel, second_rel], axis=0)
    grad_qkv, output_sum = together(grad_qkv, output_sum)
    output_sent = add_low(output_sum, output_terms[3])

    def first_part(step):
        weight = lax.dynamic_slice_in_dim(qkv_weight, back(step) * quarter, quarter, 0)
        return dot(grad_qkv, weight, NT)

    running, grad_qkv = together(first_part(1).astype(low), grad_qkv)
    running = around(running)
    grad_qkv_weight = dot(h_first, grad_qkv, TN).astype(low)
    received, term, grad_qkv_weight = together(running, first_part(2), grad_qkv_weight)
    owned_qkv = lax.psum_scatter(grad_qkv_weight, "dp", scatter_dimension=0, tiled=True)
    running = around(add_low(received, term))
    inner = jnp.sum(grad_qkv.astype(f32) * qkv.astype(f32), axis=-1)
    inner = total_over(inner.reshape(-1, LANES), "mp").reshape(-1, 1) / features
    received, term, owned_out_down = together(running, first_part(3), owned_out_down)
    running = around(add_low(received, term))
    grad_table = lax.dot_general(
        bucket_hot.astype(f32),
        rel_grad,
        (((0,), (1,)), ((), ())),
        precision=lax.Precision.HIGHEST,
        preferred_element_type=f32,
    )
    early_sq = square_sum(owned_gate_up) + square_sum(owned_out_down)
    term, output_sent = together(first_part(0), output_sent)
    output_sum = around(output_sent)
    received, term, grad_table, early_sq, inner = together(
        running, term, grad_table, early_sq, inner
    )
    grad_h_first = received.astype(f32) + term
    own_gain = lax.dynamic_slice_in_dim(first_gain, member * quarter, quarter, 0)
    x_own = x_own.astype(f32)
    grad_attn_gain = jnp.sum(grad_h_first * (x_own * inv_first), axis=0)
    grad_input = (
        column_part(grad_after, 0).astype(f32)
        + inv_first * (grad_h_first * own_gain)
        - x_own * (inv_first * inv_first) * inner
    ).astype(low)
    local_sq = early_sq + square_sum(owned_qkv)
    heads_dev = bias_table.shape[1]
    first_wide = lax.dynamic_update_slice_in_dim(
        jnp.zeros((features,), f32), grad_attn_gain, member * quarter, 0
    )
    table_wide = lax.dynamic_update_slice_in_dim(
        jnp.zeros((NB, heads_dev * tensor_count), f32), grad_table, member * heads_dev, 1
    )
    sums = jnp.concatenate([first_wide, grad_ffn_gain, table_wide.reshape(-1)])
    small_count = sums.shape[0]
    sums = jnp.concatenate([sums, jnp.broadcast_to(local_sq, (LANES,))])
    sums = jnp.sum(lax.all_gather(sums.reshape(-1, LANES), "dp", axis=0), axis=0)
    sums, grad_input, output_sum = together(sums, grad_input, output_sum)
    came_back = lax.all_to_all(
        grad_input.reshape(group_count, -1, quarter), "dp", split_axis=0, concat_axis=0, tiled=True
    )
    group_iota = lax.broadcasted_iota(jnp.int32, (group_count, group_count), 0)
    place = jnp.argmax(deal_order[None, :] == group_iota, axis=1)
    input_grad = jnp.take(came_back, place, axis=0)

    layer_out = (output_sum.astype(f32) + output_terms[0]).astype(low)[None]
    sums = total_over(sums, "mp").reshape(-1)
    total_sq = sums[small_count] + jnp.sum(sums[:small_count] * sums[:small_count])
    grad_norm = jnp.sqrt(total_sq)
    limit = math.sqrt(4 * D * H * DH + 3 * D * FF + 2 * D + NB * H)
    factor = jnp.minimum(1.0, limit / grad_norm)
    owned_first = lax.dynamic_slice_in_dim(sums, group_index * gain_size, gain_size, 0)
    owned_second = lax.dynamic_slice_in_dim(
        sums, features + group_index * gain_size, gain_size, 0
    )
    table_rows = bias_table.shape[0]
    owned_table = lax.dynamic_slice(
        sums[2 * features : small_count].reshape(NB, heads_dev * tensor_count),
        (group_index * table_rows, member * heads_dev),
        (table_rows, heads_dev),
    )
    return (
        layer_out,
        input_grad,
        grad_norm,
        update(query_moment, owned_qkv[:, :heads_columns], factor),
        update(key_moment, owned_qkv[:, heads_columns : 2 * heads_columns], factor),
        update(value_moment, owned_qkv[:, 2 * heads_columns :], factor),
        update(out_moment, owned_out_down[:heads_columns], factor),
        update(gate_moment, owned_gate_up[:, :units], factor),
        update(up_moment, owned_gate_up[:, units:], factor),
        update(down_moment, owned_out_down[heads_columns:], factor),
        update(attn_gain_moment, owned_first, factor),
        update(ffn_gain_moment, owned_second, factor),
        update(table_moment, owned_table, factor),
    )


def solution(mesh):
    in_specs = (
        P(None, "dp", "mp"),
        P("dp", None, "mp"),
        P(),
        P(),
        P(),
        P("dp", "mp"),
        P("dp", "mp"),
        P("dp", "mp"),
        P("mp", "dp"),
        P("dp", "mp"),
        P("dp", "mp"),
        P("mp", "dp"),
        P("dp"),
        P("dp"),
        P("dp", "mp"),
        P("dp", "mp"),
        P("dp", "mp"),
        P("dp", "mp"),
        P("mp", "dp"),
        P("dp", "mp"),
        P("dp", "mp"),
        P("mp", "dp"),
        P("dp"),
        P("dp"),
        P("dp", "mp"),
    )
    out_specs = (
        P("dp", None, "mp"),
        P(None, "dp", "mp"),
        P(),
        P("dp", "mp"),
        P("dp", "mp"),
        P("dp", "mp"),
        P("mp", "dp"),
        P("dp", "mp"),
        P("dp", "mp"),
        P("mp", "dp"),
        P("dp"),
        P("dp"),
        P("dp", "mp"),
    )
    return jax.shard_map(shards, mesh=mesh, in_specs=in_specs, out_specs=out_specs, check_vma=False)
```

```python
import functools
import math

import jax
import jax.numpy as jnp
from jax import lax
from jax.experimental import pallas as pl
from jax.experimental.pallas import tpu as pltpu
from jax.sharding import PartitionSpec as P

D = 2048
H = 32
DH = 64
FF = 5120
NB = 32


EPS = 1e-06
NEG = -1e30
LANES = 128
BLOCK_ROWS = 256

NN = (((1,), (0,)), ((), ()))
NT = (((1,), (1,)), ((), ()))
TN = (((0,), (0,)), ((), ()))


def dot(left, right, dims=NN):
    return lax.dot_general(left, right, dims, preferred_element_type=jnp.float32)


def pick_head(pair_rows, which):
    lane = lax.broadcasted_iota(jnp.int32, (1, LANES), 1)
    return jnp.where(lane // DH == which, pair_rows, jnp.zeros_like(pair_rows))


def forward_kernel(length, rel_ref, query_ref, key_ref, value_ref, out_ref, soft_ref, skew):
    block = pl.program_id(1)
    rows = query_ref.shape[0]
    key_count = key_ref.shape[0]
    width = rel_ref.shape[2]

    @pl.when(block == 0)
    def _():
        for which in range(2):
            spread = jnp.broadcast_to(rel_ref[0, which : which + 1, :], (LANES, width))
            skew[which] = pltpu.roll(spread, width - (LANES - 1), 1, stride=1, stride_axis=0)

    key_at = lax.broadcasted_iota(jnp.int32, (1, key_count), 1)
    key_mask = jnp.where(key_at < length[0], 0.0, NEG)
    keys = key_ref[...]
    values = value_ref[...]
    mixed = jnp.zeros((rows, LANES), jnp.float32)
    for which in range(2):
        products = dot(pick_head(query_ref[...], which), keys, NT)
        parts = []
        for part in range(rows // LANES):
            offset = pl.multiple_of(key_count - LANES * (part + 1) - rows * block, LANES)
            parts.append(
                products[LANES * part : LANES * (part + 1)] + skew[which, :, pl.ds(offset, key_count)]
            )
        scores = jnp.concatenate(parts, 0) + key_mask
        exp_terms = jnp.exp(scores - jnp.max(scores, axis=1, keepdims=True))
        total = jnp.sum(exp_terms, axis=1, keepdims=True)
        soft_low = (exp_terms * (1.0 / total)).astype(jnp.bfloat16)
        soft_ref[which] = soft_low
        mixed = mixed + dot(soft_low, pick_head(values, which))
    out_ref[...] = mixed.astype(jnp.bfloat16)


def attend_forward(qkv, rel_rows, length, first, last, so_far=None):
    seq_len = qkv.shape[0]
    columns = qkv.shape[1] // 3
    pairs = columns // LANES
    width = rel_rows.shape[1]
    rows = min(BLOCK_ROWS, seq_len)
    kernel = forward_kernel
    operands = [length.reshape(1), rel_rows.reshape(pairs, 2, width), qkv, qkv, qkv]
    in_specs = [
        pl.BlockSpec((1, 2, width), lambda pair, block, n: (first + pair, 0, 0)),
        pl.BlockSpec((rows, LANES), lambda pair, block, n: (block, first + pair)),
        pl.BlockSpec((seq_len, LANES), lambda pair, block, n: (0, pairs + first + pair)),
        pl.BlockSpec((seq_len, LANES), lambda pair, block, n: (0, 2 * pairs + first + pair)),
    ]
    aliases = {}
    if so_far is not None:
        kernel = second_forward_kernel
        operands += so_far
        in_specs += [pl.BlockSpec(memory_space=pl.ANY)] * 2
        aliases = {5: 0, 6: 1}
    return pl.pallas_call(
        kernel,
        grid_spec=pltpu.PrefetchScalarGridSpec(
            num_scalar_prefetch=1,
            grid=(last - first, seq_len // rows),
            in_specs=in_specs,
            out_specs=[
                pl.BlockSpec((rows, LANES), lambda pair, block, n: (block, first + pair)),
                pl.BlockSpec((2, rows, seq_len), lambda pair, block, n: (first + pair, block, 0)),
            ],
            scratch_shapes=[pltpu.VMEM((2, LANES, width), jnp.float32)],
        ),
        out_shape=[
            jax.ShapeDtypeStruct((seq_len, columns), jnp.bfloat16),
            jax.ShapeDtypeStruct((2 * pairs, seq_len, seq_len), jnp.bfloat16),
        ],
        input_output_aliases=aliases,
        compiler_params=pltpu.CompilerParams(vmem_limit_bytes=40 << 20),
        cost_estimate=pl.CostEstimate(
            flops=16 * seq_len * seq_len * columns * (last - first) // pairs,
            bytes_accessed=4 * (last - first) * seq_len * seq_len,
            transcendentals=2 * (last - first) * seq_len * seq_len,
        ),
        name="attend_forward",
    )(*operands)


def second_forward_kernel(
    length, rel_ref, query_ref, key_ref, value_ref, _, __, out_ref, soft_ref, skew
):
    forward_kernel(length, rel_ref, query_ref, key_ref, value_ref, out_ref, soft_ref, skew)


def backward_kernel(
    first,
    soft_ref,
    query_ref,
    grad_ref,
    out_ref,
    key_ref,
    value_ref,
    *rest,
):
    grad_qkv_ref, rel_ref, skew, key_acc, value_acc = rest[-5:]
    pair = first + pl.program_id(0)
    block = pl.program_id(1)
    rows = query_ref.shape[0]
    key_count = key_ref.shape[0]
    columns = grad_qkv_ref.shape[1] // 3

    @pl.when(block == 0)
    def _():
        skew[...] = jnp.zeros_like(skew)
        key_acc[...] = jnp.zeros_like(key_acc)
        value_acc[...] = jnp.zeros_like(value_acc)

    if len(rest) > 5:

        @pl.when((block == 0) & (pair == first))
        def _():
            grad_qkv_ref[...] = rest[0][...]

    keys = key_ref[...]
    values = value_ref[...]
    queries = query_ref[...]
    grads = grad_ref[...]
    inner = grads.astype(jnp.float32) * out_ref[...].astype(jnp.float32)
    grad_query = jnp.zeros((rows, LANES), jnp.float32)
    for which in range(2):
        grad_head = pick_head(grads, which)
        row_inner = jnp.sum(pick_head(inner, which), axis=1, keepdims=True)
        grad_soft = dot(grad_head, values, NT)
        soft_low = soft_ref[which]
        grad_scores = soft_low.astype(jnp.float32) * (grad_soft - row_inner)
        for part in range(rows // LANES):
            offset = pl.multiple_of(key_count - LANES * (part + 1) - rows * block, LANES)
            skew[which, :, pl.ds(offset, key_count)] += grad_scores[
                LANES * part : LANES * (part + 1)
            ]
        grad_low = grad_scores.astype(jnp.bfloat16)
        grad_query = grad_query + dot(grad_low, pick_head(keys, which))
        key_acc[...] += dot(pick_head(queries, which), grad_low, TN)
        value_acc[...] += dot(grad_head, soft_low, TN)
    own_rows = pl.ds(pl.multiple_of(block * rows, rows), rows)
    own_columns = pl.multiple_of(pair * LANES, LANES)
    grad_qkv_ref[own_rows, pl.ds(own_columns, LANES)] = grad_query.astype(jnp.bfloat16)

    @pl.when(block == pl.num_programs(1) - 1)
    def _():
        grad_qkv_ref[:, pl.ds(columns + own_columns, LANES)] = key_acc[...].T.astype(jnp.bfloat16)
        grad_qkv_ref[:, pl.ds(2 * columns + own_columns, LANES)] = value_acc[...].T.astype(
            jnp.bfloat16
        )
        down = lax.broadcasted_iota(jnp.int32, (LANES, LANES), 0)
        across = lax.broadcasted_iota(jnp.int32, (LANES, LANES), 1)
        flip = (down + across == LANES - 1).astype(jnp.float32)
        for which in range(2):
            turned = lax.dot_general(
                flip,
                skew[which],
                NN,
                precision=lax.Precision.HIGHEST,
                preferred_element_type=jnp.float32,
            )
            rel_ref[0, which : which + 1, :] = jnp.sum(
                pltpu.roll(turned, 0, 1, stride=1, stride_axis=0), axis=0, keepdims=True
            )


def attend_backward(soft_low, qkv, grad_heads, attended, first, last, so_far=()):
    seq_len, columns = attended.shape
    pairs = columns // LANES
    width = 2 * seq_len
    rows = min(BLOCK_ROWS, seq_len)
    row_block = pl.BlockSpec((rows, LANES), lambda pair, block: (block, first + pair))
    whole = pl.BlockSpec((seq_len, 3 * columns), lambda pair, block: (0, 0))
    grad_qkv, rel_grad = pl.pallas_call(
        functools.partial(backward_kernel, first),
        grid=(last - first, seq_len // rows),
        in_specs=[
            pl.BlockSpec((2, rows, seq_len), lambda pair, block: (first + pair, block, 0)),
            row_block,
            row_block,
            row_block,
            pl.BlockSpec((seq_len, LANES), lambda pair, block: (0, pairs + first + pair)),
            pl.BlockSpec((seq_len, LANES), lambda pair, block: (0, 2 * pairs + first + pair)),
        ]
        + [whole] * len(so_far),
        out_specs=[whole, pl.BlockSpec((1, 2, width), lambda pair, block: (pair, 0, 0))],
        scratch_shapes=[
            pltpu.VMEM((2, LANES, width), jnp.float32),
            pltpu.VMEM((LANES, seq_len), jnp.float32),
            pltpu.VMEM((LANES, seq_len), jnp.float32),
        ],
        out_shape=[
            jax.ShapeDtypeStruct((seq_len, 3 * columns), jnp.bfloat16),
            jax.ShapeDtypeStruct((last - first, 2, width), jnp.float32),
        ],
        compiler_params=pltpu.CompilerParams(vmem_limit_bytes=48 << 20),
        cost_estimate=pl.CostEstimate(
            flops=40 * seq_len * seq_len * columns * (last - first) // pairs,
            bytes_accessed=4 * (last - first) * seq_len * seq_len,
            transcendentals=0,
        ),
        name="attend_backward",
    )(soft_low, qkv, grad_heads, attended, qkv, qkv, *so_far)
    return grad_qkv, rel_grad.reshape(2 * (last - first), width)


def around(block):
    count = lax.axis_size("mp")
    return lax.ppermute(block, "mp", [(i, (i + 1) % count) for i in range(count)])


def together(*values):
    return lax.optimization_barrier(values)


def ring_gather(own):
    blocks = [own]
    for _ in range(lax.axis_size("mp") - 1):
        blocks.append(around(blocks[-1]))
    return blocks


def add_low(received, term):
    return (received.astype(jnp.float32) + term).astype(jnp.bfloat16)


def ring_scatter(part_of):
    count = lax.axis_size("mp")
    running = part_of(1).astype(jnp.bfloat16)
    for step in range(2, count):
        received, term = together(around(running), part_of(step))
        running = add_low(received, term)
    received, term = together(around(running), part_of(0))
    return received.astype(jnp.float32) + term


def total_over(value, axis):
    count = lax.axis_size(axis)
    apart = 1
    while apart < count:
        value = value + lax.ppermute(value, axis, [(i, i ^ apart) for i in range(count)])
        apart *= 2
    return value


def update(moment, grad_owned, factor):
    return 0.5 * moment + (0.5 * factor) * grad_owned


def shards(
    layer_input,
    output_grad,
    seq_lengths,
    deal_order,
    bucket_index,
    query_weight,
    key_weight,
    value_weight,
    out_weight,
    gate_weight,
    up_weight,
    down_weight,
    attn_gain,
    ffn_gain,
    bias_table,
    query_moment,
    key_moment,
    value_moment,
    out_moment,
    gate_moment,
    up_moment,
    down_moment,
    attn_gain_moment,
    ffn_gain_moment,
    table_moment,
):
    low = jnp.bfloat16
    f32 = jnp.float32
    group_index = lax.axis_index("dp")
    member = lax.axis_index("mp")
    group_count = lax.axis_size("dp")
    tensor_count = lax.axis_size("mp")

    def back(step):
        return lax.rem(member - step + tensor_count, tensor_count)

    picked = jnp.take(layer_input, deal_order, axis=0)
    dealt = lax.all_to_all(picked, "dp", split_axis=0, concat_axis=0, tiled=True)
    x_own = dealt.reshape(-1, dealt.shape[2])
    length = seq_lengths[deal_order[group_index]]
    seq_len, quarter = x_own.shape
    features = quarter * tensor_count
    part_rows = seq_len // tensor_count

    x_own, grad_next = together(x_own, around(output_grad[0]))
    grad_parts = [output_grad[0], grad_next]
    row_valid = lax.broadcasted_iota(jnp.int32, (seq_len, 1), 0) < length

    def valid_rows(part):
        return jnp.where(row_valid, part, jnp.zeros((), low))

    def row_part(array, step):
        return lax.dynamic_slice_in_dim(array, back(step) * part_rows, part_rows, 0)

    def column_part(array, step):
        return lax.dynamic_slice_in_dim(array, back(step) * quarter, quarter, 1)

    def set_rows(whole, part, step):
        return lax.dynamic_update_slice_in_dim(whole, part, back(step) * part_rows, 0)

    def set_columns(whole, part, step):
        return lax.dynamic_update_slice_in_dim(whole, part, back(step) * quarter, 1)

    def whole_columns(parts, start):
        whole = jnp.broadcast_to(start[:1, :1], (seq_len, features))
        for step, part in enumerate(parts):
            whole = set_columns(whole, part, step)
        return whole

    qkv_weight = jnp.concatenate([query_weight, key_weight, value_weight], axis=1).astype(low)
    qkv_weight, x_own = together(qkv_weight, x_own)
    qkv_weight = lax.all_gather(qkv_weight, "dp", axis=0, tiled=True)
    gate_up = jnp.concatenate([gate_weight, up_weight], axis=1).astype(low)
    out_down = jnp.concatenate([out_weight, down_weight], axis=0).astype(low)
    heads_columns = out_weight.shape[0]
    units = down_weight.shape[0]
    x_parts = [x_own, around(x_own)]
    small = jnp.concatenate([attn_gain, ffn_gain, bias_table.reshape(-1)]).astype(low)
    small, x_parts[1] = together(lax.all_gather(small, "dp", axis=0), x_parts[1])
    for step in range(1, tensor_count - 1):
        x_parts.append(around(x_parts[step]))
    out_down, x_parts[1] = together(out_down, x_parts[1])
    out_down = lax.all_gather(out_down, "dp", axis=1, tiled=True)
    gate_up, x_parts[2] = together(gate_up, x_parts[2])
    gate_up = lax.all_gather(gate_up, "dp", axis=0, tiled=True)

    gain_size = attn_gain.shape[0]
    first_gain = small[:, :gain_size].reshape(-1).astype(f32)
    second_gain = small[:, gain_size : 2 * gain_size].reshape(-1).astype(f32)
    full_table = small[:, 2 * gain_size :].reshape(NB, bias_table.shape[1])

    def down_columns(step):
        return lax.dynamic_slice(
            out_down, (heads_columns, back(step) * quarter), (units, quarter)
        )

    grad_parts[1], x_parts[-1] = together(grad_parts[1], x_parts[-1])
    x_rows = whole_columns(x_parts, x_own)
    grad_parts.append(around(grad_parts[1]))

    offsets = jnp.concatenate([bucket_index, jnp.full((1,), NB, jnp.int32)])
    bucket_hot = offsets[:, None] == lax.broadcasted_iota(jnp.int32, (2 * seq_len, NB), 1)
    rel_rows = dot(full_table, bucket_hot.astype(low), (((0,), (1,)), ((), ())))

    x_float = x_rows.astype(f32)
    inv_first = lax.rsqrt(jnp.mean(x_float * x_float, axis=-1, keepdims=True) + EPS)
    h_first = (x_float * inv_first * first_gain).astype(low)
    qkv = dot(h_first, qkv_weight).astype(low)
    pairs = heads_columns // LANES
    so_far = attend_forward(qkv, rel_rows, length, 0, 1)
    rel_rows, grad_parts[2], *so_far = together(rel_rows, grad_parts[2], *so_far)
    grad_parts.append(around(grad_parts[2]))
    attended, soft_low = attend_forward(qkv, rel_rows, length, 1, pairs, so_far)
    attended, grad_parts[3] = together(attended, grad_parts[3])

    def attended_part(step):
        return dot(row_part(attended, step), out_down[:heads_columns])

    running = around(attended_part(1).astype(low))
    grad_y = whole_columns([valid_rows(part) for part in grad_parts[:-1]], attended)
    received, term, grad_y = together(running, attended_part(2), grad_y)
    running = around(add_low(received, term))
    grad_y = set_columns(grad_y, valid_rows(grad_parts[-1]), tensor_count - 1)
    received, term, last_term, grad_y = together(
        running, attended_part(3), attended_part(0), grad_y
    )
    running = around(add_low(received, term))
    attn_branch = running.astype(f32) + last_term

    after_attn = row_part(x_rows, 0).astype(f32) + attn_branch
    inv_second = lax.rsqrt(jnp.mean(after_attn * after_attn, axis=-1, keepdims=True) + EPS)
    h_second = (after_attn * inv_second * second_gain).astype(low)

    h_parts = [h_second]
    hidden = jnp.broadcast_to(h_second[:1, :1], (seq_len, units))
    gate_up_grads = []
    terms = {}

    def square_sum(piece):
        return jnp.sum(jnp.square(piece.astype(f32)))

    def normed_part(step):
        return dot(gate_up_grads[step], gate_up, NT)

    for step in range(tensor_count):
        if step > 0:
            last = step - 1
            term = normed_part(last)
            h_parts[step], gate_up_grads[last], hidden, terms[last] = together(
                h_parts[step],
                gate_up_grads[last],
                hidden,
                term.astype(low) if last > 0 else term,
            )
        if step < tensor_count - 1:
            h_parts.append(around(h_parts[step]))
        else:
            terms[1], h_parts[step] = together(terms[1], h_parts[step])
            running = around(terms[1])
        both = dot(h_parts[step], gate_up)
        mixed, mix_back = jax.vjp(
            lambda gate_in, up_in: jax.nn.gelu(gate_in, approximate=True) * up_in,
            both[:, :units],
            both[:, units:],
        )
        hidden = set_rows(hidden, mixed.astype(low), step)
        grad_hidden = dot(row_part(grad_y, step), out_down[heads_columns:], NT)
        gate_up_grads.append(jnp.concatenate(mix_back(grad_hidden), axis=1).astype(low))

    received, terms[2], terms[3], gate_up_grads[3], hidden = together(
        running, terms[2], normed_part(3).astype(low), gate_up_grads[3], hidden
    )
    running = around(add_low(received, terms[2]))
    h_rotated = jnp.concatenate(h_parts, axis=0)
    grads_rotated = jnp.concatenate(gate_up_grads, axis=0)
    grad_gate_up = dot(h_rotated, grads_rotated, TN).astype(low)
    received, grad_gate_up = together(running, grad_gate_up)
    owned_gate_up = lax.psum_scatter(grad_gate_up, "dp", scatter_dimension=0, tiled=True)
    running = around(add_low(received, terms[3]))
    grad_down = dot(hidden, grad_y, TN).astype(low)
    received, terms[0], grad_down, hidden = together(running, terms[0], grad_down, hidden)
    grad_h_second = received.astype(f32) + terms[0]

    grad_ffn_gain = jnp.sum(grad_h_second * (after_attn * inv_second), axis=0)
    weighted = grad_h_second * second_gain
    row_inner = jnp.mean(weighted * after_attn, axis=-1, keepdims=True)
    grad_after = (
        row_part(grad_y, 0).astype(f32)
        + inv_second * weighted
        - after_attn * (inv_second * inv_second * inv_second) * row_inner
    ).astype(low)

    def output_part(step):
        part = dot(hidden, down_columns(step))
        mine = row_part(part, 0) + column_part(after_attn, step)
        return set_rows(part, mine, 0)

    after_parts = [grad_after]
    after_parts.append(around(after_parts[0]))
    output_terms = [output_part(step) for step in range(tensor_count)]
    after_parts[1], output_terms[1], output_terms[2] = together(
        after_parts[1], output_terms[1], output_terms[2]
    )
    after_parts.append(around(after_parts[1]))
    after_parts[2], output_terms[3], output_terms[0] = together(
        after_parts[2], output_terms[3], output_terms[0]
    )
    after_parts.append(around(after_parts[2]))
    grad_after = grad_y
    grad_heads = jnp.zeros((seq_len, heads_columns), low)
    for step in range(tensor_count):
        if step == tensor_count - 1:
            grad_after, grad_heads, after_parts[step] = together(
                grad_after, grad_heads, after_parts[step]
            )
        part = after_parts[step]
        grad_after = set_rows(grad_after, part, step)
        grad_heads = set_rows(grad_heads, dot(part, out_down[:heads_columns], NT).astype(low), step)
    output_first = output_terms[1].astype(low)
    output_first, grad_after, grad_heads = together(output_first, grad_after, grad_heads)
    output_sum = around(output_first)

    grad_out = dot(attended, grad_after, TN).astype(low)
    grad_heads, grad_out = together(grad_heads, grad_out)
    grad_out_down = jnp.concatenate([grad_out, grad_down], axis=0)
    owned_out_down = lax.psum_scatter(grad_out_down, "dp", scatter_dimension=1, tiled=True)
    half = pairs // 2
    first_grads, first_rel = attend_backward(soft_low, qkv, grad_heads, attended, 0, half)
    output_sum, first_grads, owned_gate_up = together(output_sum, first_grads, owned_gate_up)
    output_sum = around(add_low(output_sum, output_terms[2]))
    grad_qkv, second_rel = attend_backward(
        soft_low, qkv, grad_heads, attended, half, pairs, (first_grads,)
    )
    rel_grad = jnp.concatenate([first_rel, second_rel], axis=0)
    grad_qkv, output_sum = together(grad_qkv, output_sum)
    output_sent = add_low(output_sum, output_terms[3])

    def first_part(step):
        weight = lax.dynamic_slice_in_dim(qkv_weight, back(step) * quarter, quarter, 0)
        return dot(grad_qkv, weight, NT).astype(low)

    running, grad_qkv = together(first_part(1), grad_qkv)
    running = around(running)
    grad_qkv_weight = dot(h_first, grad_qkv, TN).astype(low)
    received, term, grad_qkv_weight = together(running, first_part(2), grad_qkv_weight)
    owned_qkv = lax.psum_scatter(grad_qkv_weight, "dp", scatter_dimension=0, tiled=True)
    running = around(add_low(received, term))
    inner = jnp.sum(grad_qkv.astype(f32) * qkv.astype(f32), axis=-1)
    inner = total_over(inner.reshape(-1, LANES), "mp").reshape(-1, 1) / features
    received, term, owned_out_down = together(running, first_part(3), owned_out_down)
    running = around(add_low(received, term))
    grad_table = lax.dot_general(
        bucket_hot.astype(f32),
        rel_grad,
        (((0,), (1,)), ((), ())),
        precision=lax.Precision.HIGHEST,
        preferred_element_type=f32,
    )
    early_sq = square_sum(owned_gate_up) + square_sum(owned_out_down)
    term, output_sent = together(first_part(0), output_sent)
    output_sum = around(output_sent)
    received, term, grad_table, early_sq, inner = together(
        running, term, grad_table, early_sq, inner
    )
    grad_h_first = received.astype(f32) + term
    own_gain = lax.dynamic_slice_in_dim(first_gain, member * quarter, quarter, 0)
    x_own = x_own.astype(f32)
    grad_attn_gain = jnp.sum(grad_h_first * (x_own * inv_first), axis=0)
    grad_input = (
        column_part(grad_after, 0).astype(f32)
        + inv_first * (grad_h_first * own_gain)
        - x_own * (inv_first * inv_first) * inner
    ).astype(low)
    local_sq = early_sq + square_sum(owned_qkv)
    heads_dev = bias_table.shape[1]
    first_wide = lax.dynamic_update_slice_in_dim(
        jnp.zeros((features,), f32), grad_attn_gain, member * quarter, 0
    )
    table_wide = lax.dynamic_update_slice_in_dim(
        jnp.zeros((NB, heads_dev * tensor_count), f32), grad_table, member * heads_dev, 1
    )
    sums = jnp.concatenate([first_wide, grad_ffn_gain, table_wide.reshape(-1)])
    small_count = sums.shape[0]
    sums = jnp.concatenate([sums, jnp.broadcast_to(local_sq, (LANES,))])
    sums = jnp.sum(lax.all_gather(sums.reshape(-1, LANES), "dp", axis=0), axis=0)
    sums, grad_input, output_sum = together(sums, grad_input, output_sum)
    came_back = lax.all_to_all(
        grad_input.reshape(group_count, -1, quarter), "dp", split_axis=0, concat_axis=0, tiled=True
    )
    group_iota = lax.broadcasted_iota(jnp.int32, (group_count, group_count), 0)
    place = jnp.argmax(deal_order[None, :] == group_iota, axis=1)
    input_grad = jnp.take(came_back, place, axis=0)

    layer_out = (output_sum.astype(f32) + output_terms[0]).astype(low)[None]
    sums = total_over(sums, "mp").reshape(-1)
    total_sq = sums[small_count] + jnp.sum(sums[:small_count] * sums[:small_count])
    grad_norm = jnp.sqrt(total_sq)
    limit = math.sqrt(4 * D * H * DH + 3 * D * FF + 2 * D + NB * H)
    factor = jnp.minimum(1.0, limit / grad_norm)
    owned_first = lax.dynamic_slice_in_dim(sums, group_index * gain_size, gain_size, 0)
    owned_second = lax.dynamic_slice_in_dim(
        sums, features + group_index * gain_size, gain_size, 0
    )
    table_rows = bias_table.shape[0]
    owned_table = lax.dynamic_slice(
        sums[2 * features : small_count].reshape(NB, heads_dev * tensor_count),
        (group_index * table_rows, member * heads_dev),
        (table_rows, heads_dev),
    )
    return (
        layer_out,
        input_grad,
        grad_norm,
        update(query_moment, owned_qkv[:, :heads_columns], factor),
        update(key_moment, owned_qkv[:, heads_columns : 2 * heads_columns], factor),
        update(value_moment, owned_qkv[:, 2 * heads_columns :], factor),
        update(out_moment, owned_out_down[:heads_columns], factor),
        update(gate_moment, owned_gate_up[:, :units], factor),
        update(up_moment, owned_gate_up[:, units:], factor),
        update(down_moment, owned_out_down[heads_columns:], factor),
        update(attn_gain_moment, owned_first, factor),
        update(ffn_gain_moment, owned_second, factor),
        update(table_moment, owned_table, factor),
    )


def solution(mesh):
    in_specs = (
        P(None, "dp", "mp"),
        P("dp", None, "mp"),
        P(),
        P(),
        P(),
        P("dp", "mp"),
        P("dp", "mp"),
        P("dp", "mp"),
        P("mp", "dp"),
        P("dp", "mp"),
        P("dp", "mp"),
        P("mp", "dp"),
        P("dp"),
        P("dp"),
        P("dp", "mp"),
        P("dp", "mp"),
        P("dp", "mp"),
        P("dp", "mp"),
        P("mp", "dp"),
        P("dp", "mp"),
        P("dp", "mp"),
        P("mp", "dp"),
        P("dp"),
        P("dp"),
        P("dp", "mp"),
    )
    out_specs = (
        P("dp", None, "mp"),
        P(None, "dp", "mp"),
        P(),
        P("dp", "mp"),
        P("dp", "mp"),
        P("dp", "mp"),
        P("mp", "dp"),
        P("dp", "mp"),
        P("dp", "mp"),
        P("mp", "dp"),
        P("dp"),
        P("dp"),
        P("dp", "mp"),
    )
    return jax.shard_map(shards, mesh=mesh, in_specs=in_specs, out_specs=out_specs, check_vma=False)
```

```python
import functools
import math

import jax
import jax.numpy as jnp
from jax import lax
from jax.experimental import pallas as pl
from jax.experimental.pallas import tpu as pltpu
from jax.sharding import PartitionSpec as P

D = 2048
H = 32
DH = 64
FF = 5120
NB = 32


EPS = 1e-06
NEG = -1e30
LANES = 128
BLOCK_ROWS = 256

NN = (((1,), (0,)), ((), ()))
NT = (((1,), (1,)), ((), ()))
TN = (((0,), (0,)), ((), ()))


def dot(left, right, dims=NN):
    return lax.dot_general(left, right, dims, preferred_element_type=jnp.float32)


def pick_head(pair_rows, which):
    lane = lax.broadcasted_iota(jnp.int32, (1, LANES), 1)
    return jnp.where(lane // DH == which, pair_rows, jnp.zeros_like(pair_rows))


def forward_kernel(length, rel_ref, query_ref, key_ref, value_ref, out_ref, soft_ref, skew):
    block = pl.program_id(1)
    rows = query_ref.shape[0]
    key_count = key_ref.shape[0]
    width = rel_ref.shape[2]

    @pl.when(block == 0)
    def _():
        for which in range(2):
            spread = jnp.broadcast_to(rel_ref[0, which : which + 1, :], (LANES, width))
            skew[which] = pltpu.roll(spread, width - (LANES - 1), 1, stride=1, stride_axis=0)

    key_at = lax.broadcasted_iota(jnp.int32, (1, key_count), 1)
    key_mask = jnp.where(key_at < length[0], 0.0, NEG)
    keys = key_ref[...]
    values = value_ref[...]
    mixed = jnp.zeros((rows, LANES), jnp.float32)
    for which in range(2):
        products = dot(pick_head(query_ref[...], which), keys, NT)
        parts = []
        for part in range(rows // LANES):
            offset = pl.multiple_of(key_count - LANES * (part + 1) - rows * block, LANES)
            parts.append(
                products[LANES * part : LANES * (part + 1)] + skew[which, :, pl.ds(offset, key_count)]
            )
        scores = jnp.concatenate(parts, 0) + key_mask
        exp_terms = jnp.exp(scores - jnp.max(scores, axis=1, keepdims=True))
        total = jnp.sum(exp_terms, axis=1, keepdims=True)
        soft_low = (exp_terms * (1.0 / total)).astype(jnp.bfloat16)
        soft_ref[which] = soft_low
        mixed = mixed + dot(soft_low, pick_head(values, which))
    out_ref[...] = mixed.astype(jnp.bfloat16)


def attend_forward(qkv, rel_rows, length, first, last, so_far=None):
    seq_len = qkv.shape[0]
    columns = qkv.shape[1] // 3
    pairs = columns // LANES
    width = rel_rows.shape[1]
    rows = min(BLOCK_ROWS, seq_len)
    kernel = forward_kernel
    operands = [length.reshape(1), rel_rows.reshape(pairs, 2, width), qkv, qkv, qkv]
    in_specs = [
        pl.BlockSpec((1, 2, width), lambda pair, block, n: (first + pair, 0, 0)),
        pl.BlockSpec((rows, LANES), lambda pair, block, n: (block, first + pair)),
        pl.BlockSpec((seq_len, LANES), lambda pair, block, n: (0, pairs + first + pair)),
        pl.BlockSpec((seq_len, LANES), lambda pair, block, n: (0, 2 * pairs + first + pair)),
    ]
    aliases = {}
    if so_far is not None:
        kernel = second_forward_kernel
        operands += so_far
        in_specs += [pl.BlockSpec(memory_space=pl.ANY)] * 2
        aliases = {5: 0, 6: 1}
    return pl.pallas_call(
        kernel,
        grid_spec=pltpu.PrefetchScalarGridSpec(
            num_scalar_prefetch=1,
            grid=(last - first, seq_len // rows),
            in_specs=in_specs,
            out_specs=[
                pl.BlockSpec((rows, LANES), lambda pair, block, n: (block, first + pair)),
                pl.BlockSpec((2, rows, seq_len), lambda pair, block, n: (first + pair, block, 0)),
            ],
            scratch_shapes=[pltpu.VMEM((2, LANES, width), jnp.float32)],
        ),
        out_shape=[
            jax.ShapeDtypeStruct((seq_len, columns), jnp.bfloat16),
            jax.ShapeDtypeStruct((2 * pairs, seq_len, seq_len), jnp.bfloat16),
        ],
        input_output_aliases=aliases,
        compiler_params=pltpu.CompilerParams(vmem_limit_bytes=40 << 20),
        cost_estimate=pl.CostEstimate(
            flops=16 * seq_len * seq_len * columns * (last - first) // pairs,
            bytes_accessed=4 * (last - first) * seq_len * seq_len,
            transcendentals=2 * (last - first) * seq_len * seq_len,
        ),
        name="attend_forward",
    )(*operands)


def second_forward_kernel(
    length, rel_ref, query_ref, key_ref, value_ref, _, __, out_ref, soft_ref, skew
):
    forward_kernel(length, rel_ref, query_ref, key_ref, value_ref, out_ref, soft_ref, skew)


def backward_kernel(
    first,
    soft_ref,
    query_ref,
    grad_ref,
    out_ref,
    key_ref,
    value_ref,
    *rest,
):
    grad_qkv_ref, rel_ref, skew, key_acc, value_acc = rest[-5:]
    pair = first + pl.program_id(0)
    block = pl.program_id(1)
    rows = query_ref.shape[0]
    key_count = key_ref.shape[0]
    columns = grad_qkv_ref.shape[1] // 3

    @pl.when(block == 0)
    def _():
        skew[...] = jnp.zeros_like(skew)
        key_acc[...] = jnp.zeros_like(key_acc)
        value_acc[...] = jnp.zeros_like(value_acc)

    if len(rest) > 5:

        @pl.when((block == 0) & (pair == first))
        def _():
            grad_qkv_ref[...] = rest[0][...]

    keys = key_ref[...]
    values = value_ref[...]
    queries = query_ref[...]
    grads = grad_ref[...]
    inner = grads.astype(jnp.float32) * out_ref[...].astype(jnp.float32)
    grad_query = jnp.zeros((rows, LANES), jnp.float32)
    for which in range(2):
        grad_head = pick_head(grads, which)
        row_inner = jnp.sum(pick_head(inner, which), axis=1, keepdims=True)
        grad_soft = dot(grad_head, values, NT)
        soft_low = soft_ref[which]
        grad_scores = soft_low.astype(jnp.float32) * (grad_soft - row_inner)
        for part in range(rows // LANES):
            offset = pl.multiple_of(key_count - LANES * (part + 1) - rows * block, LANES)
            skew[which, :, pl.ds(offset, key_count)] += grad_scores[
                LANES * part : LANES * (part + 1)
            ]
        grad_low = grad_scores.astype(jnp.bfloat16)
        grad_query = grad_query + dot(grad_low, pick_head(keys, which))
        key_acc[...] += dot(pick_head(queries, which), grad_low, TN)
        value_acc[...] += dot(grad_head, soft_low, TN)
    own_rows = pl.ds(pl.multiple_of(block * rows, rows), rows)
    own_columns = pl.multiple_of(pair * LANES, LANES)
    grad_qkv_ref[own_rows, pl.ds(own_columns, LANES)] = grad_query.astype(jnp.bfloat16)

    @pl.when(block == pl.num_programs(1) - 1)
    def _():
        grad_qkv_ref[:, pl.ds(columns + own_columns, LANES)] = key_acc[...].T.astype(jnp.bfloat16)
        grad_qkv_ref[:, pl.ds(2 * columns + own_columns, LANES)] = value_acc[...].T.astype(
            jnp.bfloat16
        )
        down = lax.broadcasted_iota(jnp.int32, (LANES, LANES), 0)
        across = lax.broadcasted_iota(jnp.int32, (LANES, LANES), 1)
        flip = (down + across == LANES - 1).astype(jnp.float32)
        for which in range(2):
            turned = lax.dot_general(
                flip,
                skew[which],
                NN,
                precision=lax.Precision.HIGHEST,
                preferred_element_type=jnp.float32,
            )
            rel_ref[0, which : which + 1, :] = jnp.sum(
                pltpu.roll(turned, 0, 1, stride=1, stride_axis=0), axis=0, keepdims=True
            )


def attend_backward(soft_low, qkv, grad_heads, attended, first, last, so_far=()):
    seq_len, columns = attended.shape
    pairs = columns // LANES
    width = 2 * seq_len
    rows = min(BLOCK_ROWS, seq_len)
    row_block = pl.BlockSpec((rows, LANES), lambda pair, block: (block, first + pair))
    whole = pl.BlockSpec((seq_len, 3 * columns), lambda pair, block: (0, 0))
    grad_qkv, rel_grad = pl.pallas_call(
        functools.partial(backward_kernel, first),
        grid=(last - first, seq_len // rows),
        in_specs=[
            pl.BlockSpec((2, rows, seq_len), lambda pair, block: (first + pair, block, 0)),
            row_block,
            row_block,
            row_block,
            pl.BlockSpec((seq_len, LANES), lambda pair, block: (0, pairs + first + pair)),
            pl.BlockSpec((seq_len, LANES), lambda pair, block: (0, 2 * pairs + first + pair)),
        ]
        + [whole] * len(so_far),
        out_specs=[whole, pl.BlockSpec((1, 2, width), lambda pair, block: (pair, 0, 0))],
        scratch_shapes=[
            pltpu.VMEM((2, LANES, width), jnp.float32),
            pltpu.VMEM((LANES, seq_len), jnp.float32),
            pltpu.VMEM((LANES, seq_len), jnp.float32),
        ],
        out_shape=[
            jax.ShapeDtypeStruct((seq_len, 3 * columns), jnp.bfloat16),
            jax.ShapeDtypeStruct((last - first, 2, width), jnp.float32),
        ],
        compiler_params=pltpu.CompilerParams(vmem_limit_bytes=48 << 20),
        cost_estimate=pl.CostEstimate(
            flops=40 * seq_len * seq_len * columns * (last - first) // pairs,
            bytes_accessed=4 * (last - first) * seq_len * seq_len,
            transcendentals=0,
        ),
        name="attend_backward",
    )(soft_low, qkv, grad_heads, attended, qkv, qkv, *so_far)
    return grad_qkv, rel_grad.reshape(2 * (last - first), width)


def around(block):
    count = lax.axis_size("mp")
    return lax.ppermute(block, "mp", [(i, (i + 1) % count) for i in range(count)])


def together(*values):
    return lax.optimization_barrier(values)


def ring_gather(own):
    blocks = [own]
    for _ in range(lax.axis_size("mp") - 1):
        blocks.append(around(blocks[-1]))
    return blocks


def add_low(received, term):
    return (received.astype(jnp.float32) + term).astype(jnp.bfloat16)


def ring_scatter(part_of):
    count = lax.axis_size("mp")
    running = part_of(1).astype(jnp.bfloat16)
    for step in range(2, count):
        received, term = together(around(running), part_of(step))
        running = add_low(received, term)
    received, term = together(around(running), part_of(0))
    return received.astype(jnp.float32) + term


def total_over(value, axis):
    count = lax.axis_size(axis)
    apart = 1
    while apart < count:
        value = value + lax.ppermute(value, axis, [(i, i ^ apart) for i in range(count)])
        apart *= 2
    return value


def update(moment, grad_owned, factor):
    return 0.5 * moment + (0.5 * factor) * grad_owned


def shards(
    layer_input,
    output_grad,
    seq_lengths,
    deal_order,
    bucket_index,
    query_weight,
    key_weight,
    value_weight,
    out_weight,
    gate_weight,
    up_weight,
    down_weight,
    attn_gain,
    ffn_gain,
    bias_table,
    query_moment,
    key_moment,
    value_moment,
    out_moment,
    gate_moment,
    up_moment,
    down_moment,
    attn_gain_moment,
    ffn_gain_moment,
    table_moment,
):
    low = jnp.bfloat16
    f32 = jnp.float32
    group_index = lax.axis_index("dp")
    member = lax.axis_index("mp")
    group_count = lax.axis_size("dp")
    tensor_count = lax.axis_size("mp")

    def back(step):
        return lax.rem(member - step + tensor_count, tensor_count)

    picked = jnp.take(layer_input, deal_order, axis=0)
    dealt = lax.all_to_all(picked, "dp", split_axis=0, concat_axis=0, tiled=True)
    x_own = dealt.reshape(-1, dealt.shape[2])
    length = seq_lengths[deal_order[group_index]]
    seq_len, quarter = x_own.shape
    features = quarter * tensor_count
    part_rows = seq_len // tensor_count

    x_own, grad_next = together(x_own, around(output_grad[0]))
    grad_parts = [output_grad[0], grad_next]
    row_valid = lax.broadcasted_iota(jnp.int32, (seq_len, 1), 0) < length

    def valid_rows(part):
        return jnp.where(row_valid, part, jnp.zeros((), low))

    def row_part(array, step):
        return lax.dynamic_slice_in_dim(array, back(step) * part_rows, part_rows, 0)

    def column_part(array, step):
        return lax.dynamic_slice_in_dim(array, back(step) * quarter, quarter, 1)

    def set_rows(whole, part, step):
        return lax.dynamic_update_slice_in_dim(whole, part, back(step) * part_rows, 0)

    def set_columns(whole, part, step):
        return lax.dynamic_update_slice_in_dim(whole, part, back(step) * quarter, 1)

    def whole_columns(parts, start):
        whole = jnp.broadcast_to(start[:1, :1], (seq_len, features))
        for step, part in enumerate(parts):
            whole = set_columns(whole, part, step)
        return whole

    qkv_weight = jnp.concatenate([query_weight, key_weight, value_weight], axis=1).astype(low)
    qkv_weight, x_own = together(qkv_weight, x_own)
    qkv_weight = lax.all_gather(qkv_weight, "dp", axis=0, tiled=True)
    gate_up = jnp.concatenate([gate_weight, up_weight], axis=1).astype(low)
    out_down = jnp.concatenate([out_weight, down_weight], axis=0).astype(low)
    heads_columns = out_weight.shape[0]
    units = down_weight.shape[0]
    x_parts = [x_own, around(x_own)]
    small = jnp.concatenate([attn_gain, ffn_gain, bias_table.reshape(-1)]).astype(low)
    small, x_parts[1] = together(lax.all_gather(small, "dp", axis=0), x_parts[1])
    for step in range(1, tensor_count - 1):
        x_parts.append(around(x_parts[step]))
    out_down, x_parts[1] = together(out_down, x_parts[1])
    out_down = lax.all_gather(out_down, "dp", axis=1, tiled=True)
    gate_up, x_parts[2] = together(gate_up, x_parts[2])
    gate_up = lax.all_gather(gate_up, "dp", axis=0, tiled=True)

    gain_size = attn_gain.shape[0]
    first_gain = small[:, :gain_size].reshape(-1).astype(f32)
    second_gain = small[:, gain_size : 2 * gain_size].reshape(-1).astype(f32)
    full_table = small[:, 2 * gain_size :].reshape(NB, bias_table.shape[1])

    def down_columns(step):
        return lax.dynamic_slice(
            out_down, (heads_columns, back(step) * quarter), (units, quarter)
        )

    grad_parts[1], x_parts[-1] = together(grad_parts[1], x_parts[-1])
    x_rows = whole_columns(x_parts, x_own)
    grad_parts.append(around(grad_parts[1]))

    offsets = jnp.concatenate([bucket_index, jnp.full((1,), NB, jnp.int32)])
    bucket_hot = offsets[:, None] == lax.broadcasted_iota(jnp.int32, (2 * seq_len, NB), 1)
    rel_rows = dot(full_table, bucket_hot.astype(low), (((0,), (1,)), ((), ())))

    x_float = x_rows.astype(f32)
    inv_first = lax.rsqrt(jnp.mean(x_float * x_float, axis=-1, keepdims=True) + EPS)
    h_first = (x_float * inv_first * first_gain).astype(low)
    qkv = dot(h_first, qkv_weight).astype(low)
    pairs = heads_columns // LANES
    so_far = attend_forward(qkv, rel_rows, length, 0, 1)
    rel_rows, grad_parts[2], *so_far = together(rel_rows, grad_parts[2], *so_far)
    grad_parts.append(around(grad_parts[2]))
    attended, soft_low = attend_forward(qkv, rel_rows, length, 1, pairs, so_far)
    attended, grad_parts[3] = together(attended, grad_parts[3])

    def attended_part(step):
        return dot(row_part(attended, step), out_down[:heads_columns])

    running = around(attended_part(1).astype(low))
    grad_y = whole_columns([valid_rows(part) for part in grad_parts[:-1]], attended)
    received, term, grad_y = together(running, attended_part(2), grad_y)
    running = around(add_low(received, term))
    grad_y = set_columns(grad_y, valid_rows(grad_parts[-1]), tensor_count - 1)
    received, term, last_term, grad_y = together(
        running, attended_part(3), attended_part(0), grad_y
    )
    running = around(add_low(received, term))
    attn_branch = running.astype(f32) + last_term

    after_attn = row_part(x_rows, 0).astype(f32) + attn_branch
    inv_second = lax.rsqrt(jnp.mean(after_attn * after_attn, axis=-1, keepdims=True) + EPS)
    h_second = (after_attn * inv_second * second_gain).astype(low)

    h_parts = [h_second]
    hidden = jnp.broadcast_to(h_second[:1, :1], (seq_len, units))
    gate_up_grads = []
    terms = {}

    def square_sum(piece):
        return jnp.sum(jnp.square(piece.astype(f32)))

    def normed_part(step):
        return dot(gate_up_grads[step], gate_up, NT)

    for step in range(tensor_count):
        if step > 0:
            last = step - 1
            term = normed_part(last)
            h_parts[step], gate_up_grads[last], hidden, terms[last] = together(
                h_parts[step],
                gate_up_grads[last],
                hidden,
                term.astype(low) if last > 0 else term,
            )
        if step < tensor_count - 1:
            h_parts.append(around(h_parts[step]))
        else:
            terms[1], h_parts[step] = together(terms[1], h_parts[step])
            running = around(terms[1])
        both = dot(h_parts[step], gate_up)
        mixed, mix_back = jax.vjp(
            lambda gate_in, up_in: jax.nn.gelu(gate_in, approximate=True) * up_in,
            both[:, :units],
            both[:, units:],
        )
        hidden = set_rows(hidden, mixed.astype(low), step)
        grad_hidden = dot(row_part(grad_y, step), out_down[heads_columns:], NT)
        gate_up_grads.append(jnp.concatenate(mix_back(grad_hidden), axis=1).astype(low))

    received, terms[2], terms[3], gate_up_grads[3], hidden = together(
        running, terms[2], normed_part(3).astype(low), gate_up_grads[3], hidden
    )
    running = around(add_low(received, terms[2]))
    h_rotated = jnp.concatenate(h_parts, axis=0)
    grads_rotated = jnp.concatenate(gate_up_grads, axis=0)
    grad_gate_up = dot(h_rotated, grads_rotated, TN).astype(low)
    received, grad_gate_up = together(running, grad_gate_up)
    owned_gate_up = lax.psum_scatter(grad_gate_up, "dp", scatter_dimension=0, tiled=True)
    running = around(add_low(received, terms[3]))
    grad_down = dot(hidden, grad_y, TN).astype(low)
    received, terms[0], grad_down, hidden = together(running, terms[0], grad_down, hidden)
    grad_h_second = received.astype(f32) + terms[0]

    grad_ffn_gain = jnp.sum(grad_h_second * (after_attn * inv_second), axis=0)
    weighted = grad_h_second * second_gain
    row_inner = jnp.mean(weighted * after_attn, axis=-1, keepdims=True)
    grad_after = (
        row_part(grad_y, 0).astype(f32)
        + inv_second * weighted
        - after_attn * (inv_second * inv_second * inv_second) * row_inner
    ).astype(low)

    def output_part(step):
        part = dot(hidden, down_columns(step))
        mine = row_part(part, 0) + column_part(after_attn, step)
        return set_rows(part, mine, 0)

    after_parts = [grad_after]
    after_parts.append(around(after_parts[0]))
    output_terms = [output_part(step) for step in range(tensor_count)]
    after_parts[1], output_terms[1], output_terms[2] = together(
        after_parts[1], output_terms[1], output_terms[2]
    )
    after_parts.append(around(after_parts[1]))
    grad_out_down = jnp.pad(grad_down, ((heads_columns, 0), (0, 0)))
    after_parts[2], output_terms[3], output_terms[0], grad_out_down = together(
        after_parts[2], output_terms[3], output_terms[0], grad_out_down
    )
    after_parts.append(around(after_parts[2]))
    grad_after = grad_y
    grad_heads = jnp.zeros((seq_len, heads_columns), low)
    for step in range(tensor_count):
        if step == tensor_count - 1:
            grad_after, grad_heads, after_parts[step] = together(
                grad_after, grad_heads, after_parts[step]
            )
        part = after_parts[step]
        grad_after = set_rows(grad_after, part, step)
        grad_heads = set_rows(grad_heads, dot(part, out_down[:heads_columns], NT).astype(low), step)
    output_first = output_terms[1].astype(low)
    output_first, grad_after, grad_heads = together(output_first, grad_after, grad_heads)
    output_sum = around(output_first)

    grad_out = dot(attended, grad_after, TN).astype(low)
    grad_out_down = lax.dynamic_update_slice(grad_out_down, grad_out, (0, 0))
    grad_heads, grad_out_down = together(grad_heads, grad_out_down)
    owned_out_down = lax.psum_scatter(grad_out_down, "dp", scatter_dimension=1, tiled=True)
    half = pairs // 2
    first_grads, first_rel = attend_backward(soft_low, qkv, grad_heads, attended, 0, half)
    output_sum, first_grads, owned_gate_up = together(output_sum, first_grads, owned_gate_up)
    output_sum = around(add_low(output_sum, output_terms[2]))
    grad_qkv, second_rel = attend_backward(
        soft_low, qkv, grad_heads, attended, half, pairs, (first_grads,)
    )
    rel_grad = jnp.concatenate([first_rel, second_rel], axis=0)
    grad_qkv, output_sum = together(grad_qkv, output_sum)
    output_sent = add_low(output_sum, output_terms[3])

    def first_part(step):
        weight = lax.dynamic_slice_in_dim(qkv_weight, back(step) * quarter, quarter, 0)
        return dot(grad_qkv, weight, NT).astype(low)

    running, grad_qkv = together(first_part(1), grad_qkv)
    running = around(running)
    grad_qkv_weight = dot(h_first, grad_qkv, TN).astype(low)
    received, term, grad_qkv_weight = together(running, first_part(2), grad_qkv_weight)
    owned_qkv = lax.psum_scatter(grad_qkv_weight, "dp", scatter_dimension=0, tiled=True)
    running = around(add_low(received, term))
    inner = jnp.sum(grad_qkv.astype(f32) * qkv.astype(f32), axis=-1)
    inner = total_over(inner.reshape(-1, LANES), "mp").reshape(-1, 1) / features
    received, term, owned_out_down = together(running, first_part(3), owned_out_down)
    running = around(add_low(received, term))
    grad_table = lax.dot_general(
        bucket_hot.astype(f32),
        rel_grad,
        (((0,), (1,)), ((), ())),
        precision=lax.Precision.HIGHEST,
        preferred_element_type=f32,
    )
    early_sq = square_sum(owned_gate_up) + square_sum(owned_out_down)
    term, output_sent = together(first_part(0), output_sent)
    output_sum = around(output_sent)
    received, term, grad_table, early_sq, inner = together(
        running, term, grad_table, early_sq, inner
    )
    grad_h_first = received.astype(f32) + term
    own_gain = lax.dynamic_slice_in_dim(first_gain, member * quarter, quarter, 0)
    x_own = x_own.astype(f32)
    grad_attn_gain = jnp.sum(grad_h_first * (x_own * inv_first), axis=0)
    grad_input = (
        column_part(grad_after, 0).astype(f32)
        + inv_first * (grad_h_first * own_gain)
        - x_own * (inv_first * inv_first) * inner
    ).astype(low)
    local_sq = early_sq + square_sum(owned_qkv)
    heads_dev = bias_table.shape[1]
    first_wide = lax.dynamic_update_slice_in_dim(
        jnp.zeros((features,), f32), grad_attn_gain, member * quarter, 0
    )
    table_wide = lax.dynamic_update_slice_in_dim(
        jnp.zeros((NB, heads_dev * tensor_count), f32), grad_table, member * heads_dev, 1
    )
    sums = jnp.concatenate([first_wide, grad_ffn_gain, table_wide.reshape(-1)])
    small_count = sums.shape[0]
    sums = jnp.concatenate([sums, jnp.broadcast_to(local_sq, (LANES,))])
    sums = jnp.sum(lax.all_gather(sums.reshape(-1, LANES), "dp", axis=0), axis=0)
    sums, grad_input, output_sum = together(sums, grad_input, output_sum)
    came_back = lax.all_to_all(
        grad_input.reshape(group_count, -1, quarter), "dp", split_axis=0, concat_axis=0, tiled=True
    )
    group_iota = lax.broadcasted_iota(jnp.int32, (group_count, group_count), 0)
    place = jnp.argmax(deal_order[None, :] == group_iota, axis=1)
    input_grad = jnp.take(came_back, place, axis=0)

    layer_out = (output_sum.astype(f32) + output_terms[0]).astype(low)[None]
    sums = total_over(sums, "mp").reshape(-1)
    total_sq = sums[small_count] + jnp.sum(sums[:small_count] * sums[:small_count])
    grad_norm = jnp.sqrt(total_sq)
    limit = math.sqrt(4 * D * H * DH + 3 * D * FF + 2 * D + NB * H)
    factor = jnp.minimum(1.0, limit / grad_norm)
    owned_first = lax.dynamic_slice_in_dim(sums, group_index * gain_size, gain_size, 0)
    owned_second = lax.dynamic_slice_in_dim(
        sums, features + group_index * gain_size, gain_size, 0
    )
    table_rows = bias_table.shape[0]
    owned_table = lax.dynamic_slice(
        sums[2 * features : small_count].reshape(NB, heads_dev * tensor_count),
        (group_index * table_rows, member * heads_dev),
        (table_rows, heads_dev),
    )
    return (
        layer_out,
        input_grad,
        grad_norm,
        update(query_moment, owned_qkv[:, :heads_columns], factor),
        update(key_moment, owned_qkv[:, heads_columns : 2 * heads_columns], factor),
        update(value_moment, owned_qkv[:, 2 * heads_columns :], factor),
        update(out_moment, owned_out_down[:heads_columns], factor),
        update(gate_moment, owned_gate_up[:, :units], factor),
        update(up_moment, owned_gate_up[:, units:], factor),
        update(down_moment, owned_out_down[heads_columns:], factor),
        update(attn_gain_moment, owned_first, factor),
        update(ffn_gain_moment, owned_second, factor),
        update(table_moment, owned_table, factor),
    )


def solution(mesh):
    in_specs = (
        P(None, "dp", "mp"),
        P("dp", None, "mp"),
        P(),
        P(),
        P(),
        P("dp", "mp"),
        P("dp", "mp"),
        P("dp", "mp"),
        P("mp", "dp"),
        P("dp", "mp"),
        P("dp", "mp"),
        P("mp", "dp"),
        P("dp"),
        P("dp"),
        P("dp", "mp"),
        P("dp", "mp"),
        P("dp", "mp"),
        P("dp", "mp"),
        P("mp", "dp"),
        P("dp", "mp"),
        P("dp", "mp"),
        P("mp", "dp"),
        P("dp"),
        P("dp"),
        P("dp", "mp"),
    )
    out_specs = (
        P("dp", None, "mp"),
        P(None, "dp", "mp"),
        P(),
        P("dp", "mp"),
        P("dp", "mp"),
        P("dp", "mp"),
        P("mp", "dp"),
        P("dp", "mp"),
        P("dp", "mp"),
        P("mp", "dp"),
        P("dp"),
        P("dp"),
        P("dp", "mp"),
    )
    return jax.shard_map(shards, mesh=mesh, in_specs=in_specs, out_specs=out_specs, check_vma=False)
```

```python
import functools
import math

import jax
import jax.numpy as jnp
from jax import lax
from jax.experimental import pallas as pl
from jax.experimental.pallas import tpu as pltpu
from jax.sharding import PartitionSpec as P

D = 2048
H = 32
DH = 64
FF = 5120
NB = 32


EPS = 1e-06
NEG = -1e30
LANES = 128
BLOCK_ROWS = 256

NN = (((1,), (0,)), ((), ()))
NT = (((1,), (1,)), ((), ()))
TN = (((0,), (0,)), ((), ()))


def dot(left, right, dims=NN):
    return lax.dot_general(left, right, dims, preferred_element_type=jnp.float32)


def pick_head(pair_rows, which):
    lane = lax.broadcasted_iota(jnp.int32, (1, LANES), 1)
    return jnp.where(lane // DH == which, pair_rows, jnp.zeros_like(pair_rows))


def forward_kernel(length, rel_ref, query_ref, key_ref, value_ref, out_ref, soft_ref, skew):
    block = pl.program_id(1)
    rows = query_ref.shape[0]
    key_count = key_ref.shape[0]
    width = rel_ref.shape[2]

    @pl.when(block == 0)
    def _():
        for which in range(2):
            spread = jnp.broadcast_to(rel_ref[0, which : which + 1, :], (LANES, width))
            skew[which] = pltpu.roll(spread, width - (LANES - 1), 1, stride=1, stride_axis=0)

    key_at = lax.broadcasted_iota(jnp.int32, (1, key_count), 1)
    key_mask = jnp.where(key_at < length[0], 0.0, NEG)
    keys = key_ref[...]
    values = value_ref[...]
    mixed = jnp.zeros((rows, LANES), jnp.float32)
    for which in range(2):
        products = dot(pick_head(query_ref[...], which), keys, NT)
        parts = []
        for part in range(rows // LANES):
            offset = pl.multiple_of(key_count - LANES * (part + 1) - rows * block, LANES)
            parts.append(
                products[LANES * part : LANES * (part + 1)] + skew[which, :, pl.ds(offset, key_count)]
            )
        scores = jnp.concatenate(parts, 0) + key_mask
        exp_terms = jnp.exp(scores - jnp.max(scores, axis=1, keepdims=True))
        total = jnp.sum(exp_terms, axis=1, keepdims=True)
        soft_low = (exp_terms * (1.0 / total)).astype(jnp.bfloat16)
        soft_ref[which] = soft_low
        mixed = mixed + dot(soft_low, pick_head(values, which))
    out_ref[...] = mixed.astype(jnp.bfloat16)


def attend_forward(qkv, rel_rows, length, first, last, so_far=None):
    seq_len = qkv.shape[0]
    columns = qkv.shape[1] // 3
    pairs = columns // LANES
    width = rel_rows.shape[1]
    rows = min(BLOCK_ROWS, seq_len)
    kernel = forward_kernel
    operands = [length.reshape(1), rel_rows.reshape(pairs, 2, width), qkv, qkv, qkv]
    in_specs = [
        pl.BlockSpec((1, 2, width), lambda pair, block, n: (first + pair, 0, 0)),
        pl.BlockSpec((rows, LANES), lambda pair, block, n: (block, first + pair)),
        pl.BlockSpec((seq_len, LANES), lambda pair, block, n: (0, pairs + first + pair)),
        pl.BlockSpec((seq_len, LANES), lambda pair, block, n: (0, 2 * pairs + first + pair)),
    ]
    aliases = {}
    if so_far is not None:
        kernel = second_forward_kernel
        operands += so_far
        in_specs += [pl.BlockSpec(memory_space=pl.ANY)] * 2
        aliases = {5: 0, 6: 1}
    return pl.pallas_call(
        kernel,
        grid_spec=pltpu.PrefetchScalarGridSpec(
            num_scalar_prefetch=1,
            grid=(last - first, seq_len // rows),
            in_specs=in_specs,
            out_specs=[
                pl.BlockSpec((rows, LANES), lambda pair, block, n: (block, first + pair)),
                pl.BlockSpec((2, rows, seq_len), lambda pair, block, n: (first + pair, block, 0)),
            ],
            scratch_shapes=[pltpu.VMEM((2, LANES, width), jnp.float32)],
        ),
        out_shape=[
            jax.ShapeDtypeStruct((seq_len, columns), jnp.bfloat16),
            jax.ShapeDtypeStruct((2 * pairs, seq_len, seq_len), jnp.bfloat16),
        ],
        input_output_aliases=aliases,
        compiler_params=pltpu.CompilerParams(vmem_limit_bytes=40 << 20),
        cost_estimate=pl.CostEstimate(
            flops=16 * seq_len * seq_len * columns * (last - first) // pairs,
            bytes_accessed=4 * (last - first) * seq_len * seq_len,
            transcendentals=2 * (last - first) * seq_len * seq_len,
        ),
        name="attend_forward",
    )(*operands)


def second_forward_kernel(
    length, rel_ref, query_ref, key_ref, value_ref, _, __, out_ref, soft_ref, skew
):
    forward_kernel(length, rel_ref, query_ref, key_ref, value_ref, out_ref, soft_ref, skew)


def backward_kernel(
    first,
    soft_ref,
    query_ref,
    grad_ref,
    out_ref,
    key_ref,
    value_ref,
    *rest,
):
    grad_qkv_ref, rel_ref, skew, key_acc, value_acc = rest[-5:]
    pair = first + pl.program_id(0)
    block = pl.program_id(1)
    rows = query_ref.shape[0]
    key_count = key_ref.shape[0]
    columns = grad_qkv_ref.shape[1] // 3

    @pl.when(block == 0)
    def _():
        skew[...] = jnp.zeros_like(skew)
        key_acc[...] = jnp.zeros_like(key_acc)
        value_acc[...] = jnp.zeros_like(value_acc)

    if len(rest) > 5:

        @pl.when((block == 0) & (pair == first))
        def _():
            grad_qkv_ref[...] = rest[0][...]

    keys = key_ref[...]
    values = value_ref[...]
    queries = query_ref[...]
    grads = grad_ref[...]
    inner = grads.astype(jnp.float32) * out_ref[...].astype(jnp.float32)
    grad_query = jnp.zeros((rows, LANES), jnp.float32)
    for which in range(2):
        grad_head = pick_head(grads, which)
        row_inner = jnp.sum(pick_head(inner, which), axis=1, keepdims=True)
        grad_soft = dot(grad_head, values, NT)
        soft_low = soft_ref[which]
        grad_scores = soft_low.astype(jnp.float32) * (grad_soft - row_inner)
        for part in range(rows // LANES):
            offset = pl.multiple_of(key_count - LANES * (part + 1) - rows * block, LANES)
            skew[which, :, pl.ds(offset, key_count)] += grad_scores[
                LANES * part : LANES * (part + 1)
            ]
        grad_low = grad_scores.astype(jnp.bfloat16)
        grad_query = grad_query + dot(grad_low, pick_head(keys, which))
        key_acc[...] += dot(pick_head(queries, which), grad_low, TN)
        value_acc[...] += dot(grad_head, soft_low, TN)
    own_rows = pl.ds(pl.multiple_of(block * rows, rows), rows)
    own_columns = pl.multiple_of(pair * LANES, LANES)
    grad_qkv_ref[own_rows, pl.ds(own_columns, LANES)] = grad_query.astype(jnp.bfloat16)

    @pl.when(block == pl.num_programs(1) - 1)
    def _():
        grad_qkv_ref[:, pl.ds(columns + own_columns, LANES)] = key_acc[...].T.astype(jnp.bfloat16)
        grad_qkv_ref[:, pl.ds(2 * columns + own_columns, LANES)] = value_acc[...].T.astype(
            jnp.bfloat16
        )
        down = lax.broadcasted_iota(jnp.int32, (LANES, LANES), 0)
        across = lax.broadcasted_iota(jnp.int32, (LANES, LANES), 1)
        flip = (down + across == LANES - 1).astype(jnp.float32)
        for which in range(2):
            turned = lax.dot_general(
                flip,
                skew[which],
                NN,
                precision=lax.Precision.HIGHEST,
                preferred_element_type=jnp.float32,
            )
            rel_ref[0, which : which + 1, :] = jnp.sum(
                pltpu.roll(turned, 0, 1, stride=1, stride_axis=0), axis=0, keepdims=True
            )


def attend_backward(soft_low, qkv, grad_heads, attended, first, last, so_far=()):
    seq_len, columns = attended.shape
    pairs = columns // LANES
    width = 2 * seq_len
    rows = min(BLOCK_ROWS, seq_len)
    row_block = pl.BlockSpec((rows, LANES), lambda pair, block: (block, first + pair))
    whole = pl.BlockSpec((seq_len, 3 * columns), lambda pair, block: (0, 0))
    grad_qkv, rel_grad = pl.pallas_call(
        functools.partial(backward_kernel, first),
        grid=(last - first, seq_len // rows),
        in_specs=[
            pl.BlockSpec((2, rows, seq_len), lambda pair, block: (first + pair, block, 0)),
            row_block,
            row_block,
            row_block,
            pl.BlockSpec((seq_len, LANES), lambda pair, block: (0, pairs + first + pair)),
            pl.BlockSpec((seq_len, LANES), lambda pair, block: (0, 2 * pairs + first + pair)),
        ]
        + [whole] * len(so_far),
        out_specs=[whole, pl.BlockSpec((1, 2, width), lambda pair, block: (pair, 0, 0))],
        scratch_shapes=[
            pltpu.VMEM((2, LANES, width), jnp.float32),
            pltpu.VMEM((LANES, seq_len), jnp.float32),
            pltpu.VMEM((LANES, seq_len), jnp.float32),
        ],
        out_shape=[
            jax.ShapeDtypeStruct((seq_len, 3 * columns), jnp.bfloat16),
            jax.ShapeDtypeStruct((last - first, 2, width), jnp.float32),
        ],
        compiler_params=pltpu.CompilerParams(vmem_limit_bytes=48 << 20),
        cost_estimate=pl.CostEstimate(
            flops=40 * seq_len * seq_len * columns * (last - first) // pairs,
            bytes_accessed=4 * (last - first) * seq_len * seq_len,
            transcendentals=0,
        ),
        name="attend_backward",
    )(soft_low, qkv, grad_heads, attended, qkv, qkv, *so_far)
    return grad_qkv, rel_grad.reshape(2 * (last - first), width)


def around(block):
    count = lax.axis_size("mp")
    return lax.ppermute(block, "mp", [(i, (i + 1) % count) for i in range(count)])


def together(*values):
    return lax.optimization_barrier(values)


def ring_gather(own):
    blocks = [own]
    for _ in range(lax.axis_size("mp") - 1):
        blocks.append(around(blocks[-1]))
    return blocks


def add_low(received, term):
    return (received.astype(jnp.float32) + term).astype(jnp.bfloat16)


def ring_scatter(part_of):
    count = lax.axis_size("mp")
    running = part_of(1).astype(jnp.bfloat16)
    for step in range(2, count):
        received, term = together(around(running), part_of(step))
        running = add_low(received, term)
    received, term = together(around(running), part_of(0))
    return received.astype(jnp.float32) + term


def total_over(value, axis):
    count = lax.axis_size(axis)
    apart = 1
    while apart < count:
        value = value + lax.ppermute(value, axis, [(i, i ^ apart) for i in range(count)])
        apart *= 2
    return value


def update(moment, grad_owned, factor):
    return 0.5 * moment + (0.5 * factor) * grad_owned


def shards(
    layer_input,
    output_grad,
    seq_lengths,
    deal_order,
    bucket_index,
    query_weight,
    key_weight,
    value_weight,
    out_weight,
    gate_weight,
    up_weight,
    down_weight,
    attn_gain,
    ffn_gain,
    bias_table,
    query_moment,
    key_moment,
    value_moment,
    out_moment,
    gate_moment,
    up_moment,
    down_moment,
    attn_gain_moment,
    ffn_gain_moment,
    table_moment,
):
    low = jnp.bfloat16
    f32 = jnp.float32
    group_index = lax.axis_index("dp")
    member = lax.axis_index("mp")
    group_count = lax.axis_size("dp")
    tensor_count = lax.axis_size("mp")

    def back(step):
        return lax.rem(member - step + tensor_count, tensor_count)

    picked = jnp.take(layer_input, deal_order, axis=0)
    dealt = lax.all_to_all(picked, "dp", split_axis=0, concat_axis=0, tiled=True)
    x_own = dealt.reshape(-1, dealt.shape[2])
    length = seq_lengths[deal_order[group_index]]
    seq_len, quarter = x_own.shape
    features = quarter * tensor_count
    part_rows = seq_len // tensor_count

    grad_next = around(output_grad[0])
    grad_parts = [output_grad[0], grad_next]
    row_valid = lax.broadcasted_iota(jnp.int32, (seq_len, 1), 0) < length

    def valid_rows(part):
        return jnp.where(row_valid, part, jnp.zeros((), low))

    def row_part(array, step):
        return lax.dynamic_slice_in_dim(array, back(step) * part_rows, part_rows, 0)

    def column_part(array, step):
        return lax.dynamic_slice_in_dim(array, back(step) * quarter, quarter, 1)

    def set_rows(whole, part, step):
        return lax.dynamic_update_slice_in_dim(whole, part, back(step) * part_rows, 0)

    def set_columns(whole, part, step):
        return lax.dynamic_update_slice_in_dim(whole, part, back(step) * quarter, 1)

    def whole_columns(parts, start):
        whole = jnp.broadcast_to(start[:1, :1], (seq_len, features))
        for step, part in enumerate(parts):
            whole = set_columns(whole, part, step)
        return whole

    qkv_weight = jnp.concatenate([query_weight, key_weight, value_weight], axis=1).astype(low)
    qkv_weight, x_own = together(qkv_weight, x_own)
    qkv_weight = lax.all_gather(qkv_weight, "dp", axis=0, tiled=True)
    gate_up = jnp.concatenate([gate_weight, up_weight], axis=1).astype(low)
    out_down = jnp.concatenate([out_weight, down_weight], axis=0).astype(low)
    heads_columns = out_weight.shape[0]
    units = down_weight.shape[0]
    x_parts = [x_own, around(x_own)]
    small = jnp.concatenate([attn_gain, ffn_gain, bias_table.reshape(-1)]).astype(low)
    small, grad_parts[1], x_parts[1] = together(
        lax.all_gather(small, "dp", axis=0), grad_parts[1], x_parts[1]
    )
    for step in range(1, tensor_count - 1):
        x_parts.append(around(x_parts[step]))
    out_down, x_parts[1] = together(out_down, x_parts[1])
    out_down = lax.all_gather(out_down, "dp", axis=1, tiled=True)
    gate_up, x_parts[2] = together(gate_up, x_parts[2])
    gate_up = lax.all_gather(gate_up, "dp", axis=0, tiled=True)

    gain_size = attn_gain.shape[0]
    first_gain = small[:, :gain_size].reshape(-1).astype(f32)
    second_gain = small[:, gain_size : 2 * gain_size].reshape(-1).astype(f32)
    full_table = small[:, 2 * gain_size :].reshape(NB, bias_table.shape[1])

    def down_columns(step):
        return lax.dynamic_slice(
            out_down, (heads_columns, back(step) * quarter), (units, quarter)
        )

    grad_parts[1], x_parts[-1] = together(grad_parts[1], x_parts[-1])
    x_rows = whole_columns(x_parts, x_own)
    grad_parts.append(around(grad_parts[1]))

    offsets = jnp.concatenate([bucket_index, jnp.full((1,), NB, jnp.int32)])
    bucket_hot = offsets[:, None] == lax.broadcasted_iota(jnp.int32, (2 * seq_len, NB), 1)
    rel_rows = dot(full_table, bucket_hot.astype(low), (((0,), (1,)), ((), ())))

    x_float = x_rows.astype(f32)
    inv_first = lax.rsqrt(jnp.mean(x_float * x_float, axis=-1, keepdims=True) + EPS)
    h_first = (x_float * inv_first * first_gain).astype(low)
    qkv = dot(h_first, qkv_weight).astype(low)
    pairs = heads_columns // LANES
    so_far = attend_forward(qkv, rel_rows, length, 0, 1)
    rel_rows, grad_parts[2], *so_far = together(rel_rows, grad_parts[2], *so_far)
    grad_parts.append(around(grad_parts[2]))
    attended, soft_low = attend_forward(qkv, rel_rows, length, 1, pairs, so_far)
    attended, grad_parts[3] = together(attended, grad_parts[3])

    def attended_part(step):
        return dot(row_part(attended, step), out_down[:heads_columns])

    running = around(attended_part(1).astype(low))
    grad_y = whole_columns([valid_rows(part) for part in grad_parts[:-1]], attended)
    received, term, grad_y = together(running, attended_part(2), grad_y)
    running = around(add_low(received, term))
    grad_y = set_columns(grad_y, valid_rows(grad_parts[-1]), tensor_count - 1)
    received, term, last_term, grad_y = together(
        running, attended_part(3), attended_part(0), grad_y
    )
    running = around(add_low(received, term))
    attn_branch = running.astype(f32) + last_term

    after_attn = row_part(x_rows, 0).astype(f32) + attn_branch
    inv_second = lax.rsqrt(jnp.mean(after_attn * after_attn, axis=-1, keepdims=True) + EPS)
    h_second = (after_attn * inv_second * second_gain).astype(low)

    h_parts = [h_second]
    hidden = jnp.broadcast_to(h_second[:1, :1], (seq_len, units))
    gate_up_grads = []
    terms = {}

    def square_sum(piece):
        return jnp.sum(jnp.square(piece.astype(f32)))

    def normed_part(step):
        return dot(gate_up_grads[step], gate_up, NT)

    for step in range(tensor_count):
        if step > 0:
            last = step - 1
            term = normed_part(last)
            h_parts[step], gate_up_grads[last], hidden, terms[last] = together(
                h_parts[step],
                gate_up_grads[last],
                hidden,
                term.astype(low) if last > 0 else term,
            )
        if step < tensor_count - 1:
            h_parts.append(around(h_parts[step]))
        else:
            terms[1], h_parts[step] = together(terms[1], h_parts[step])
            running = around(terms[1])
        both = dot(h_parts[step], gate_up)
        mixed, mix_back = jax.vjp(
            lambda gate_in, up_in: jax.nn.gelu(gate_in, approximate=True) * up_in,
            both[:, :units],
            both[:, units:],
        )
        hidden = set_rows(hidden, mixed.astype(low), step)
        grad_hidden = dot(row_part(grad_y, step), out_down[heads_columns:], NT)
        gate_up_grads.append(jnp.concatenate(mix_back(grad_hidden), axis=1).astype(low))

    received, terms[2], terms[3], gate_up_grads[3], hidden = together(
        running, terms[2], normed_part(3).astype(low), gate_up_grads[3], hidden
    )
    running = around(add_low(received, terms[2]))
    h_rotated = jnp.concatenate(h_parts, axis=0)
    grads_rotated = jnp.concatenate(gate_up_grads, axis=0)
    grad_gate_up = dot(h_rotated, grads_rotated, TN).astype(low)
    received, grad_gate_up = together(running, grad_gate_up)
    owned_gate_up = lax.psum_scatter(grad_gate_up, "dp", scatter_dimension=0, tiled=True)
    running = around(add_low(received, terms[3]))
    grad_down = dot(hidden, grad_y, TN).astype(low)
    received, terms[0], grad_down, hidden = together(running, terms[0], grad_down, hidden)
    grad_h_second = received.astype(f32) + terms[0]

    grad_ffn_gain = jnp.sum(grad_h_second * (after_attn * inv_second), axis=0)
    weighted = grad_h_second * second_gain
    row_inner = jnp.mean(weighted * after_attn, axis=-1, keepdims=True)
    grad_after = (
        row_part(grad_y, 0).astype(f32)
        + inv_second * weighted
        - after_attn * (inv_second * inv_second * inv_second) * row_inner
    ).astype(low)

    def output_part(step):
        part = dot(hidden, down_columns(step))
        mine = row_part(part, 0) + column_part(after_attn, step)
        return set_rows(part, mine, 0)

    after_parts = [grad_after]
    after_parts.append(around(after_parts[0]))
    output_terms = [output_part(step) for step in range(tensor_count)]
    after_parts[1], output_terms[1], output_terms[2] = together(
        after_parts[1], output_terms[1], output_terms[2]
    )
    after_parts.append(around(after_parts[1]))
    grad_out_down = jnp.pad(grad_down, ((heads_columns, 0), (0, 0)))
    after_parts[2], output_terms[3], output_terms[0], grad_out_down = together(
        after_parts[2], output_terms[3], output_terms[0], grad_out_down
    )
    after_parts.append(around(after_parts[2]))
    grad_after = grad_y
    grad_heads = jnp.zeros((seq_len, heads_columns), low)
    for step in range(tensor_count):
        if step == tensor_count - 1:
            grad_after, grad_heads, after_parts[step] = together(
                grad_after, grad_heads, after_parts[step]
            )
        part = after_parts[step]
        grad_after = set_rows(grad_after, part, step)
        grad_heads = set_rows(grad_heads, dot(part, out_down[:heads_columns], NT).astype(low), step)
    output_first = output_terms[1].astype(low)
    output_first, grad_after, grad_heads = together(output_first, grad_after, grad_heads)
    output_sum = around(output_first)

    grad_out = dot(attended, grad_after, TN).astype(low)
    grad_out_down = lax.dynamic_update_slice(grad_out_down, grad_out, (0, 0))
    grad_heads, grad_out_down = together(grad_heads, grad_out_down)
    owned_out_down = lax.psum_scatter(grad_out_down, "dp", scatter_dimension=1, tiled=True)
    half = pairs // 2
    first_grads, first_rel = attend_backward(soft_low, qkv, grad_heads, attended, 0, half)
    output_sum, first_grads, owned_gate_up = together(output_sum, first_grads, owned_gate_up)
    output_sum = around(add_low(output_sum, output_terms[2]))
    grad_qkv, second_rel = attend_backward(
        soft_low, qkv, grad_heads, attended, half, pairs, (first_grads,)
    )
    rel_grad = jnp.concatenate([first_rel, second_rel], axis=0)
    grad_qkv, output_sum = together(grad_qkv, output_sum)
    output_sent = add_low(output_sum, output_terms[3])

    def first_part(step):
        weight = lax.dynamic_slice_in_dim(qkv_weight, back(step) * quarter, quarter, 0)
        return dot(grad_qkv, weight, NT).astype(low)

    running, grad_qkv = together(first_part(1), grad_qkv)
    running = around(running)
    grad_qkv_weight = dot(h_first, grad_qkv, TN).astype(low)
    received, term, grad_qkv_weight = together(running, first_part(2), grad_qkv_weight)
    owned_qkv = lax.psum_scatter(grad_qkv_weight, "dp", scatter_dimension=0, tiled=True)
    running = around(add_low(received, term))
    inner = jnp.sum(grad_qkv.astype(f32) * qkv.astype(f32), axis=-1)
    inner = total_over(inner.reshape(-1, LANES), "mp").reshape(-1, 1) / features
    received, term, owned_out_down = together(running, first_part(3), owned_out_down)
    running = around(add_low(received, term))
    grad_table = lax.dot_general(
        bucket_hot.astype(f32),
        rel_grad,
        (((0,), (1,)), ((), ())),
        precision=lax.Precision.HIGHEST,
        preferred_element_type=f32,
    )
    early_sq = square_sum(owned_gate_up) + square_sum(owned_out_down)
    term, output_sent = together(first_part(0), output_sent)
    output_sum = around(output_sent)
    received, term, grad_table, early_sq, inner = together(
        running, term, grad_table, early_sq, inner
    )
    grad_h_first = received.astype(f32) + term
    own_gain = lax.dynamic_slice_in_dim(first_gain, member * quarter, quarter, 0)
    x_own = x_own.astype(f32)
    grad_attn_gain = jnp.sum(grad_h_first * (x_own * inv_first), axis=0)
    grad_input = (
        column_part(grad_after, 0).astype(f32)
        + inv_first * (grad_h_first * own_gain)
        - x_own * (inv_first * inv_first) * inner
    ).astype(low)
    local_sq = early_sq + square_sum(owned_qkv)
    heads_dev = bias_table.shape[1]
    first_wide = lax.dynamic_update_slice_in_dim(
        jnp.zeros((features,), f32), grad_attn_gain, member * quarter, 0
    )
    table_wide = lax.dynamic_update_slice_in_dim(
        jnp.zeros((NB, heads_dev * tensor_count), f32), grad_table, member * heads_dev, 1
    )
    sums = jnp.concatenate([first_wide, grad_ffn_gain, table_wide.reshape(-1)])
    small_count = sums.shape[0]
    sums = jnp.concatenate([sums, jnp.broadcast_to(local_sq, (LANES,))])
    sums = jnp.sum(lax.all_gather(sums.reshape(-1, LANES), "dp", axis=0), axis=0)
    sums, grad_input, output_sum = together(sums, grad_input, output_sum)
    came_back = lax.all_to_all(
        grad_input.reshape(group_count, -1, quarter), "dp", split_axis=0, concat_axis=0, tiled=True
    )
    group_iota = lax.broadcasted_iota(jnp.int32, (group_count, group_count), 0)
    place = jnp.argmax(deal_order[None, :] == group_iota, axis=1)
    input_grad = jnp.take(came_back, place, axis=0)

    layer_out = (output_sum.astype(f32) + output_terms[0]).astype(low)[None]
    sums = total_over(sums, "mp").reshape(-1)
    total_sq = sums[small_count] + jnp.sum(sums[:small_count] * sums[:small_count])
    grad_norm = jnp.sqrt(total_sq)
    limit = math.sqrt(4 * D * H * DH + 3 * D * FF + 2 * D + NB * H)
    factor = jnp.minimum(1.0, limit / grad_norm)
    owned_first = lax.dynamic_slice_in_dim(sums, group_index * gain_size, gain_size, 0)
    owned_second = lax.dynamic_slice_in_dim(
        sums, features + group_index * gain_size, gain_size, 0
    )
    table_rows = bias_table.shape[0]
    owned_table = lax.dynamic_slice(
        sums[2 * features : small_count].reshape(NB, heads_dev * tensor_count),
        (group_index * table_rows, member * heads_dev),
        (table_rows, heads_dev),
    )
    return (
        layer_out,
        input_grad,
        grad_norm,
        update(query_moment, owned_qkv[:, :heads_columns], factor),
        update(key_moment, owned_qkv[:, heads_columns : 2 * heads_columns], factor),
        update(value_moment, owned_qkv[:, 2 * heads_columns :], factor),
        update(out_moment, owned_out_down[:heads_columns], factor),
        update(gate_moment, owned_gate_up[:, :units], factor),
        update(up_moment, owned_gate_up[:, units:], factor),
        update(down_moment, owned_out_down[heads_columns:], factor),
        update(attn_gain_moment, owned_first, factor),
        update(ffn_gain_moment, owned_second, factor),
        update(table_moment, owned_table, factor),
    )


def solution(mesh):
    in_specs = (
        P(None, "dp", "mp"),
        P("dp", None, "mp"),
        P(),
        P(),
        P(),
        P("dp", "mp"),
        P("dp", "mp"),
        P("dp", "mp"),
        P("mp", "dp"),
        P("dp", "mp"),
        P("dp", "mp"),
        P("mp", "dp"),
        P("dp"),
        P("dp"),
        P("dp", "mp"),
        P("dp", "mp"),
        P("dp", "mp"),
        P("dp", "mp"),
        P("mp", "dp"),
        P("dp", "mp"),
        P("dp", "mp"),
        P("mp", "dp"),
        P("dp"),
        P("dp"),
        P("dp", "mp"),
    )
    out_specs = (
        P("dp", None, "mp"),
        P(None, "dp", "mp"),
        P(),
        P("dp", "mp"),
        P("dp", "mp"),
        P("dp", "mp"),
        P("mp", "dp"),
        P("dp", "mp"),
        P("dp", "mp"),
        P("mp", "dp"),
        P("dp"),
        P("dp"),
        P("dp", "mp"),
    )
    return jax.shard_map(shards, mesh=mesh, in_specs=in_specs, out_specs=out_specs, check_vma=False)
```
